32 devices in a mesh: dp: 8 (over y, x, core), mp: 4 (over z).
Axes of the slice: x: 2, y: 2, z: 4, core: 2. Of those that a mesh axis runs over, the one named last changes fastest.
Arguments:
- token_ids: int32 [16, 1024], P('dp'), may hold values from 0 to 30719
- mlm_flags: int32 [16, 1024], P('dp'), may hold values 0 or 1
- pad_lengths: int32 [16], P('dp'), may hold values from 256 to 1024, as said below
- group_ids: int32 [16], P('dp'), may hold values from 0 to 1
- group_weight: float32 [2], replicated, may hold values from 0.5 to 2
- teacher_table: bfloat16 [30720, 512], P('mp'), may hold values from -2 to 2
- teacher_position: bfloat16 [1024, 512], replicated, may hold values from -0.59765625 to 0.59765625
- teacher_project: bfloat16 [3, 512, 512], P(None, None, 'mp'), may hold values from -0.25 to 0.25
- teacher_output: bfloat16 [512, 512], P('mp'), may hold values from -1 to 1
- teacher_expand: bfloat16 [512, 2048], P(None, 'mp'), may hold values from -0.25 to 0.25
- teacher_reduce: bfloat16 [2048, 512], P('mp'), may hold values from -0.125 to 0.125
- teacher_vectors: bfloat16 [8, 512], replicated, may hold values from -2 to 3
- student_table: float32 [30720, 512], P('mp', 'dp'), may hold values from -2 to 2
- student_position: float32 [1024, 512], P(None, 'dp'), may hold values from -0.6 to 0.6
- student_project: float32 [3, 512, 512], P(None, 'dp', 'mp'), may hold values from -0.25 to 0.25
- student_output: float32 [512, 512], P('mp', 'dp'), may hold values from -1 to 1
- student_expand: float32 [512, 2048], P('dp', 'mp'), may hold values from -0.25 to 0.25
- student_reduce: float32 [2048, 512], P('mp', 'dp'), may hold values from -0.125 to 0.125
- student_vectors: float32 [8, 512], P(None, 'dp'), may hold values from -2 to 3
- first_table: float32 [30720, 512], P('mp', 'dp'), may hold values from -1 to 1
- first_position: float32 [1024, 512], P(None, 'dp'), may hold values from -1 to 1
- first_project: float32 [3, 512, 512], P(None, 'dp', 'mp'), may hold values from -1 to 1
- first_output: float32 [512, 512], P('mp', 'dp'), may hold values from -1 to 1
- first_expand: float32 [512, 2048], P('dp', 'mp'), may hold values from -1 to 1
- first_reduce: float32 [2048, 512], P('mp', 'dp'), may hold values from -1 to 1
- first_vectors: float32 [8, 512], P(None, 'dp'), may hold values from -1 to 1
- square_table: float32 [30720, 512], P('mp', 'dp'), may hold values from 0 to 1, as said below
- square_position: float32 [1024, 512], P(None, 'dp'), may hold values from 0 to 1, as said below
- square_project: float32 [3, 512, 512], P(None, 'dp', 'mp'), may hold values from 0 to 1, as said below
- square_output: float32 [512, 512], P('mp', 'dp'), may hold values from 0 to 1, as said below
- square_expand: float32 [512, 2048], P('dp', 'mp'), may hold values from 0 to 1, as said below
- square_reduce: float32 [2048, 512], P('mp', 'dp'), may hold values from 0 to 1, as said below
- square_vectors: float32 [8, 512], P(None, 'dp'), may hold values from 0 to 1, as said below
Outputs:
- updated_table: float32 [30720, 512], P('mp', 'dp')
- moment_table: float32 [30720, 512], P('mp', 'dp')
- second_table: float32 [30720, 512], P('mp', 'dp')
- updated_position: float32 [1024, 512], P(None, 'dp')
- moment_position: float32 [1024, 512], P(None, 'dp')
- second_position: float32 [1024, 512], P(None, 'dp')
- updated_project: float32 [3, 512, 512], P(None, 'dp', 'mp')
- moment_project: float32 [3, 512, 512], P(None, 'dp', 'mp')
- second_project: float32 [3, 512, 512], P(None, 'dp', 'mp')
- updated_output: float32 [512, 512], P('mp', 'dp')
- moment_output: float32 [512, 512], P('mp', 'dp')
- second_output: float32 [512, 512], P('mp', 'dp')
- updated_expand: float32 [512, 2048], P('dp', 'mp')
- moment_expand: float32 [512, 2048], P('dp', 'mp')
- second_expand: float32 [512, 2048], P('dp', 'mp')
- updated_reduce: float32 [2048, 512], P('mp', 'dp')
- moment_reduce: float32 [2048, 512], P('mp', 'dp')
- second_reduce: float32 [2048, 512], P('mp', 'dp')
- updated_vectors: float32 [8, 512], P(None, 'dp')
- moment_vectors: float32 [8, 512], P(None, 'dp')
- second_vectors: float32 [8, 512], P(None, 'dp')
- grad_norm: float32 [], replicated
- loss_terms: float32 [16, 3], P('dp')
- loss_counts: float32 [2], replicated
The draws below stay inside these ranges and needn't reach their ends.
Inputs may be any that keep to these rules, and one draw needn't show every extreme that they name: Tokens t < pad_lengths[s] of sequence s are real, the rest padding; the longest sequence has 1024 tokens. `square_table`: Positive. `square_position`: Positive. `square_project`: Positive. `square_output`: Positive. `square_expand`: Positive. `square_reduce`: Positive. `square_vectors`: Positive.
All inputs are finite; a program needn't handle non-finite values. No bound on the sum of `mlm_flags` on one device may be relied on, other than what follows from the above.
Results may differ from the reference program's by a relative error of at most 0.011.
Values may be sent and summed in bfloat16 or wider, within the bound.
No kernel may reach another device: no remote copies, remote signals or barrier semaphores. Data moves between devices by JAX's collectives and lax.ppermute only.
A program may use at most 384 MiB of HBM per device.

```python
import math
from functools import partial
import jax
import jax.numpy as jnp
import numpy as np
from jax import lax

D = 512
HD = 64
HEADS = 8
FF = 2048
V = 30720
SEQ = 1024
GROUPS = 2
STEP = 10
SEQS = 16
NPARAM = 19402752


def rising_rows(rows, top):
    return 1.0 + (top - 1.0) * jnp.arange(rows, dtype=jnp.float32) / (rows - 1)


def vector_rows(jitter, shifts):
    slope = 0.6 + 1.2 * jnp.arange(D, dtype=jnp.float32) / (D - 1)
    is_gain = jnp.asarray(np.array([1, 0, 0, 1, 0, 0, 1, 0]) == 1)
    return jnp.where(is_gain[:, None], slope[None, :] * jitter, shifts)


def first_moment(key, shape, scale):
    base = jnp.clip(jax.random.normal(key, shape, jnp.float32), -4.0, 4.0)
    return base * (0.11 * scale / math.sqrt(NPARAM))


def second_moment(key, shape, scale):
    ratio = jnp.exp(jax.random.uniform(key, shape, jnp.float32, math.log(0.001), math.log(0.004)))
    return ratio * (scale * scale / NPARAM)


def draw_pad_lengths(key, part):
    key = jax.random.fold_in(key, 9)
    order = jnp.arange(SEQS, dtype=jnp.int32)
    base = SEQ // 4 + SEQ // 8 + (SEQ - SEQ // 4 - SEQ // 8) * order // (SEQS - 1)
    jitter = jax.random.randint(key, (SEQS,), 0, SEQ // 8, dtype=jnp.int32)
    return jnp.where(order == SEQS - 1, SEQ, base - jitter).astype(jnp.int32)


def draw_teacher_table(key, part):
    key = jax.random.fold_in(key, 1)
    base = jnp.clip(jax.random.normal(key, (V, D), jnp.float32), -4.0, 4.0)
    top = 3.0
    return (base * rising_rows(V, top)[:, None] / math.sqrt(D)).astype(jnp.bfloat16)


def draw_student_table(key, part):
    key = jax.random.fold_in(key, 2)
    base = jnp.clip(jax.random.normal(key, (V, D), jnp.float32), -4.0, 4.0)
    top = 3.0
    return base * rising_rows(V, top)[:, None] / math.sqrt(D)


def draw_teacher_vectors(key, part):
    key = jax.random.fold_in(key, 3)
    key_gain, key_shift = jax.random.split(key)
    jitter = jax.random.uniform(key_gain, (8, D), jnp.float32, 0.8, 1.2)
    shifts = jnp.clip(jax.random.normal(key_shift, (8, D), jnp.float32), -4.0, 4.0) * 0.3
    return vector_rows(jitter, shifts).astype(jnp.bfloat16)


def draw_student_vectors(key, part):
    key = jax.random.fold_in(key, 4)
    key_gain, key_shift = jax.random.split(key)
    jitter = jax.random.uniform(key_gain, (8, D), jnp.float32, 0.8, 1.2)
    shifts = jnp.clip(jax.random.normal(key_shift, (8, D), jnp.float32), -4.0, 4.0) * 0.3
    return vector_rows(jitter, shifts)


def draw_first_table(key, part):
    key = jax.random.fold_in(key, 11)
    return first_moment(key, (V, D), 1.0)


def draw_first_position(key, part):
    key = jax.random.fold_in(key, 12)
    return first_moment(key, (SEQ, D), 1.0)


def draw_first_project(key, part):
    key = jax.random.fold_in(key, 13)
    return first_moment(key, (3, D, D), 1.0)


def draw_first_output(key, part):
    key = jax.random.fold_in(key, 14)
    return first_moment(key, (D, D), 1.0)


def draw_first_expand(key, part):
    key = jax.random.fold_in(key, 15)
    return first_moment(key, (D, FF), 1.0)


def draw_first_reduce(key, part):
    key = jax.random.fold_in(key, 16)
    return first_moment(key, (FF, D), 1.0)


def draw_first_vectors(key, part):
    key = jax.random.fold_in(key, 17)
    return first_moment(key, (8, D), 4.0)


def draw_square_table(key, part):
    key = jax.random.fold_in(key, 21)
    return second_moment(key, (V, D), 6.0)


def draw_square_position(key, part):
    key = jax.random.fold_in(key, 22)
    return second_moment(key, (SEQ, D), 1.0)


def draw_square_project(key, part):
    key = jax.random.fold_in(key, 23)
    return second_moment(key, (3, D, D), 1.0)


def draw_square_output(key, part):
    key = jax.random.fold_in(key, 24)
    return second_moment(key, (D, D), 1.0)


def draw_square_expand(key, part):
    key = jax.random.fold_in(key, 25)
    return second_moment(key, (D, FF), 1.0)


def draw_square_reduce(key, part):
    key = jax.random.fold_in(key, 26)
    return second_moment(key, (FF, D), 1.0)


def draw_square_vectors(key, part):
    key = jax.random.fold_in(key, 27)
    return second_moment(key, (8, D), 4.0)


def plant(result, key, least, high):
    place = [jax.random.randint(jax.random.fold_in(key, axis), (), 0, length) for axis, length in enumerate(result.shape)]
    widest = result.shape.index(max(result.shape))
    beside = place[:widest] + [(place[widest] + 1) % result.shape[widest]] + place[widest + 1:]
    return result.at[tuple(place)].set(least).at[tuple(beside)].set(high)


def levels(own_key, shape, cuts, least, top_value):
    factor_of = 1.0
    for axis_at, shards_of in cuts:
        draws = jax.random.uniform(jax.random.fold_in(jax.random.fold_in(own_key, 6), axis_at), (shards_of,), jnp.float32, least / len(cuts), top_value / len(cuts))
        factor_of = factor_of * jnp.repeat(jnp.exp(draws), shape[axis_at] // shards_of).reshape((-1,) + (1,) * (len(shape) - 1 - axis_at))
    return factor_of


def gaussian(stream_key, dims, scale, most, shards=(), kind=jnp.bfloat16):
    factor_of = levels(stream_key, dims, shards, -0.22, 0.18) if shards else 1.0
    drawn = jax.random.normal(stream_key, dims, jnp.float32) * scale * factor_of
    return jnp.minimum(jnp.maximum(drawn, -most), most).astype(kind)


def setup_inputs(seed: int = 0) -> dict:
    arg_keys = jax.random.split(jax.random.key(seed), 34)
    token_ids = plant(jax.random.randint(arg_keys[0], (SEQS, SEQ), 0, V), jax.random.fold_in(arg_keys[0], 1), 0, V - 1).astype(jnp.int32)
    mlm_flags = plant((jax.random.randint(arg_keys[1], (SEQS, SEQ), 0, 20) < 3).astype(jnp.int32), jax.random.fold_in(arg_keys[1], 1), 0, 1)
    pad_lengths = draw_pad_lengths(jax.random.fold_in(arg_keys[33], 71), 0)
    group_ids = plant(jax.random.randint(arg_keys[3], (SEQS,), 0, GROUPS), jax.random.fold_in(arg_keys[3], 1), 0, GROUPS - 1).astype(jnp.int32)
    group_weight = jnp.clip(jnp.exp(jax.random.uniform(arg_keys[4], (GROUPS,), jnp.float32, math.log(0.5), math.log(2.0))), 0.5, 2.0)
    teacher_table = draw_teacher_table(jax.random.fold_in(arg_keys[33], 71), 0)
    teacher_position = gaussian(arg_keys[6], (SEQ, D), 0.1, 0.59765625)
    teacher_project = gaussian(arg_keys[7], (3, D, D), D ** -0.5, 0.25, ((2, 4),))
    teacher_output = gaussian(arg_keys[8], (D, D), (D // 16) ** -0.5, 1.0, ((0, 4),))
    teacher_expand = gaussian(arg_keys[9], (D, FF), D ** -0.5, 0.25, ((1, 4),))
    teacher_reduce = gaussian(arg_keys[10], (FF, D), FF ** -0.5, 0.125, ((0, 4),))
    teacher_vectors = draw_teacher_vectors(jax.random.fold_in(arg_keys[33], 71), 0)
    student_table = draw_student_table(jax.random.fold_in(arg_keys[33], 71), 0)
    student_position = gaussian(arg_keys[13], (SEQ, D), 0.1, 0.6, ((1, 8),), jnp.float32)
    student_project = gaussian(arg_keys[14], (3, D, D), D ** -0.5, 0.25, ((1, 8), (2, 4)), jnp.float32)
    student_output = gaussian(arg_keys[15], (D, D), (D // 16) ** -0.5, 1.0, ((0, 4), (1, 8)), jnp.float32)
    student_expand = gaussian(arg_keys[16], (D, FF), D ** -0.5, 0.25, ((0, 8), (1, 4)), jnp.float32)
    student_reduce = gaussian(arg_keys[17], (FF, D), FF ** -0.5, 0.125, ((0, 4), (1, 8)), jnp.float32)
    student_vectors = draw_student_vectors(jax.random.fold_in(arg_keys[33], 71), 0)
    first_table = draw_first_table(jax.random.fold_in(arg_keys[33], 71), 0)
    first_position = draw_first_position(jax.random.fold_in(arg_keys[33], 71), 0)
    first_project = draw_first_project(jax.random.fold_in(arg_keys[33], 71), 0)
    first_output = draw_first_output(jax.random.fold_in(arg_keys[33], 71), 0)
    first_expand = draw_first_expand(jax.random.fold_in(arg_keys[33], 71), 0)
    first_reduce = draw_first_reduce(jax.random.fold_in(arg_keys[33], 71), 0)
    first_vectors = draw_first_vectors(jax.random.fold_in(arg_keys[33], 71), 0)
    square_table = draw_square_table(jax.random.fold_in(arg_keys[33], 71), 0)
    square_position = draw_square_position(jax.random.fold_in(arg_keys[33], 71), 0)
    square_project = draw_square_project(jax.random.fold_in(arg_keys[33], 71), 0)
    square_output = draw_square_output(jax.random.fold_in(arg_keys[33], 71), 0)
    square_expand = draw_square_expand(jax.random.fold_in(arg_keys[33], 71), 0)
    square_reduce = draw_square_reduce(jax.random.fold_in(arg_keys[33], 71), 0)
    square_vectors = draw_square_vectors(jax.random.fold_in(arg_keys[33], 71), 0)
    return dict(token_ids=token_ids, mlm_flags=mlm_flags, pad_lengths=pad_lengths, group_ids=group_ids, group_weight=group_weight, teacher_table=teacher_table, teacher_position=teacher_position, teacher_project=teacher_project, teacher_output=teacher_output, teacher_expand=teacher_expand, teacher_reduce=teacher_reduce, teacher_vectors=teacher_vectors, student_table=student_table, student_position=student_position, student_project=student_project, student_output=student_output, student_expand=student_expand, student_reduce=student_reduce, student_vectors=student_vectors, first_table=first_table, first_position=first_position, first_project=first_project, first_output=first_output, first_expand=first_expand, first_reduce=first_reduce, first_vectors=first_vectors, square_table=square_table, square_position=square_position, square_project=square_project, square_output=square_output, square_expand=square_expand, square_reduce=square_reduce, square_vectors=square_vectors)


@jax.custom_vjp
def low(v):
    return lax.optimization_barrier(v.astype(jnp.bfloat16)).astype(jnp.float32)

@jax.custom_vjp
def low_back(v):
    return v

def low_keep(v):
    return (low(v), None)

def low_pass(kept, grad):
    return (grad,)

def back_keep(v):
    return (v, None)

def back_low(kept, grad):
    return (low(grad),)
low.defvjp(low_keep, low_pass)
low_back.defvjp(back_keep, back_low)
highest = lax.Precision.HIGHEST
eps_norm = 1e-05
mask_token = 103
temper = 2.0
beta_first = 0.9
beta_second = 0.999
adam_eps = 1e-08
rate_table = 0.5
rate_matrix = 0.1
rate_vector = 0.3
weight_decay = 0.01
clip_limit = 1.0

def layer_norm(x, gain, shift):
    centre = x - lax.optimization_barrier(jnp.mean(x, -1, keepdims=True))
    spread = lax.optimization_barrier(jnp.mean(centre * centre, -1, keepdims=True))
    return centre * lax.rsqrt(spread + eps_norm) * gain + shift

def matmul(left, right):
    return jnp.dot(left, right, precision=highest)

def encode(weights, inputs, length):
    table, position, project, output, expand, reduce_value, vectors = weights
    embedded = jnp.take(table, inputs, axis=0) + position
    x_zero = layer_norm(embedded, vectors[0], vectors[1])
    x_low = low(x_zero)
    parts = [low(low_back(matmul(x_low, project[t]))).reshape(SEQ, HEADS, HD) for t in range(3)]
    score = jnp.einsum('qhe,khe->hqk', parts[0], parts[1], precision=highest) * HD ** (-0.5)
    score = low_back(score)
    valid = jnp.arange(SEQ) < length
    score = jnp.where(valid[None, None, :], score, -1e+30)
    weight = low(jax.nn.softmax(score, axis=-1))
    attn = jnp.einsum('hqk,khe->qhe', weight, parts[2], precision=highest).reshape(SEQ, D)
    attn = low(low_back(attn))
    branch = low_back(matmul(attn, output))
    x_one = layer_norm(branch + vectors[2] + x_zero, vectors[3], vectors[4])
    hidden = low_back(matmul(low(x_one), expand))
    active = low(jax.nn.gelu(hidden, approximate=False))
    x_two = layer_norm(low_back(matmul(active, reduce_value)) + vectors[5] + x_one, vectors[6], vectors[7])
    return x_two

def sequence_terms(student, teacher, inputs, targets, length, tok_weight, mask_weight):
    x_student = encode(student, inputs, length)
    x_teacher = encode(teacher, inputs, length)
    s_logit = low_back(matmul(low(x_student), student[0].T))
    t_logit = matmul(low(x_teacher), teacher[0].T)
    s_half = jax.nn.log_softmax(s_logit / temper, axis=-1)
    t_half = jax.nn.log_softmax(t_logit / temper, axis=-1)
    diverge = temper * temper * lax.optimization_barrier(jnp.sum(jnp.exp(t_half) * (t_half - s_half), -1))
    s_full = jax.nn.log_softmax(s_logit, axis=-1)
    missed = -jnp.take_along_axis(s_full, targets[:, None], axis=-1)[:, 0]
    s_len = jnp.sqrt(lax.optimization_barrier(jnp.sum(x_student * x_student, -1)))
    t_len = jnp.sqrt(lax.optimization_barrier(jnp.sum(x_teacher * x_teacher, -1)))
    align = lax.optimization_barrier(jnp.sum(x_student * x_teacher, -1)) / (s_len * t_len)
    return jnp.stack([jnp.sum(tok_weight * diverge), jnp.sum(mask_weight * missed), jnp.sum(tok_weight * (1.0 - align))])

def reference(token_ids, mlm_flags, pad_lengths, group_ids, group_weight, teacher_table, teacher_position, teacher_project, teacher_output, teacher_expand, teacher_reduce, teacher_vectors, student_table, student_position, student_project, student_output, student_expand, student_reduce, student_vectors, first_table, first_position, first_project, first_output, first_expand, first_reduce, first_vectors, square_table, square_position, square_project, square_output, square_expand, square_reduce, square_vectors):
    teacher = tuple((w.astype(jnp.float32) for w in (teacher_table, teacher_position, teacher_project, teacher_output, teacher_expand, teacher_reduce, teacher_vectors)))
    masters = (student_table, student_position, student_project, student_output, student_expand, student_reduce, student_vectors)
    firsts = (first_table, first_position, first_project, first_output, first_expand, first_reduce, first_vectors)
    squares_in = (square_table, square_position, square_project, square_output, square_expand, square_reduce, square_vectors)
    inputs = jnp.where(mlm_flags == 1, mask_token, token_ids).astype(jnp.int32)
    nonpad = (jnp.arange(SEQ)[None, :] < pad_lengths[:, None]).astype(jnp.float32)
    masked = mlm_flags.astype(jnp.float32) * nonpad
    chosen = group_ids[:, None] == jnp.arange(GROUPS)[None, :]
    seq_weight = lax.optimization_barrier(jnp.sum(jnp.where(chosen, group_weight[None, :], 0.0), -1))
    tok_weight = seq_weight[:, None] * nonpad
    mask_weight = seq_weight[:, None] * masked
    count_tok = jnp.sum(nonpad)
    count_mask = jnp.maximum(jnp.sum(masked), 1.0)

    def total(params):
        student = tuple((low(w) for w in params))

        def one_sequence(carry, row):
            terms = jax.checkpoint(partial(sequence_terms, student, teacher))(*row)
            return (carry, terms)
        _, per_seq = lax.scan(one_sequence, jnp.zeros((), jnp.float32), (inputs, token_ids, pad_lengths, tok_weight, mask_weight))
        sums = lax.optimization_barrier(jnp.sum(per_seq, 0))
        loss = (5.0 * sums[0] + sums[2]) / count_tok + 2.0 * sums[1] / count_mask
        return (loss, per_seq)
    loss, pull, per_seq = jax.vjp(total, masters, has_aux=True)
    grads = pull(jnp.ones_like(loss))[0]
    norm = jnp.sqrt(sum((jnp.sum(g * g) for g in grads)))
    factor = clip_limit / jnp.maximum(norm, clip_limit)
    results = []
    for index in range(7):
        rate = rate_vector if index == 6 else rate_table if index == 0 else rate_matrix
        decay = 0.0 if index == 6 else weight_decay
        clipped = grads[index] * factor
        new_first = beta_first * firsts[index] + (1.0 - beta_first) * clipped
        new_square = beta_second * squares_in[index] + (1.0 - beta_second) * clipped * clipped
        first_hat = new_first / (1.0 - beta_first ** STEP)
        square_hat = new_square / (1.0 - beta_second ** STEP)
        master = masters[index]
        updated = master - rate * (first_hat / (jnp.sqrt(square_hat) + adam_eps) + decay * master)
        results += [updated, new_first, new_square]
    counts = jnp.stack([count_tok, count_mask])
    return (*results, norm, per_seq, counts)
```

```python
from functools import partial

import jax
import jax.numpy as jnp
from jax import lax
from jax.experimental import pallas as pl
from jax.experimental.pallas import tpu as pltpu
from jax.sharding import PartitionSpec as P

HD = 64
STEP = 10
LANES = 128


eps_norm = 1e-05
mask_token = 103
temper = 2.0
beta_first = 0.9
beta_second = 0.999
adam_eps = 1e-08
rate_table = 0.5
rate_matrix = 0.1
rate_vector = 0.3
weight_decay = 0.01
clip_limit = 1.0
bf = jnp.bfloat16
f32 = jnp.float32
vmem_bytes = 56 * 1024 * 1024


def layer_norm(x, gain, shift):
    centre = x - jnp.mean(x, -1, keepdims=True)
    spread = jnp.mean(centre * centre, -1, keepdims=True)
    return centre * lax.rsqrt(spread + eps_norm) * gain + shift


def norm_grad(pre, gain, shift, grad):
    _, pull = jax.vjp(layer_norm, pre, gain, shift)
    return pull(grad)


def swap(x, bit):
    count = lax.axis_size("dp")
    return lax.ppermute(x, "dp", [(i, i ^ bit) for i in range(count)])


def rotate(x, by=1):
    count = lax.axis_size("mp")
    return lax.ppermute(x, "mp", [(i, (i + by) % count) for i in range(count)])


def chip_bits():
    count = lax.axis_size("dp")
    bits = []
    bit = 2
    while bit < count:
        bits.append(bit)
        bit *= 2
    return bits


def ordered(bit, mine, other, axis):
    low = (lax.axis_index("dp") & bit) == 0
    return jnp.where(
        low, jnp.concatenate([mine, other], axis), jnp.concatenate([other, mine], axis)
    )


def gather_dp(x):
    rows, columns = x.shape
    core = lax.axis_index("dp") & 1
    half = columns // 2
    keep = lax.dynamic_slice_in_dim(x, core * half, half, 1)
    give = lax.dynamic_slice_in_dim(x, (1 - core) * half, half, 1)
    pair = ordered(1, keep, swap(give, 1), 0)
    parts = [pair[:, : half // 2], pair[:, half // 2 :]]
    bits = chip_bits()
    one = parts[0]
    for bit in bits:
        one = ordered(bit, one, swap(one, bit), 0)
    two = parts[1][None]
    for bit in bits[::-1]:
        got = swap(two, bit)
        low = (lax.axis_index("dp") & bit) == 0
        two = jnp.where(
            low, jnp.stack([two, got], 1), jnp.stack([got, two], 1)
        ).reshape(-1, 2 * rows, half - half // 2)
    two = two.reshape(-1, half - half // 2)
    return ordered(
        1,
        jnp.concatenate([one, two], 1),
        jnp.concatenate([swap(one, 1), swap(two, 1)], 1),
        1,
    )


def scatter_dp(y):
    total_rows, columns = y.shape
    count = lax.axis_size("dp")
    rows = total_rows // count
    index = lax.axis_index("dp")
    core = index & 1
    half = columns // 2
    keep = lax.dynamic_slice_in_dim(y, core * half, half, 1)
    give = lax.dynamic_slice_in_dim(y, (1 - core) * half, half, 1).astype(bf)
    summed = keep.astype(f32) + swap(give, 1).astype(f32)
    parts = [summed[:, : half // 2], summed[:, half // 2 :]]
    bits = chip_bits()
    done = []
    for which, part in enumerate(parts):
        left = part.reshape(count // 2, 2 * rows, -1)
        low = 1
        for bit in bits[::-1] if which == 0 else bits:
            mine = (index & bit) != 0
            groups = left.shape[0]
            if which == 0:
                split = left.reshape(2, groups // 2, 2 * rows, -1)
                first, second = split[0], split[1]
            else:
                split = left.reshape(groups // 2, 2, 2 * rows, -1)
                first, second = split[:, 0], split[:, 1]
            send = jnp.where(mine, first, second).astype(bf)
            left = jnp.where(mine, second, first) + swap(send, bit).astype(f32)
        done.append(left[0])
    left = jnp.concatenate(done, 1)
    keep = lax.dynamic_slice_in_dim(left, core * rows, rows, 0)
    give = lax.dynamic_slice_in_dim(left, (1 - core) * rows, rows, 0).astype(bf)
    return ordered(1, keep, swap(give, 1).astype(f32), 1)


def ring_list(x):
    got = [x]
    for _ in range(lax.axis_size("mp") - 1):
        got.append(rotate(got[-1]))
    return got


def natural(entries):
    count = lax.axis_size("mp")
    index = lax.axis_index("mp")
    stacked = jnp.stack(entries)
    return jnp.stack(
        [
            lax.dynamic_index_in_dim(stacked, (index - i) % count, 0, keepdims=False)
            for i in range(count)
        ]
    )


def ring_sum(terms):
    count = lax.axis_size("mp")
    total = terms[1 % count]
    for k in range(2, count + 1):
        total = terms[k % count].astype(f32) + rotate(total.astype(bf)).astype(f32)
    return total


def sum_all(x):
    bit = 1
    while bit < lax.axis_size("dp"):
        x = x + swap(x, bit)
        bit *= 2
    count = lax.axis_size("mp")
    return jnp.sum(natural([x] + [rotate(x, by) for by in range(1, count)]), 0)


def tile_of(total, cap):
    best = LANES
    for size in range(LANES, min(total, cap) + 1, LANES):
        if total % size == 0:
            best = size
    return best


def call(body, grid, in_specs, out_specs, out_shape, scratch, flops, moved):
    return pl.pallas_call(
        body,
        grid=grid,
        in_specs=in_specs,
        out_specs=out_specs,
        out_shape=out_shape,
        scratch_shapes=scratch,
        compiler_params=pltpu.CompilerParams(
            dimension_semantics=("arbitrary",) * len(grid), vmem_limit_bytes=vmem_bytes
        ),
        cost_estimate=pl.CostEstimate(flops=flops, bytes_accessed=moved, transcendentals=0),
    )


def whole(shape):
    return pl.BlockSpec(shape, lambda j: (0,) * len(shape))


def against(x, table, flipped):
    dims = (((1,), (0,)), ((), ())) if flipped else (((1,), (1,)), ((), ()))
    return lax.dot_general(x, table, dims, preferred_element_type=f32)


def table_spec(width, tile, flipped):
    if flipped:
        return pl.BlockSpec((width, tile), lambda j: (0, j))
    return pl.BlockSpec((tile, width), lambda j: (j, 0))


def pick_rows(ids, table, flipped):
    width, vocab = table.shape if flipped else table.shape[::-1]
    rows = ids.shape[0]
    tile = tile_of(vocab, 1536)

    def body(ids_ref, table_ref, out_ref, total):
        j = pl.program_id(0)

        @pl.when(j == 0)
        def _():
            total[...] = jnp.zeros_like(total)

        lane = lax.broadcasted_iota(jnp.int32, (rows, tile), 1)
        hot = jnp.where(lane == ids_ref[...] - j * tile, 1.0, 0.0).astype(bf)
        dims = (((1,), (1,)), ((), ())) if flipped else (((1,), (0,)), ((), ()))
        total[...] += lax.dot_general(hot, table_ref[...], dims, preferred_element_type=f32)

        @pl.when(j == pl.num_programs(0) - 1)
        def _():
            out_ref[...] = total[...].astype(bf)

    return call(
        body,
        (vocab // tile,),
        [whole((rows, 1)), table_spec(width, tile, flipped)],
        whole((rows, width)),
        jax.ShapeDtypeStruct((rows, width), bf),
        [pltpu.VMEM((rows, width), f32)],
        2 * rows * width * vocab,
        2 * width * vocab,
    )(ids, table)


def lane_value(values, j):
    lane = lax.broadcasted_iota(jnp.int32, values.shape, 1)
    return jnp.sum(jnp.where(lane == j, values, 0.0), 1, keepdims=True)


def head_tile(vocab):
    return tile_of(vocab, 1536)


def head_pass(x, table, flipped, beside=None):
    width, vocab = table.shape if flipped else table.shape[::-1]
    rows = x.shape[0]
    tile = head_tile(vocab)
    student = beside is not None
    step = min(rows, 128)

    def body(*refs):
        if student:
            x_ref, table_ref, other_ref, weight_ref, target_ref, half_ref, peaks_ref, stats_ref = refs
        else:
            x_ref, table_ref, half_ref, peaks_ref, stats_ref = refs
        j = pl.program_id(0)

        @pl.when(j == 0)
        def _():
            lane = lax.broadcasted_iota(jnp.int32, stats_ref.shape, 1)
            stats_ref[...] = jnp.where(lane == 0, -1e30, 0.0)
            peaks_ref[...] = jnp.zeros_like(peaks_ref)

        for begin in range(0, rows, step):
            part = pl.ds(begin, step)
            z = against(x_ref[part, :], table_ref[...], flipped)
            before = stats_ref[part, :]
            peak = jnp.maximum(before[:, 0:1], jnp.max(z, 1, keepdims=True))
            half = jnp.exp((z - peak) * 0.5)
            half_ref[part, :] = half.astype(bf)
            shrink = jnp.exp((before[:, 0:1] - peak) * 0.5)
            half_sum = before[:, 1:2] * shrink + jnp.sum(half, 1, keepdims=True)
            if student:
                full_sum = before[:, 2:3] * (shrink * shrink) + jnp.sum(
                    half * half, 1, keepdims=True
                )
                weight = lane_value(weight_ref[part, :], j)
                cross = before[:, 3:4] + weight * jnp.sum(
                    other_ref[part, :].astype(f32) * z, 1, keepdims=True
                )
                lane = lax.broadcasted_iota(jnp.int32, z.shape, 1)
                hit = lane == target_ref[part, :] - j * tile
                target = before[:, 4:5] + jnp.sum(jnp.where(hit, z, 0.0), 1, keepdims=True)
                values = (peak, half_sum, full_sum, cross, target)
            else:
                own = before[:, 3:4] * shrink + jnp.sum(half * z, 1, keepdims=True)
                values = (peak, half_sum, before[:, 2:3], own)
            lane = lax.broadcasted_iota(jnp.int32, before.shape, 1)
            after = before
            for slot, value in enumerate(values):
                after = jnp.where(lane == slot, value, after)
            stats_ref[part, :] = after
            peaks_ref[part, :] = jnp.where(lane == j, peak, peaks_ref[part, :])

    block = pl.BlockSpec((rows, tile), lambda j: (0, j))
    lanes = whole((rows, LANES))
    in_specs = [whole((rows, width)), table_spec(width, tile, flipped)]
    operands = [x, table]
    if student:
        in_specs += [block, lanes, whole((rows, 1))]
        operands += list(beside)
    stat = jax.ShapeDtypeStruct((rows, LANES), f32)
    return call(
        body,
        (vocab // tile,),
        in_specs,
        [block, lanes, lanes],
        [jax.ShapeDtypeStruct((rows, vocab), bf), stat, stat],
        [],
        4 * rows * width * vocab,
        2 * width * vocab + 2 * rows * vocab * (2 if student else 1),
    )(*operands)


def head_back(s_half, t_half, s_scale, t_scale, f_scale, hit_scale, targets, table):
    width, vocab = table.shape
    rows = s_half.shape[0]
    tile = head_tile(vocab)
    step = min(rows, 128)

    def body(s_ref, t_ref, a_ref, b_ref, c_ref, h_ref, target_ref, table_ref, d_ref, out_ref, total):
        j = pl.program_id(0)

        @pl.when(j == 0)
        def _():
            total[...] = jnp.zeros_like(total)

        for begin in range(0, rows, step):
            part = pl.ds(begin, step)
            half = s_ref[part, :].astype(f32)
            grad = half * (lane_value(a_ref[part, :], j) + half * lane_value(c_ref[part, :], j))
            grad -= t_ref[part, :].astype(f32) * lane_value(b_ref[part, :], j)
            lane = lax.broadcasted_iota(jnp.int32, half.shape, 1)
            hit = lane == target_ref[part, :] - j * tile
            low = (grad - jnp.where(hit, h_ref[part, :], 0.0)).astype(bf)
            d_ref[part, :] = low
            total[part, :] += lax.dot_general(
                low, table_ref[...], (((1,), (1,)), ((), ())), preferred_element_type=f32
            )

        @pl.when(j == pl.num_programs(0) - 1)
        def _():
            out_ref[...] = total[...].astype(bf)

    block = pl.BlockSpec((rows, tile), lambda j: (0, j))
    lanes = whole((rows, LANES))
    column = whole((rows, 1))
    return call(
        body,
        (vocab // tile,),
        [block, block, lanes, lanes, lanes, column, column, table_spec(width, tile, True)],
        [block, whole((rows, width))],
        [jax.ShapeDtypeStruct((rows, vocab), bf), jax.ShapeDtypeStruct((rows, width), bf)],
        [pltpu.VMEM((rows, width), f32)],
        2 * rows * width * vocab,
        2 * width * vocab + 6 * rows * vocab,
    )(s_half, t_half, s_scale, t_scale, f_scale, hit_scale, targets, table)


def table_grad(x_flipped, d_logits):
    width, rows = x_flipped[0].shape
    vocab = d_logits[0].shape[1]
    tile = tile_of(vocab, 1536)
    count = len(d_logits)

    def body(*refs):
        total = None
        for x_ref, d_ref in zip(refs[:count], refs[count : 2 * count]):
            term = jnp.dot(x_ref[...], d_ref[...], preferred_element_type=f32)
            total = term if total is None else total + term
        refs[-1][...] = total

    return call(
        body,
        (vocab // tile,),
        [whole((width, rows))] * count + [pl.BlockSpec((rows, tile), lambda j: (0, j))] * count,
        pl.BlockSpec((width, tile), lambda j: (0, j)),
        jax.ShapeDtypeStruct((width, vocab), f32),
        [],
        2 * rows * count * width * vocab,
        2 * rows * count * vocab + 4 * width * vocab,
    )(*x_flipped, *d_logits)


def add_rows(base, e_flipped, ids):
    width, vocab = base.shape
    rows = ids[0].shape[0]
    tile = tile_of(vocab, 1536)
    count = len(ids)

    def body(*refs):
        j = pl.program_id(0)
        total = refs[0][...]
        for e_ref, ids_ref in zip(refs[1 : 1 + count], refs[1 + count : 1 + 2 * count]):
            lane = lax.broadcasted_iota(jnp.int32, (rows, tile), 1)
            hot = jnp.where(lane == ids_ref[...] - j * tile, 1.0, 0.0).astype(bf)
            total += jnp.dot(e_ref[...], hot, preferred_element_type=f32)
        refs[-1][...] = total.astype(bf)

    block = pl.BlockSpec((width, tile), lambda j: (0, j))
    return call(
        body,
        (vocab // tile,),
        [block] + [whole((width, rows))] * count + [whole((rows, 1))] * count,
        block,
        jax.ShapeDtypeStruct((width, vocab), bf),
        [],
        2 * rows * count * width * vocab,
        6 * width * vocab,
    )(base, *e_flipped, *ids)


def gather_sequence(x, spans):
    whole_x = ordered(1, x, swap(x, 1), 1)
    if spans > 1:
        count = lax.axis_size("mp")
        groups = [list(range(i, i + spans)) for i in range(0, count, spans)]
        whole_x = lax.all_gather(
            whole_x, "mp", axis=1, axis_index_groups=groups, tiled=True
        )
    return whole_x


def scatter_sequence(x, spans):
    if spans > 1:
        count = lax.axis_size("mp")
        groups = [list(range(i, i + spans)) for i in range(0, count, spans)]
        x = lax.psum_scatter(
            x, "mp", scatter_dimension=1, axis_index_groups=groups, tiled=True
        )
    rows = x.shape[1] // 2
    core = lax.axis_index("dp") & 1
    keep = lax.dynamic_slice_in_dim(x, core * rows, rows, 1)
    give = lax.dynamic_slice_in_dim(x, (1 - core) * rows, rows, 1)
    return keep + swap(give, 1)


def masked_scores(query, keys, valid):
    score = jnp.einsum("qhe,khe->hqk", query, keys, preferred_element_type=f32) * HD ** (-0.5)
    return jnp.where(valid[None, None, :], score, -1e30)


def rows_times(x, flipped):
    return lax.dot_general(x, flipped, (((1,), (1,)), ((), ())), preferred_element_type=f32)


def layer_forward(weights, embedded, valid, spans):
    project, output_t, expand, reduce_t, vectors = weights
    rows = embedded.shape[0]
    x_zero = layer_norm(embedded, vectors[0], vectors[1])
    x_low = x_zero.astype(bf)
    query, keys, values = [
        jnp.dot(x_low, project[t], preferred_element_type=f32).astype(bf) for t in range(3)
    ]
    both = gather_sequence(jnp.stack([keys, values]), spans)
    query = query.reshape(rows, -1, HD)
    keys = both[0].reshape(both.shape[1], -1, HD)
    values = both[1].reshape(both.shape[1], -1, HD)
    score = masked_scores(query, keys, valid)
    peak = jnp.max(score, -1, keepdims=True)
    expo = jnp.exp(score - peak)
    total = jnp.sum(expo, -1, keepdims=True)
    weight = expo / total
    log_total = peak + jnp.log(total)
    attn = jnp.einsum("hqk,khe->qhe", weight.astype(bf), values, preferred_element_type=f32)
    attn = attn.reshape(rows, -1).astype(bf)
    x_one_pre = rows_times(attn, output_t) + vectors[2] + x_zero
    x_one = layer_norm(x_one_pre, vectors[3], vectors[4])
    x_one_low = x_one.astype(bf)
    hidden = jnp.dot(x_one_low, expand, preferred_element_type=f32)
    active = jax.nn.gelu(hidden, approximate=False).astype(bf)
    x_two_pre = rows_times(active, reduce_t) + vectors[5] + x_one
    x_two = layer_norm(x_two_pre, vectors[6], vectors[7])
    kept = (
        embedded, x_low, query, keys, values, log_total, attn, x_one_pre, x_one_low, hidden,
        active, x_two_pre,
    )
    return (x_two, kept)


def layer_backward(weights, kept, d_two, valid, spans):
    project, output_t, expand, reduce_t, vectors = weights
    (
        embedded, x_low, query, keys, values, log_total, attn, x_one_pre, x_one_low, hidden,
        active, x_two_pre,
    ) = kept
    rows = embedded.shape[0]
    d_two_pre, g_six, g_seven = norm_grad(x_two_pre, vectors[6], vectors[7], d_two)
    d_reduce = d_two_pre.astype(bf)
    g_reduce_t = jnp.dot(d_reduce.T, active, preferred_element_type=f32)
    d_active = jnp.dot(d_reduce, reduce_t, preferred_element_type=f32)
    _, gelu_pull = jax.vjp(partial(jax.nn.gelu, approximate=False), hidden)
    d_hidden = gelu_pull(d_active)[0].astype(bf)
    g_expand = jnp.dot(x_one_low.T, d_hidden, preferred_element_type=f32)
    d_one = rows_times(d_hidden, expand) + d_two_pre
    d_one_pre, g_three, g_four = norm_grad(x_one_pre, vectors[3], vectors[4], d_one)
    d_branch = d_one_pre.astype(bf)
    g_output_t = jnp.dot(d_branch.T, attn, preferred_element_type=f32)
    d_attn = jnp.dot(d_branch, output_t, preferred_element_type=f32).astype(bf)
    d_attn = d_attn.reshape(query.shape)
    weight = jnp.exp(masked_scores(query, keys, valid) - log_total)
    d_values = jnp.einsum("hqk,qhe->khe", weight.astype(bf), d_attn, preferred_element_type=f32)
    d_weight = jnp.einsum("qhe,khe->hqk", d_attn, values, preferred_element_type=f32)
    d_score = (weight * (d_weight - jnp.sum(weight * d_weight, -1, keepdims=True))).astype(bf)
    d_query = jnp.einsum("hqk,khe->qhe", d_score, keys, preferred_element_type=f32) * HD ** (-0.5)
    d_keys = jnp.einsum("hqk,qhe->khe", d_score, query, preferred_element_type=f32) * HD ** (-0.5)
    length = keys.shape[0]
    d_both = scatter_sequence(
        jnp.stack([d_keys.reshape(length, -1), d_values.reshape(length, -1)]), spans
    )
    d_stacked = [
        d_query.reshape(rows, -1).astype(bf),
        d_both[0].astype(bf),
        d_both[1].astype(bf),
    ]
    g_project = [jnp.dot(x_low.T, d, preferred_element_type=f32) for d in d_stacked]
    d_zero = sum(rows_times(d, project[t]) for t, d in enumerate(d_stacked)) + d_one_pre
    d_embed, g_one, g_two = norm_grad(embedded, vectors[0], vectors[1], d_zero)
    g_vectors = jnp.stack(
        [g_one, g_two, jnp.sum(d_one_pre, 0), g_three, g_four, jnp.sum(d_two_pre, 0), g_six, g_seven]
    )
    return (d_embed, (g_project, g_output_t, g_expand, g_reduce_t, g_vectors))


def cosine_loss(x_student, x_teacher):
    s_len = jnp.sqrt(jnp.sum(x_student * x_student, -1))
    t_len = jnp.sqrt(jnp.sum(x_teacher * x_teacher, -1))
    return 1.0 - jnp.sum(x_student * x_teacher, -1) / (s_len * t_len)


def adam_update(master, first, square, grad, factor, rate, decay):
    clipped = grad * factor
    new_first = beta_first * first + (1.0 - beta_first) * clipped
    new_square = beta_second * square + (1.0 - beta_second) * clipped * clipped
    first_hat = new_first / (1.0 - beta_first**STEP)
    square_hat = new_square / (1.0 - beta_second**STEP)
    updated = master - rate * (first_hat / (jnp.sqrt(square_hat) + adam_eps) + decay * master)
    return [updated, new_first, new_square]


def body(
    token_ids,
    mlm_flags,
    pad_lengths,
    group_ids,
    group_weight,
    teacher_table,
    teacher_position,
    teacher_project,
    teacher_output,
    teacher_expand,
    teacher_reduce,
    teacher_vectors,
    student_table,
    student_position,
    student_project,
    student_output,
    student_expand,
    student_reduce,
    student_vectors,
    first_table,
    first_position,
    first_project,
    first_output,
    first_expand,
    first_reduce,
    first_vectors,
    square_table,
    square_position,
    square_project,
    square_output,
    square_expand,
    square_reduce,
    square_vectors,
):
    mp, dp = lax.axis_size("mp"), lax.axis_size("dp")
    place, index = lax.axis_index("mp"), lax.axis_index("dp")
    core = index & 1
    batch, length = token_ids.shape
    spans = mp // (2 * batch)
    rows = length // (2 * spans)
    vocab_rows = student_table.shape[0]
    share = student_table.shape[1]
    features = share * dp
    start = place * vocab_rows

    packed = jnp.concatenate(
        [
            token_ids * 2 + mlm_flags,
            jnp.pad((pad_lengths * 256 + group_ids)[None], ((0, 0), (0, length - batch))),
        ]
    )
    packed = ordered(1, packed[None], swap(packed, 1)[None], 0)
    column_ids = packed[:, :batch].reshape(2 * batch, spans, 2, rows)
    lengths = (packed[:, batch, :batch] // 256).reshape(-1)
    groups = (packed[:, batch, :batch] % 256).reshape(-1)
    chosen = groups[:, None] == jnp.arange(group_weight.shape[0])[None, :]
    seq_weight = jnp.sum(jnp.where(chosen, group_weight[None, :], 0.0), -1)
    line = lax.dynamic_index_in_dim(column_ids, core, 2, keepdims=False).reshape(mp, rows)
    line_targets, line_flags = line // 2, line % 2
    line_inputs = jnp.where(line_flags == 1, mask_token, line_targets)
    line_sequence = jnp.arange(mp) // spans
    line_part = (jnp.arange(mp) % spans) * 2 + core
    line_positions = line_part[:, None] * rows + jnp.arange(rows)[None, :]
    line_real = (line_positions < jnp.repeat(lengths, spans)[:, None]).astype(f32)
    line_masked = line_flags.astype(f32) * line_real
    line_weight = jnp.repeat(seq_weight, spans)[:, None]
    tok_weight, mask_weight = line_weight * line_real, line_weight * line_masked
    own_part = lax.dynamic_index_in_dim(line_part, place, 0, keepdims=False)
    own_length = lax.dynamic_index_in_dim(jnp.repeat(lengths, spans), place, 0, keepdims=False)
    valid = jnp.arange(length) < own_length

    def chunk(values, k):
        return lax.dynamic_index_in_dim(values, (place - k) % mp, 0, keepdims=False)

    local_inputs = [(chunk(line_inputs, k) - start)[:, None] for k in range(mp)]
    local_targets = [(chunk(line_targets, k) - start)[:, None] for k in range(mp)]

    nonpad = (jnp.arange(length)[None, :] < pad_lengths[:, None]).astype(f32)
    masked = mlm_flags.astype(f32) * nonpad
    counts = jnp.stack([jnp.sum(nonpad), jnp.sum(masked)])
    counts = jnp.pad(counts[None], ((0, 7), (0, LANES - 2)))
    bit = 1
    while bit < dp:
        counts = counts + swap(counts, bit)
        bit *= 2
    count_tok, count_mask = counts[0, 0], jnp.maximum(counts[0, 1], 1.0)

    def joined(project, output, expand, reduce_value):
        return jnp.concatenate(
            [project[0], project[1], project[2], output.T, expand, reduce_value.T], 1
        )

    def opened(gathered):
        blocks = gathered.reshape(features, mp, -1)
        head_cut = student_project.shape[2]
        unit_cut = student_expand.shape[1]
        cuts = [head_cut] * 4 + [unit_cut] * 2
        pieces, at = [], 0
        for cut in cuts:
            pieces.append(blocks[:, :, at : at + cut].reshape(features, mp * cut))
            at += cut
        return (pieces[:3], pieces[3], pieces[4], pieces[5])

    def cut_rows(x, axis):
        return lax.dynamic_slice_in_dim(x, index * share, share, axis)

    table_low = student_table.T.astype(bf)
    s_table = gather_dp(table_low)
    t_share = joined(
        cut_rows(teacher_project, 1),
        cut_rows(teacher_output, 1),
        cut_rows(teacher_expand, 0),
        cut_rows(teacher_reduce, 1),
    )
    s_share = joined(
        student_project.astype(bf),
        student_output.astype(bf),
        student_expand.astype(bf),
        student_reduce.astype(bf),
    )
    t_share = natural(ring_list(t_share)).transpose(1, 0, 2).reshape(share, -1)
    s_share = natural(ring_list(s_share)).transpose(1, 0, 2).reshape(share, -1)
    small = jnp.concatenate([student_position.T, student_vectors.T], 1).astype(bf)
    small = jnp.pad(small, ((0, 0), (0, LANES - student_vectors.shape[0])))
    t_layer = opened(gather_dp(t_share)) + (teacher_vectors.astype(f32),)
    s_share = gather_dp(jnp.concatenate([s_share, small], 1))
    s_small = s_share[:, -(length + LANES) :]
    s_vectors = s_small[:, length : length + student_vectors.shape[0]].T.astype(f32)
    s_layer = opened(s_share[:, : -(length + LANES)]) + (s_vectors,)
    s_position = lax.dynamic_slice_in_dim(s_small, own_part * rows, rows, 1).T
    t_position = lax.dynamic_slice_in_dim(teacher_position, own_part * rows, rows, 0)

    t_rows = ring_sum([pick_rows(ids, teacher_table, False) for ids in local_inputs])
    s_rows = ring_sum([pick_rows(ids, s_table, True) for ids in local_inputs])
    t_two, _ = layer_forward(t_layer, t_rows + t_position.astype(f32), valid, spans)
    t_chunks = ring_list(t_two.astype(bf))
    s_two, kept = layer_forward(s_layer, s_rows + s_position.astype(f32), valid, spans)
    s_chunks = ring_list(s_two.astype(bf))

    t_out = [head_pass(x, teacher_table, False) for x in t_chunks]
    t_tile_weight = [jnp.exp((peaks - stats[:, 0:1]) * 0.5) for _, peaks, stats in t_out]
    s_out = [
        head_pass(x, s_table, True, (t_out[k][0], t_tile_weight[k], local_targets[k]))
        for k, x in enumerate(s_chunks)
    ]

    def shared(stats_list, extra):
        mine = jnp.stack([stats[:, :8].T for stats in stats_list])
        if extra is not None:
            mine = jnp.concatenate([mine[:, :7], jnp.broadcast_to(extra, (mp, 1, rows))], 1)
        mine = natural([mine[k] for k in range(mp)])
        return natural([mine] + [rotate(mine, by) for by in range(1, mp)])

    cos_terms, cos_pull = jax.vjp(lambda x: cosine_loss(x, t_two), s_two)
    own_weight = chunk(tok_weight, 0)
    t_stats = shared([stats for _, _, stats in t_out], None)
    s_stats = shared([stats for _, _, stats in s_out], jnp.sum(own_weight * cos_terms))
    t_peak = jnp.max(t_stats[:, :, 0], 0)
    t_grow = jnp.exp((t_stats[:, :, 0] - t_peak) / temper)
    t_half_sum = jnp.sum(t_grow * t_stats[:, :, 1], 0)
    s_peak = jnp.max(s_stats[:, :, 0], 0)
    s_grow = jnp.exp((s_stats[:, :, 0] - s_peak) / temper)
    s_half_sum = jnp.sum(s_grow * s_stats[:, :, 1], 0)
    s_full_sum = jnp.sum(s_grow * s_grow * s_stats[:, :, 2], 0)
    apart = jnp.sum(t_grow * (t_stats[:, :, 3] - s_stats[:, :, 3]), 0) / temper
    target_logit = jnp.sum(s_stats[:, :, 4], 0)
    log_half_s = s_peak / temper + jnp.log(s_half_sum)
    log_half_t = t_peak / temper + jnp.log(t_half_sum)
    log_full = s_peak + jnp.log(s_full_sum)
    diverge = temper * temper * (apart / t_half_sum - log_half_t + log_half_s)
    missed = log_full - target_logit
    line_terms = jnp.stack(
        [jnp.sum(tok_weight * diverge, -1), jnp.sum(mask_weight * missed, -1), s_stats[:, 0, 7, 0]],
        -1,
    )
    line_terms = line_terms + swap(line_terms, 1)
    seq_terms = jnp.sum(line_terms.reshape(2 * batch, spans, 3), 1)
    loss_terms = lax.dynamic_slice_in_dim(seq_terms, core * batch, batch, 0)

    coef_kl = 5.0 * temper * tok_weight / count_tok
    coef_mlm = 2.0 * mask_weight / count_mask
    s_scale = coef_kl / s_half_sum
    t_scale = coef_kl / t_half_sum
    f_scale = coef_mlm / s_full_sum
    d_logits, d_rows = [None] * mp, [None] * mp
    for step in range(mp):
        k = (step + 1) % mp
        s_tiles = jnp.exp((s_out[k][1] - chunk(s_peak, k)[:, None]) / temper)
        t_tiles = jnp.exp((t_out[k][1] - chunk(t_peak, k)[:, None]) / temper)
        d_logits[k], d_rows[k] = head_back(
            s_out[k][0],
            t_out[k][0],
            s_tiles * chunk(s_scale, k)[:, None],
            t_tiles * chunk(t_scale, k)[:, None],
            s_tiles * s_tiles * chunk(f_scale, k)[:, None],
            chunk(coef_mlm, k)[:, None],
            local_targets[k],
            s_table,
        )
    d_head = ring_sum(d_rows)
    g_head = table_grad([x.T for x in s_chunks], d_logits)
    d_two = d_head + cos_pull(own_weight / count_tok)[0]

    d_embed, layer_grads = layer_backward(s_layer, kept, d_two, valid, spans)
    g_project, g_output_t, g_expand, g_reduce_t, g_vectors = layer_grads
    d_chunks = ring_list(d_embed.astype(bf))
    g_table = add_rows(g_head, [d.T for d in d_chunks], local_inputs)

    def by_place(grads):
        return jnp.concatenate(
            [g.astype(bf).reshape(features, mp, -1) for g in grads], 2
        ).reshape(features, -1)

    own_table = scatter_dp(g_table)
    units = scatter_dp(by_place([g_expand, g_reduce_t])).reshape(share, mp, -1)
    g_position = lax.dynamic_update_slice_in_dim(
        jnp.zeros((features, length), bf), d_embed.T.astype(bf), own_part * rows, 1
    )
    g_small = jnp.pad(g_vectors.T.astype(bf), ((0, 0), (0, LANES - g_vectors.shape[0])))
    heads = by_place(list(g_project) + [g_output_t])
    late = scatter_dp(jnp.concatenate([heads, g_position, g_small], 1))
    heads = late[:, : heads.shape[1]].reshape(share, mp, -1)
    own_small = late[:, mp * heads.shape[2] :].astype(bf)
    own_units = ring_sum([chunk(units.transpose(1, 0, 2), k) for k in range(mp)])
    own_heads = ring_sum([chunk(heads.transpose(1, 0, 2), k) for k in range(mp)])
    own_small = jnp.sum(natural(ring_list(own_small)).astype(f32), 0)

    shared_sq = jnp.sum(own_small * own_small) / mp
    squares = (
        jnp.sum(own_table * own_table)
        + jnp.sum(own_units * own_units)
        + jnp.sum(own_heads * own_heads)
        + shared_sq
    )
    squares = sum_all(jnp.broadcast_to(squares, (8, LANES)))[0, 0]
    norm = jnp.sqrt(squares)
    factor = clip_limit / jnp.maximum(norm, clip_limit)

    head_cut = student_project.shape[2]
    unit_cut = student_expand.shape[1]
    vector_rows = student_vectors.shape[0]
    owned = (
        own_table.T,
        own_small[:, :length].T,
        jnp.stack([own_heads[:, t * head_cut : (t + 1) * head_cut] for t in range(3)]),
        own_heads[:, 3 * head_cut :].T,
        own_units[:, :unit_cut],
        own_units[:, unit_cut:].T,
        own_small[:, length : length + vector_rows].T,
    )
    masters = (
        student_table,
        student_position,
        student_project,
        student_output,
        student_expand,
        student_reduce,
        student_vectors,
    )
    firsts = (
        first_table,
        first_position,
        first_project,
        first_output,
        first_expand,
        first_reduce,
        first_vectors,
    )
    seconds = (
        square_table,
        square_position,
        square_project,
        square_output,
        square_expand,
        square_reduce,
        square_vectors,
    )
    results = []
    for index in range(7):
        rate = rate_vector if index == 6 else rate_table if index == 0 else rate_matrix
        decay = 0.0 if index == 6 else weight_decay
        results += adam_update(
            masters[index], firsts[index], seconds[index], owned[index], factor, rate, decay
        )
    loss_counts = jnp.stack([count_tok, count_mask])
    return (*results, norm, loss_terms, loss_counts)


def solution(mesh):
    in_specs = (
        P("dp", None),
        P("dp", None),
        P("dp"),
        P("dp"),
        P(),
        P("mp", None),
        P(),
        P(None, None, "mp"),
        P("mp", None),
        P(None, "mp"),
        P("mp", None),
        P(),
        P("mp", "dp"),
        P(None, "dp"),
        P(None, "dp", "mp"),
        P("mp", "dp"),
        P("dp", "mp"),
        P("mp", "dp"),
        P(None, "dp"),
        P("mp", "dp"),
        P(None, "dp"),
        P(None, "dp", "mp"),
        P("mp", "dp"),
        P("dp", "mp"),
        P("mp", "dp"),
        P(None, "dp"),
        P("mp", "dp"),
        P(None, "dp"),
        P(None, "dp", "mp"),
        P("mp", "dp"),
        P("dp", "mp"),
        P("mp", "dp"),
        P(None, "dp"),
    )
    out_specs = (
        P("mp", "dp"),
        P("mp", "dp"),
        P("mp", "dp"),
        P(None, "dp"),
        P(None, "dp"),
        P(None, "dp"),
        P(None, "dp", "mp"),
        P(None, "dp", "mp"),
        P(None, "dp", "mp"),
        P("mp", "dp"),
        P("mp", "dp"),
        P("mp", "dp"),
        P("dp", "mp"),
        P("dp", "mp"),
        P("dp", "mp"),
        P("mp", "dp"),
        P("mp", "dp"),
        P("mp", "dp"),
        P(None, "dp"),
        P(None, "dp"),
        P(None, "dp"),
        P(),
        P("dp", None),
        P(),
    )
    return jax.shard_map(body, mesh=mesh, in_specs=in_specs, out_specs=out_specs, check_vma=False)
```

```python
import jax
import jax.numpy as jnp
from jax import lax
from jax.experimental import pallas as pl
from jax.experimental.pallas import tpu as pltpu
from jax.sharding import PartitionSpec as P

HD = 64
STEP = 10
LANES = 128


eps_norm = 1e-05
mask_token = 103
temper = 2.0
beta_first = 0.9
beta_second = 0.999
adam_eps = 1e-08
rate_table = 0.5
rate_matrix = 0.1
rate_vector = 0.3
weight_decay = 0.01
clip_limit = 1.0
bf = jnp.bfloat16
f32 = jnp.float32
vmem_bytes = 56 * 1024 * 1024


def swap(x, bit):
    count = lax.axis_size("dp")
    return lax.ppermute(x, "dp", [(i, i ^ bit) for i in range(count)])


def rotate(x, by=1):
    count = lax.axis_size("mp")
    return lax.ppermute(x, "mp", [(i, (i + by) % count) for i in range(count)])


def chip_bits():
    count = lax.axis_size("dp")
    bits = []
    bit = 2
    while bit < count:
        bits.append(bit)
        bit *= 2
    return bits


def ordered(bit, mine, other, axis):
    low = (lax.axis_index("dp") & bit) == 0
    return jnp.where(
        low, jnp.concatenate([mine, other], axis), jnp.concatenate([other, mine], axis)
    )


def gather_dp(x):
    rows, columns = x.shape
    half = columns // 2
    bits = chip_bits()
    one = x[:, :half]
    for bit in bits:
        one = jnp.concatenate([one, swap(one, bit)], 0)
    two = x[None, :, half:]
    for bit in bits[::-1]:
        two = jnp.stack([two, swap(two, bit)], 1).reshape(-1, rows, columns - half)
    mine = jnp.concatenate([one, two.reshape(-1, columns - half)], 1)
    return mine, swap(mine, 1)


def scatter_dp(y):
    total_rows, columns = y.shape
    count = lax.axis_size("dp")
    rows = total_rows // count
    half = columns // 2
    bits = chip_bits()
    done = []
    for which in range(2):
        part = y[:, :half] if which == 0 else y[:, half:]
        mine, other = part[: total_rows // 2], part[total_rows // 2 :]
        left = mine.astype(f32) + swap(other.astype(bf), 1).astype(f32)
        left = left.reshape(count // 2, rows, -1)
        for bit in bits[::-1] if which == 0 else bits:
            groups = left.shape[0] // 2
            if which == 0:
                keep, give = left[:groups], left[groups:]
            else:
                split = left.reshape(groups, 2, rows, -1)
                keep, give = split[:, 0], split[:, 1]
            left = keep + swap(give.astype(bf), bit).astype(f32)
        done.append(left[0])
    return jnp.concatenate(done, 1)


def order_matrix(features, share):
    count = lax.axis_size("dp")
    at = jnp.arange(features)
    block, inside = at // share, at % share
    other_core, chip = block // (count // 2), block % (count // 2)
    source = (lax.axis_index("dp") ^ (chip * 2 + other_core)) * share + inside
    return (jnp.arange(features)[:, None] == source[None, :]).astype(bf)


def ring_list(x):
    got = [x]
    for _ in range(lax.axis_size("mp") - 1):
        got.append(rotate(got[-1]))
    return got


def natural(entries):
    count = lax.axis_size("mp")
    index = lax.axis_index("mp")
    stacked = jnp.stack(entries)
    return jnp.stack(
        [
            lax.dynamic_index_in_dim(stacked, (index - i) % count, 0, keepdims=False)
            for i in range(count)
        ]
    )


def ring_sum(terms):
    count = lax.axis_size("mp")
    total = terms[1 % count]
    for k in range(2, count + 1):
        total = terms[k % count].astype(f32) + rotate(total.astype(bf)).astype(f32)
    return total


def sum_all(x):
    bit = 1
    while bit < lax.axis_size("dp"):
        x = x + swap(x, bit)
        bit *= 2
    count = lax.axis_size("mp")
    return jnp.sum(natural([x] + [rotate(x, by) for by in range(1, count)]), 0)


def tile_of(total, cap):
    best = LANES
    for size in range(LANES, min(total, cap) + 1, LANES):
        if total % size == 0:
            best = size
    return best


def call(body, grid, in_specs, out_specs, out_shape, scratch, flops, moved):
    return pl.pallas_call(
        body,
        grid=grid,
        in_specs=in_specs,
        out_specs=out_specs,
        out_shape=out_shape,
        scratch_shapes=scratch,
        compiler_params=pltpu.CompilerParams(
            dimension_semantics=("arbitrary",) * len(grid), vmem_limit_bytes=vmem_bytes
        ),
        cost_estimate=pl.CostEstimate(flops=flops, bytes_accessed=moved, transcendentals=0),
    )


def whole(shape):
    return pl.BlockSpec(shape, lambda *_: (0,) * len(shape))


def onto(x, tables):
    total, at = None, 0
    for table in tables:
        wide = table.shape[0]
        term = jnp.dot(x[:, at : at + wide], table, preferred_element_type=f32)
        total = term if total is None else total + term
        at += wide
    return total


def rows_times(x, flipped):
    return lax.dot_general(x, flipped, (((1,), (1,)), ((), ())), preferred_element_type=f32)


def pick_rows(ids, first, count, rows, tables):
    half, vocab = tables[0].shape
    width = half * len(tables)
    tile = tile_of(vocab, 1536)
    total_rows = count * rows

    def body(*refs):
        ids_refs, table_refs = refs[:count], refs[count : count + len(tables)]
        out_ref, total = refs[-2], refs[-1]
        j = pl.program_id(0)

        @pl.when(j == 0)
        def _():
            total[...] = jnp.zeros_like(total)

        for c, ids_ref in enumerate(ids_refs):
            lane = lax.broadcasted_iota(jnp.int32, (rows, tile), 1)
            hot = jnp.where(lane == ids_ref[...] - j * tile, 1.0, 0.0).astype(bf)
            for t, table_ref in enumerate(table_refs):
                total[c * rows : (c + 1) * rows, t * half : (t + 1) * half] += rows_times(
                    hot, table_ref[...]
                )

        @pl.when(j == pl.num_programs(0) - 1)
        def _():
            out_ref[...] = total[...].astype(bf)

    return call(
        body,
        (vocab // tile,),
        [pl.BlockSpec((rows, 1), lambda j, k=k: (k, 0)) for k in range(first, first + count)]
        + [pl.BlockSpec((half, tile), lambda j: (0, j))] * len(tables),
        whole((total_rows, width)),
        jax.ShapeDtypeStruct((total_rows, width), bf),
        [pltpu.VMEM((total_rows, width), f32)],
        2 * total_rows * width * vocab,
        2 * width * vocab,
    )(*[ids] * count, *tables)


def lane_value(values, j):
    lane = lax.broadcasted_iota(jnp.int32, values.shape, 1)
    return jnp.sum(jnp.where(lane == j, values, 0.0), 1, keepdims=True)


def head_tile(vocab):
    return tile_of(vocab, 1536)


def head_pass(x, tables, flipped, beside=None):
    vocab = tables[0].shape[1] if flipped else tables[0].shape[0]
    rows, width = x.shape
    tile = head_tile(vocab)
    student = beside is not None
    step = min(rows, 256)
    count = len(tables)
    fold = range(0, tile, LANES)

    def body(x_ref, *refs):
        table_refs, refs = refs[:count], refs[count:]
        if flipped:
            whole_table, refs = refs[-1], refs[:-1]
            for t, table_ref in enumerate(table_refs):
                high = table_ref.shape[0]
                whole_table[t * high : (t + 1) * high, :] = table_ref[...]
        if student:
            other_ref, weight_ref, target_ref, half_ref, peaks_ref, stats_ref = refs
        else:
            half_ref, peaks_ref, stats_ref = refs
        j = pl.program_id(0)

        @pl.when(j == 0)
        def _():
            lane = lax.broadcasted_iota(jnp.int32, stats_ref.shape, 1)
            stats_ref[...] = jnp.where(lane == 0, -1e30, 0.0)
            peaks_ref[...] = jnp.zeros_like(peaks_ref)

        for begin in range(0, rows, step):
            part = pl.ds(begin, step)
            if flipped:
                z = jnp.dot(x_ref[part, :], whole_table[...], preferred_element_type=f32)
            else:
                z = rows_times(x_ref[part, :], table_refs[0][...])
            before = stats_ref[part, :]
            highest = z[:, :LANES]
            for at in fold[1:]:
                highest = jnp.maximum(highest, z[:, at : at + LANES])
            peak = jnp.maximum(before[:, 0:1], jnp.max(highest, 1, keepdims=True))
            shrink = jnp.exp((before[:, 0:1] - peak) * 0.5)
            lane = lax.broadcasted_iota(jnp.int32, (step, LANES), 1)
            sums = [jnp.zeros((step, LANES), f32) for _ in range(4)]
            if student:
                target = target_ref[part, :] - j * tile
            for at in fold:
                piece = z[:, at : at + LANES]
                half = jnp.exp((piece - peak) * 0.5)
                half_ref[part, at : at + LANES] = half.astype(bf)
                sums[0] += half
                if student:
                    sums[1] += half * half
                    sums[2] += other_ref[part, at : at + LANES].astype(f32) * piece
                    sums[3] += jnp.where(lane == target - at, piece, 0.0)
                else:
                    sums[2] += half * piece
            sums = [jnp.sum(s, 1, keepdims=True) for s in sums]
            half_sum = before[:, 1:2] * shrink + sums[0]
            if student:
                full_sum = before[:, 2:3] * (shrink * shrink) + sums[1]
                cross = before[:, 3:4] + lane_value(weight_ref[part, :], j) * sums[2]
                values = (peak, half_sum, full_sum, cross, before[:, 4:5] + sums[3])
            else:
                values = (peak, half_sum, before[:, 2:3], before[:, 3:4] * shrink + sums[2])
            after = before
            for slot, value in enumerate(values):
                after = jnp.where(lane == slot, value, after)
            stats_ref[part, :] = after
            peaks_ref[part, :] = jnp.where(lane == j, peak, peaks_ref[part, :])

    block = pl.BlockSpec((rows, tile), lambda j: (0, j))
    lanes = whole((rows, LANES))
    in_specs = [whole((rows, width))]
    for table in tables:
        if flipped:
            in_specs.append(pl.BlockSpec((table.shape[0], tile), lambda j: (0, j)))
        else:
            in_specs.append(pl.BlockSpec((tile, width), lambda j: (j, 0)))
    operands = [x, *tables]
    if student:
        in_specs += [block, lanes, whole((rows, 1))]
        operands += list(beside)
    stat = jax.ShapeDtypeStruct((rows, LANES), f32)
    return call(
        body,
        (vocab // tile,),
        in_specs,
        [block, lanes, lanes],
        [jax.ShapeDtypeStruct((rows, vocab), bf), stat, stat],
        [pltpu.VMEM((width, tile), bf)] if flipped else [],
        4 * rows * width * vocab,
        2 * width * vocab + 2 * rows * vocab * (2 if student else 1),
    )(*operands)


def head_back(k, rows, s_half, t_half, s_scale, t_scale, f_scale, hit_scale, targets, tables):
    part_width, vocab = tables[0].shape
    width = part_width * len(tables)
    tile = head_tile(vocab)
    step = min(rows, 256)

    def body(s_ref, t_ref, a_ref, b_ref, c_ref, h_ref, target_ref, *refs):
        table_refs, (d_ref, out_ref, total) = refs[: len(tables)], refs[len(tables) :]
        j = pl.program_id(0)

        @pl.when(j == 0)
        def _():
            total[...] = jnp.zeros_like(total)

        for begin in range(0, rows, step):
            part = pl.ds(begin, step)
            a = jnp.broadcast_to(lane_value(a_ref[part, :], j), (step, LANES))
            b = jnp.broadcast_to(lane_value(b_ref[part, :], j), (step, LANES))
            c = jnp.broadcast_to(lane_value(c_ref[part, :], j), (step, LANES))
            h = jnp.broadcast_to(h_ref[part, :], (step, LANES))
            target = jnp.broadcast_to(target_ref[part, :] - j * tile, (step, LANES))
            lane = lax.broadcasted_iota(jnp.int32, (step, LANES), 1)
            for at in range(0, tile, LANES):
                half = s_ref[part, at : at + LANES].astype(f32)
                grad = half * (a + half * c) - t_ref[part, at : at + LANES].astype(f32) * b
                grad -= jnp.where(lane == target - at, h, 0.0)
                d_ref[part, at : at + LANES] = grad.astype(bf)
            for t, table_ref in enumerate(table_refs):
                total[part, t * part_width : (t + 1) * part_width] += rows_times(
                    d_ref[part, :], table_ref[...]
                )

        @pl.when(j == pl.num_programs(0) - 1)
        def _():
            out_ref[...] = total[...].astype(bf)

    block = pl.BlockSpec((rows, tile), lambda j: (k, j))
    lanes = pl.BlockSpec((rows, LANES), lambda j: (k, 0))
    column = pl.BlockSpec((rows, 1), lambda j: (k, 0))
    return call(
        body,
        (vocab // tile,),
        [block, block, lanes, lanes, lanes, column, column]
        + [pl.BlockSpec((part_width, tile), lambda j: (0, j))] * len(tables),
        [pl.BlockSpec((rows, tile), lambda j: (0, j)), whole((rows, width))],
        [jax.ShapeDtypeStruct((rows, vocab), bf), jax.ShapeDtypeStruct((rows, width), bf)],
        [pltpu.VMEM((rows, width), f32)],
        2 * rows * width * vocab,
        2 * width * vocab + 6 * rows * vocab,
    )(s_half, t_half, s_scale, t_scale, f_scale, hit_scale, targets, *tables)


def table_grad(x_flipped, d_logits):
    width = x_flipped.shape[0]
    rows, vocab = d_logits[0].shape
    tile = tile_of(vocab, 1536)
    count = len(d_logits)

    def body(x_ref, *refs):
        total = None
        for k, d_ref in enumerate(refs[:-1]):
            term = jnp.dot(
                x_ref[:, k * rows : (k + 1) * rows], d_ref[...], preferred_element_type=f32
            )
            total = term if total is None else total + term
        refs[-1][...] = total

    return call(
        body,
        (vocab // tile,),
        [whole((width, rows * count))] + [pl.BlockSpec((rows, tile), lambda j: (0, j))] * count,
        pl.BlockSpec((width, tile), lambda j: (0, j)),
        jax.ShapeDtypeStruct((width, vocab), f32),
        [],
        2 * rows * count * width * vocab,
        2 * rows * count * vocab + 4 * width * vocab,
    )(x_flipped, *d_logits)


def add_rows(base, e_flipped, ids):
    width, vocab = base.shape
    rows = ids.shape[0]
    tile = tile_of(vocab, 768)

    def body(base_ref, e_ref, ids_ref, out_ref):
        j = pl.program_id(0)
        lane = lax.broadcasted_iota(jnp.int32, (rows, tile), 1)
        hot = jnp.where(lane == ids_ref[...] - j * tile, 1.0, 0.0).astype(bf)
        total = base_ref[...] + jnp.dot(e_ref[...], hot, preferred_element_type=f32)
        out_ref[...] = total.astype(bf)

    block = pl.BlockSpec((width, tile), lambda j: (0, j))
    return call(
        body,
        (vocab // tile,),
        [block, whole((width, rows)), whole((rows, 1))],
        block,
        jax.ShapeDtypeStruct((width, vocab), bf),
        [],
        2 * rows * width * vocab,
        6 * width * vocab,
    )(base, e_flipped, ids)


def heads_reordered(x):
    count = lax.axis_size("mp")
    return jnp.concatenate(list(natural(jnp.split(x, count, -1))), -1)


def gather_sequence(x, spans):
    whole_x = ordered(1, x, swap(x, 1), 1)
    if spans > 1:
        count = lax.axis_size("mp")
        whole_x = heads_reordered(whole_x)
        groups = [list(range(i, i + spans)) for i in range(0, count, spans)]
        whole_x = lax.all_gather(
            whole_x, "mp", axis=1, axis_index_groups=groups, tiled=True
        )
        whole_x = heads_reordered(whole_x)
    return whole_x


def scatter_sequence(x, spans):
    if spans > 1:
        count = lax.axis_size("mp")
        groups = [list(range(i, i + spans)) for i in range(0, count, spans)]
        x = lax.psum_scatter(
            heads_reordered(x), "mp", scatter_dimension=1, axis_index_groups=groups, tiled=True
        )
        x = heads_reordered(x)
    rows = x.shape[1] // 2
    core = lax.axis_index("dp") & 1
    keep = lax.dynamic_slice_in_dim(x, core * rows, rows, 1)
    give = lax.dynamic_slice_in_dim(x, (1 - core) * rows, rows, 1)
    return keep + swap(give, 1)


def norm_parts(x):
    centre = x - jnp.mean(x, -1, keepdims=True)
    spread = jnp.mean(centre * centre, -1, keepdims=True)
    scale = lax.rsqrt(spread + eps_norm)
    return centre * scale, scale


def norm_back(unit, scale, gain, grad):
    inner = grad * gain
    slope = inner - jnp.mean(inner, -1, keepdims=True)
    slope = (slope - unit * jnp.mean(inner * unit, -1, keepdims=True)) * scale
    return slope, jnp.sum(grad * unit, 0, keepdims=True), jnp.sum(grad, 0, keepdims=True)


def resident(shape):
    return pl.BlockSpec(shape, lambda *_: (0,) * len(shape), pipeline_mode=pl.Buffered(1))


def put_rows(ref, j, values):
    row = lax.broadcasted_iota(jnp.int32, ref.shape, 0)
    add = jnp.zeros(ref.shape, f32)
    for at, value in values.items():
        add = jnp.where(row == at, value, add)

    @pl.when(j == 0)
    def _():
        ref[...] = add

    @pl.when(j > 0)
    def _():
        ref[...] += add


def columns_of(features, units):
    cuts, at = [], 0
    for wide in [features] * 4 + [units] * 2:
        cuts.append(slice(at, at + wide))
        at += wide
    return cuts


def side_by_side(x, classes, cut):
    return jnp.concatenate([rows_times(x, c[:, cut]) for c in classes], 1)


def through(x, classes, cut):
    high = classes[0].shape[0]
    total = None
    for t, c in enumerate(classes):
        term = jnp.dot(x[:, t * high : (t + 1) * high], c[:, cut], preferred_element_type=f32)
        total = term if total is None else total + term
    return total


def layer_open(embedded, vectors, classes, units):
    rows, features = embedded.shape
    cuts = columns_of(features, units)
    step = min(rows, 256)
    count = len(classes)

    def body(x_ref, vectors_ref, *refs):
        class_refs, (zero_ref, q_ref, kv_ref) = refs[:count], refs[count:]
        unit, _ = norm_parts(x_ref[...])
        zero = unit * vectors_ref[0:1, :] + vectors_ref[1:2, :]
        zero_ref[...] = zero
        low = zero.astype(bf)
        q_ref[...] = through(low, class_refs, cuts[0]).astype(bf)
        kv_ref[0] = through(low, class_refs, cuts[1]).astype(bf)
        kv_ref[1] = through(low, class_refs, cuts[2]).astype(bf)

    block = pl.BlockSpec((step, features), lambda j: (j, 0))
    return call(
        body,
        (rows // step,),
        [block, whole(vectors.shape)] + [resident((c.shape[0], 3 * features)) for c in classes],
        [block, block, pl.BlockSpec((2, step, features), lambda j: (0, j, 0))],
        [
            jax.ShapeDtypeStruct((rows, features), f32),
            jax.ShapeDtypeStruct((rows, features), bf),
            jax.ShapeDtypeStruct((2, rows, features), bf),
        ],
        [],
        6 * rows * features * features,
        6 * features * features + 16 * rows * features,
    )(embedded, vectors, *classes)


def head_lanes(shape, which):
    return (lax.broadcasted_iota(jnp.int32, shape, 1) // HD) == which


def layer_close(zero, query, both, valid, vectors, classes, units):
    rows, features = zero.shape
    length = both.shape[1]
    cuts = columns_of(features, units)
    step = min(rows, 256)
    count = len(classes)
    pair = LANES // HD

    def body(zero_ref, q_ref, both_ref, valid_ref, vectors_ref, *refs):
        class_refs, refs = refs[:count], refs[count:]
        two_ref, attn_ref, log_ref, one_pre_ref, two_pre_ref = refs
        allowed = valid_ref[...] > 0.0
        log_lane = lax.broadcasted_iota(jnp.int32, (step, LANES), 1)
        logs = jnp.zeros((step, LANES), f32)
        pieces = []
        for block in range(features // LANES):
            lanes = slice(block * LANES, (block + 1) * LANES)
            keys, values = both_ref[0, :, lanes], both_ref[1, :, lanes]
            merged = jnp.zeros((step, LANES), f32)
            for which in range(pair):
                mine = head_lanes((step, LANES), which)
                q = jnp.where(mine, q_ref[:, lanes] * HD ** (-0.5), 0.0).astype(bf)
                score = jnp.where(allowed, rows_times(q, keys), -1e30)
                peak = jnp.max(score, 1, keepdims=True)
                expo = jnp.exp(score - peak)
                total = jnp.sum(expo, 1, keepdims=True)
                weight = (expo * (1.0 / total)).astype(bf)
                merged = jnp.where(
                    mine, jnp.dot(weight, values, preferred_element_type=f32), merged
                )
                logs = jnp.where(log_lane == block * pair + which, peak + jnp.log(total), logs)
            pieces.append(merged)
        log_ref[...] = logs
        attn = jnp.concatenate(pieces, 1).astype(bf)
        attn_ref[...] = attn
        one_pre = side_by_side(attn, class_refs, cuts[3]) + vectors_ref[2:3, :] + zero_ref[...]
        one_pre_ref[...] = one_pre
        one = norm_parts(one_pre)[0] * vectors_ref[3:4, :] + vectors_ref[4:5, :]
        hidden = through(one.astype(bf), class_refs, cuts[4])
        active = gelu(hidden).astype(bf)
        two_pre = side_by_side(active, class_refs, cuts[5]) + vectors_ref[5:6, :] + one
        two_pre_ref[...] = two_pre
        two_ref[...] = norm_parts(two_pre)[0] * vectors_ref[6:7, :] + vectors_ref[7:8, :]

    block = pl.BlockSpec((step, features), lambda j: (j, 0))
    wide = jax.ShapeDtypeStruct((rows, features), f32)
    columns = cuts[-1].stop
    return call(
        body,
        (rows // step,),
        [block, block, resident(both.shape), whole(valid.shape), whole(vectors.shape)]
        + [resident((c.shape[0], columns)) for c in classes],
        [block, block, pl.BlockSpec((step, LANES), lambda j: (j, 0)), block, block],
        [
            wide,
            jax.ShapeDtypeStruct((rows, features), bf),
            jax.ShapeDtypeStruct((rows, LANES), f32),
            wide,
            wide,
        ],
        [],
        2 * rows * features * (2 * length + features + 2 * units),
        2 * features * columns + 20 * rows * features,
    )(zero, query, both, valid, vectors, *classes)


def gelu(x):
    return 0.5 * x * (1.0 + lax.erf(x * 0.7071067811865476))


def gelu_slope(x):
    return 0.5 * (1.0 + lax.erf(x * 0.7071067811865476)) + x * 0.3989422804014327 * jnp.exp(
        -0.5 * x * x
    )


def units_back(d_two, two_pre, one_pre, vectors, classes, units):
    rows, features = d_two.shape
    cuts = columns_of(features, units)
    step = min(rows, 256)
    count = len(classes)

    def body(d_ref, two_pre_ref, one_pre_ref, vectors_ref, *refs):
        class_refs, refs = refs[:count], refs[count:]
        reduce_ref, active_ref, low_ref, hidden_ref, branch_ref, pre_ref, attn_ref, sums_ref = refs
        unit, scale = norm_parts(two_pre_ref[...])
        d_two_pre, gain_two, shift_two = norm_back(unit, scale, vectors_ref[6:7, :], d_ref[...])
        low = d_two_pre.astype(bf)
        reduce_ref[...] = low
        d_active = through(low, class_refs, cuts[5])
        unit, scale = norm_parts(one_pre_ref[...])
        one_low = (unit * vectors_ref[3:4, :] + vectors_ref[4:5, :]).astype(bf)
        low_ref[...] = one_low
        hidden = through(one_low, class_refs, cuts[4])
        bell = 0.5 * (1.0 + lax.erf(hidden * 0.7071067811865476))
        active_ref[...] = (hidden * bell).astype(bf)
        slope = bell + hidden * 0.3989422804014327 * jnp.exp(-0.5 * hidden * hidden)
        d_hidden = (d_active * slope).astype(bf)
        hidden_ref[...] = d_hidden
        d_one = side_by_side(d_hidden, class_refs, cuts[4]) + d_two_pre
        d_one_pre, gain_one, shift_one = norm_back(unit, scale, vectors_ref[3:4, :], d_one)
        pre_ref[...] = d_one_pre
        d_branch = d_one_pre.astype(bf)
        branch_ref[...] = d_branch
        attn_ref[...] = through(d_branch, class_refs, cuts[3]).astype(bf)
        put_rows(
            sums_ref,
            pl.program_id(0),
            {
                2: jnp.sum(d_one_pre, 0, keepdims=True),
                3: gain_one,
                4: shift_one,
                5: jnp.sum(d_two_pre, 0, keepdims=True),
                6: gain_two,
                7: shift_two,
            },
        )

    block = pl.BlockSpec((step, features), lambda j: (j, 0))
    broad = pl.BlockSpec((step, units), lambda j: (j, 0))
    columns = cuts[-1].stop
    low = jax.ShapeDtypeStruct((rows, features), bf)
    full = jax.ShapeDtypeStruct((rows, features), f32)
    high = jax.ShapeDtypeStruct((rows, units), bf)
    return call(
        body,
        (rows // step,),
        [block, block, block, whole(vectors.shape)]
        + [resident((c.shape[0], columns)) for c in classes],
        [block, broad, block, broad, block, block, block, whole((8, features))],
        [low, high, low, high, low, full, low, jax.ShapeDtypeStruct((8, features), f32)],
        [],
        2 * rows * features * (features + 3 * units),
        2 * features * columns + 20 * rows * features + 4 * rows * units,
    )(d_two, two_pre, one_pre, vectors, *classes)


def columns_times(left, right):
    return lax.dot_general(left, right, (((0,), (0,)), ((), ())), preferred_element_type=f32)


def attention_back(query, both, d_attn, logs, valid):
    rows, features = query.shape
    length = both.shape[1]
    pair = LANES // HD

    def body(q_ref, both_ref, d_ref, log_ref, valid_ref, dq_ref, dboth_ref):
        j = pl.program_id(0)
        allowed = valid_ref[...] > 0.0
        keys, values = both_ref[0], both_ref[1]
        merged = jnp.zeros((rows, LANES), f32)
        for which in range(pair):
            mine = head_lanes((rows, LANES), which)
            q = jnp.where(mine, q_ref[...] * HD ** (-0.5), 0.0).astype(bf)
            d = jnp.where(mine, d_ref[...], 0.0).astype(bf)
            log_total = lane_value(log_ref[...], j * pair + which)
            score = jnp.where(allowed, rows_times(q, keys), -1e30)
            weight = jnp.exp(score - log_total)
            slope = rows_times(d, values)
            low = weight.astype(bf)
            inner = jnp.sum(weight * slope, 1, keepdims=True)
            d_score = (weight * (slope - inner)).astype(bf)
            merged = jnp.where(
                mine, jnp.dot(d_score, keys, preferred_element_type=f32), merged
            )
            d_keys = columns_times(d_score, q)
            d_values = columns_times(low, d)
            if which == 0:
                dboth_ref[0] = d_keys
                dboth_ref[1] = d_values
            else:
                dboth_ref[0] += d_keys
                dboth_ref[1] += d_values
        dq_ref[...] = (merged * HD ** (-0.5)).astype(bf)

    block = pl.BlockSpec((rows, LANES), lambda j: (0, j))
    tall = pl.BlockSpec((2, length, LANES), lambda j: (0, 0, j))
    return call(
        body,
        (features // LANES,),
        [block, tall, block, whole(logs.shape), whole(valid.shape)],
        [block, tall],
        [
            jax.ShapeDtypeStruct((rows, features), bf),
            jax.ShapeDtypeStruct((2, length, features), f32),
        ],
        [],
        10 * rows * features * length,
        16 * length * features,
    )(query, both, d_attn, logs, valid)


def embed_back(d_parts, d_one_pre, embedded, vectors, classes, units):
    rows, features = d_one_pre.shape
    cuts = columns_of(features, units)
    step = min(rows, 256)
    count = len(classes)

    def body(q_ref, k_ref, v_ref, pre_ref, x_ref, vectors_ref, *refs):
        class_refs, (out_ref, sums_ref) = refs[:count], refs[count:]
        d_zero = pre_ref[...]
        for t, part in enumerate((q_ref, k_ref, v_ref)):
            d_zero += side_by_side(part[...], class_refs, cuts[t])
        unit, scale = norm_parts(x_ref[...])
        d_embed, gain, shift = norm_back(unit, scale, vectors_ref[0:1, :], d_zero)
        out_ref[...] = d_embed.astype(bf)
        put_rows(sums_ref, pl.program_id(0), {0: gain, 1: shift})

    block = pl.BlockSpec((step, features), lambda j: (j, 0))
    return call(
        body,
        (rows // step,),
        [block] * 5
        + [whole(vectors.shape)]
        + [resident((c.shape[0], 3 * features)) for c in classes],
        [block, whole((8, features))],
        [
            jax.ShapeDtypeStruct((rows, features), bf),
            jax.ShapeDtypeStruct((8, features), f32),
        ],
        [],
        6 * rows * features * features,
        6 * features * features + 16 * rows * features,
    )(*d_parts, d_one_pre, embedded, vectors, *classes)


def layer_forward(classes, vectors, units, embedded, valid, spans):
    zero, query, own = layer_open(embedded, vectors, classes, units)
    both = gather_sequence(own, spans)
    two, attn, logs, one_pre, two_pre = layer_close(
        zero, query, both, valid, vectors, classes, units
    )
    return two, (embedded, zero, query, both, attn, logs, one_pre, two_pre)


def layer_backward(classes, vectors, units, kept, d_two, valid, spans):
    embedded, zero, query, both, attn, logs, one_pre, two_pre = kept
    d_reduce, active, one_low, d_hidden, d_branch, d_one_pre, d_attn, sums = units_back(
        d_two, two_pre, one_pre, vectors, classes, units
    )
    g_reduce_t = columns_times(d_reduce, active).astype(bf)
    g_expand = columns_times(one_low, d_hidden).astype(bf)
    g_output_t = columns_times(d_branch, attn).astype(bf)
    d_query, d_partial = attention_back(query, both, d_attn, logs, valid)
    d_both = scatter_sequence(d_partial, spans).astype(bf)
    d_parts = (d_query, d_both[0], d_both[1])
    low = zero.astype(bf)
    g_project = [columns_times(low, d).astype(bf) for d in d_parts]
    d_embed, first_sums = embed_back(d_parts, d_one_pre, embedded, vectors, classes, units)
    return d_embed, g_project + [g_output_t], [g_expand, g_reduce_t], sums + first_sums


def cosine_loss(x_student, x_teacher):
    s_len = jnp.sqrt(jnp.sum(x_student * x_student, -1))
    t_len = jnp.sqrt(jnp.sum(x_teacher * x_teacher, -1))
    return 1.0 - jnp.sum(x_student * x_teacher, -1) / (s_len * t_len)


def adam_update(master, first, square, grad, factor, rate, decay):
    clipped = grad * factor
    new_first = beta_first * first + (1.0 - beta_first) * clipped
    new_square = beta_second * square + (1.0 - beta_second) * clipped * clipped
    first_hat = new_first / (1.0 - beta_first**STEP)
    square_hat = new_square / (1.0 - beta_second**STEP)
    updated = master - rate * (first_hat / (jnp.sqrt(square_hat) + adam_eps) + decay * master)
    return [updated, new_first, new_square]


def body(
    token_ids,
    mlm_flags,
    pad_lengths,
    group_ids,
    group_weight,
    teacher_table,
    teacher_position,
    teacher_project,
    teacher_output,
    teacher_expand,
    teacher_reduce,
    teacher_vectors,
    student_table,
    student_position,
    student_project,
    student_output,
    student_expand,
    student_reduce,
    student_vectors,
    first_table,
    first_position,
    first_project,
    first_output,
    first_expand,
    first_reduce,
    first_vectors,
    square_table,
    square_position,
    square_project,
    square_output,
    square_expand,
    square_reduce,
    square_vectors,
):
    mp, dp = lax.axis_size("mp"), lax.axis_size("dp")
    place, index = lax.axis_index("mp"), lax.axis_index("dp")
    core = index & 1
    batch, length = token_ids.shape
    spans = mp // (2 * batch)
    rows = length // (2 * spans)
    vocab_rows = student_table.shape[0]
    share = student_table.shape[1]
    features = share * dp
    start = place * vocab_rows

    packed = jnp.concatenate(
        [
            token_ids * 2 + mlm_flags,
            jnp.pad((pad_lengths * 256 + group_ids)[None], ((0, 0), (0, length - batch))),
        ]
    )
    packed = ordered(1, packed[None], swap(packed, 1)[None], 0)
    column_ids = packed[:, :batch].reshape(2 * batch, spans, 2, rows)
    lengths = (packed[:, batch, :batch] // 256).reshape(-1)
    groups = (packed[:, batch, :batch] % 256).reshape(-1)
    chosen = groups[:, None] == jnp.arange(group_weight.shape[0])[None, :]
    seq_weight = jnp.sum(jnp.where(chosen, group_weight[None, :], 0.0), -1)
    line_place = (place - jnp.arange(mp)) % mp
    line = lax.dynamic_index_in_dim(column_ids, core, 2, keepdims=False).reshape(mp, rows)
    line = jnp.take(line, line_place, axis=0)
    line_targets, line_flags = line // 2, line % 2
    line_inputs = jnp.where(line_flags == 1, mask_token, line_targets)
    line_sequence = line_place // spans
    line_part = (line_place % spans) * 2 + core
    line_positions = line_part[:, None] * rows + jnp.arange(rows)[None, :]
    line_lengths = jnp.take(lengths, line_sequence)
    line_real = (line_positions < line_lengths[:, None]).astype(f32)
    line_masked = line_flags.astype(f32) * line_real
    line_weight = jnp.take(seq_weight, line_sequence)[:, None]
    tok_weight, mask_weight = line_weight * line_real, line_weight * line_masked
    own_part = line_part[0]
    valid = (jnp.arange(length) < line_lengths[0]).astype(f32)[None]
    local_inputs = (line_inputs - start).reshape(-1, 1)
    local_targets = (line_targets - start).reshape(-1, 1)

    nonpad = (jnp.arange(length)[None, :] < pad_lengths[:, None]).astype(f32)
    masked = mlm_flags.astype(f32) * nonpad
    counts = jnp.stack([jnp.sum(nonpad), jnp.sum(masked)])
    counts = jnp.pad(counts[None], ((0, 7), (0, LANES - 2)))
    bit = 1
    while bit < dp:
        counts = counts + swap(counts, bit)
        bit *= 2
    count_tok, count_mask = counts[0, 0], jnp.maximum(counts[0, 1], 1.0)

    def joined(project, output, expand, reduce_value):
        return jnp.concatenate(
            [project[0], project[1], project[2], output.T, expand, reduce_value.T], 1
        )

    head_cut = student_project.shape[2]
    unit_cut = student_expand.shape[1]
    share_columns = 4 * head_cut + 2 * unit_cut

    def by_kind(shares):
        columns, at = [], 0
        for cut in [head_cut] * 4 + [unit_cut] * 2:
            columns += [x[:, at : at + cut] for x in shares]
            at += cut
        return columns

    def cut_rows(x, axis):
        return lax.dynamic_slice_in_dim(x, index * share, share, axis)

    s_table = gather_dp(student_table.T.astype(bf))
    t_share = joined(
        cut_rows(teacher_project, 1),
        cut_rows(teacher_output, 1),
        cut_rows(teacher_expand, 0),
        cut_rows(teacher_reduce, 1),
    )
    s_share = joined(
        student_project.astype(bf),
        student_output.astype(bf),
        student_expand.astype(bf),
        student_reduce.astype(bf),
    )
    order = order_matrix(features, share)

    def reordered(x, back=False):
        return rows_times(x, order) if back else jnp.dot(x, order, preferred_element_type=f32)

    t_classes = gather_dp(jnp.concatenate(by_kind(ring_list(t_share)), 1))
    t_vectors = reordered(teacher_vectors)
    vector_rows = student_vectors.shape[0]
    small_at = mp * share_columns
    padded = -(small_at + length + vector_rows) % (2 * LANES)
    s_classes = gather_dp(
        jnp.concatenate(
            by_kind(ring_list(s_share))
            + [
                student_position.T.astype(bf),
                student_vectors.T.astype(bf),
                jnp.zeros((share, padded), bf),
            ],
            1,
        )
    )
    s_small = jnp.concatenate([c[:, small_at:] for c in s_classes], 0)
    s_vectors = s_small[:, length : length + vector_rows].T.astype(f32)
    units = mp * unit_cut
    s_position = lax.dynamic_slice_in_dim(s_small, own_part * rows, rows, 1).T
    t_position = lax.dynamic_slice_in_dim(teacher_position, own_part * rows, rows, 0)

    inside = (local_inputs >= 0) & (local_inputs < vocab_rows)
    clipped = jnp.clip(local_inputs[:, 0], 0, vocab_rows - 1)
    t_found = jnp.where(inside, jnp.take(teacher_table, clipped, axis=0), 0)
    t_rows = ring_sum([t_found[k * rows : (k + 1) * rows] for k in range(mp)])
    s_first = pick_rows(local_inputs, 1, 1, rows, s_table)
    s_later = pick_rows(local_inputs, 2, mp - 2, rows, s_table) if mp > 2 else None
    s_own = pick_rows(local_inputs, 0, 1, rows, s_table)
    s_rows = ring_sum(
        [s_own, s_first] + [s_later[k * rows : (k + 1) * rows] for k in range(mp - 2)]
    )
    t_embedded = reordered(t_rows.astype(bf)) + reordered(t_position)
    t_two, _ = layer_forward(t_classes, t_vectors, units, t_embedded, valid, spans)
    t_all = jnp.concatenate(ring_list(reordered(t_two.astype(bf), True).astype(bf)), 0)
    s_embedded = s_rows + s_position.astype(f32)
    s_two, kept = layer_forward(s_classes, s_vectors, units, s_embedded, valid, spans)
    s_all = jnp.concatenate(ring_list(s_two.astype(bf)), 0)

    t_half, t_peaks, t_tail = head_pass(t_all, [teacher_table], False)
    t_tile_weight = jnp.exp((t_peaks - t_tail[:, 0:1]) * 0.5)
    s_half, s_peaks, s_tail = head_pass(
        s_all, s_table, True, (t_half, t_tile_weight, local_targets)
    )

    def shared(tail):
        mine = tail[:, :8].T.reshape(8, mp, rows)
        return jnp.stack(
            [mine] + [jnp.roll(rotate(mine, by), by, 1) for by in range(1, mp)]
        )

    cos_terms, cos_pull = jax.vjp(lambda x: cosine_loss(x, t_two), s_two)
    own_weight = tok_weight[0]
    t_stats, s_stats = shared(t_tail), shared(s_tail)
    t_peak = jnp.max(t_stats[:, 0], 0)
    t_grow = jnp.exp((t_stats[:, 0] - t_peak) / temper)
    t_half_sum = jnp.sum(t_grow * t_stats[:, 1], 0)
    s_peak = jnp.max(s_stats[:, 0], 0)
    s_grow = jnp.exp((s_stats[:, 0] - s_peak) / temper)
    s_half_sum = jnp.sum(s_grow * s_stats[:, 1], 0)
    s_full_sum = jnp.sum(s_grow * s_grow * s_stats[:, 2], 0)

    apart = jnp.sum(t_grow[:, 0] * (t_stats[:, 3, 0] - s_stats[:, 3, 0]), 0) / temper
    log_half_s = s_peak[0] / temper + jnp.log(s_half_sum[0])
    log_half_t = t_peak[0] / temper + jnp.log(t_half_sum[0])
    log_full = s_peak[0] + jnp.log(s_full_sum[0])
    diverge = temper * temper * (apart / t_half_sum[0] - log_half_t + log_half_s)
    missed = log_full - jnp.sum(s_stats[:, 4, 0], 0)
    own_terms = jnp.stack(
        [
            jnp.sum(own_weight * diverge),
            jnp.sum(mask_weight[0] * missed),
            jnp.sum(own_weight * cos_terms),
        ]
    )
    own_terms = jnp.pad(own_terms[None], ((0, 7), (0, LANES - 3)))
    own_terms = own_terms + swap(own_terms, 1)
    line_terms = natural([own_terms] + [rotate(own_terms, by) for by in range(1, mp)])
    seq_terms = jnp.sum(line_terms[:, 0, :3].reshape(2 * batch, spans, 3), 1)
    loss_terms = lax.dynamic_slice_in_dim(seq_terms, core * batch, batch, 0)

    coef_kl = 5.0 * temper * tok_weight / count_tok
    coef_mlm = 2.0 * mask_weight / count_mask

    def by_token(values):
        return values.reshape(-1, 1)

    s_tiles = jnp.exp((s_peaks - by_token(s_peak)) / temper)
    t_tiles = jnp.exp((t_peaks - by_token(t_peak)) / temper)
    back = (
        s_half,
        t_half,
        s_tiles * by_token(coef_kl / s_half_sum),
        t_tiles * by_token(coef_kl / t_half_sum),
        s_tiles * s_tiles * by_token(coef_mlm / s_full_sum),
        by_token(coef_mlm),
        local_targets,
        s_table,
    )
    d_logits, d_rows = [None] * mp, [None] * mp
    for step in range(mp):
        k = (step + 1) % mp
        d_logits[k], d_rows[k] = head_back(k, rows, *back)
    d_head = ring_sum(d_rows)
    g_head = table_grad(s_all.T, d_logits)
    d_two = d_head + cos_pull(own_weight / count_tok)[0]

    d_embed, g_heads, g_units, g_vectors = layer_backward(
        s_classes, s_vectors, units, kept, d_two, valid, spans
    )
    d_all = jnp.concatenate(ring_list(d_embed), 0)
    g_table = add_rows(g_head, d_all.T, local_inputs)

    def by_place(summed, kinds, cut):
        return [
            jnp.concatenate(
                [summed[:, (t * mp + k) * cut : (t * mp + k + 1) * cut] for t in range(kinds)], 1
            )
            for k in range(mp)
        ]

    units_sum = scatter_dp(jnp.concatenate(g_units, 1))
    g_position = lax.dynamic_update_slice_in_dim(
        jnp.zeros((features, length), bf), d_embed.T, own_part * rows, 1
    )
    heads_at = mp * 4 * head_cut
    late_padded = -(heads_at + length + vector_rows) % (2 * LANES)
    late = scatter_dp(
        jnp.concatenate(
            g_heads
            + [g_position, g_vectors.T.astype(bf), jnp.zeros((features, late_padded), bf)],
            1,
        )
    )
    own_table = scatter_dp(g_table)
    own_units = ring_sum(by_place(units_sum, 2, unit_cut))
    own_heads = ring_sum(by_place(late, 4, head_cut))
    own_small = jnp.sum(natural(ring_list(late[:, heads_at:].astype(bf))).astype(f32), 0)

    shared_sq = jnp.sum(own_small * own_small) / mp
    squares = (
        jnp.sum(own_table * own_table)
        + jnp.sum(own_units * own_units)
        + jnp.sum(own_heads * own_heads)
        + shared_sq
    )
    squares = sum_all(jnp.broadcast_to(squares, (8, LANES)))[0, 0]
    norm = jnp.sqrt(squares)
    factor = clip_limit / jnp.maximum(norm, clip_limit)

    owned = (
        own_table.T,
        own_small[:, :length].T,
        jnp.stack([own_heads[:, t * head_cut : (t + 1) * head_cut] for t in range(3)]),
        own_heads[:, 3 * head_cut :].T,
        own_units[:, :unit_cut],
        own_units[:, unit_cut:].T,
        own_small[:, length : length + vector_rows].T,
    )
    masters = (
        student_table,
        student_position,
        student_project,
        student_output,
        student_expand,
        student_reduce,
        student_vectors,
    )
    firsts = (
        first_table,
        first_position,
        first_project,
        first_output,
        first_expand,
        first_reduce,
        first_vectors,
    )
    seconds = (
        square_table,
        square_position,
        square_project,
        square_output,
        square_expand,
        square_reduce,
        square_vectors,
    )
    results = []
    for index in range(7):
        rate = rate_vector if index == 6 else rate_table if index == 0 else rate_matrix
        decay = 0.0 if index == 6 else weight_decay
        results += adam_update(
            masters[index], firsts[index], seconds[index], owned[index], factor, rate, decay
        )
    loss_counts = jnp.stack([count_tok, count_mask])
    return (*results, norm, loss_terms, loss_counts)


def solution(mesh):
    in_specs = (
        P("dp", None),
        P("dp", None),
        P("dp"),
        P("dp"),
        P(),
        P("mp", None),
        P(),
        P(None, None, "mp"),
        P("mp", None),
        P(None, "mp"),
        P("mp", None),
        P(),
        P("mp", "dp"),
        P(None, "dp"),
        P(None, "dp", "mp"),
        P("mp", "dp"),
        P("dp", "mp"),
        P("mp", "dp"),
        P(None, "dp"),
        P("mp", "dp"),
        P(None, "dp"),
        P(None, "dp", "mp"),
        P("mp", "dp"),
        P("dp", "mp"),
        P("mp", "dp"),
        P(None, "dp"),
        P("mp", "dp"),
        P(None, "dp"),
        P(None, "dp", "mp"),
        P("mp", "dp"),
        P("dp", "mp"),
        P("mp", "dp"),
        P(None, "dp"),
    )
    out_specs = (
        P("mp", "dp"),
        P("mp", "dp"),
        P("mp", "dp"),
        P(None, "dp"),
        P(None, "dp"),
        P(None, "dp"),
        P(None, "dp", "mp"),
        P(None, "dp", "mp"),
        P(None, "dp", "mp"),
        P("mp", "dp"),
        P("mp", "dp"),
        P("mp", "dp"),
        P("dp", "mp"),
        P("dp", "mp"),
        P("dp", "mp"),
        P("mp", "dp"),
        P("mp", "dp"),
        P("mp", "dp"),
        P(None, "dp"),
        P(None, "dp"),
        P(None, "dp"),
        P(),
        P("dp", None),
        P(),
    )
    return jax.shard_map(body, mesh=mesh, in_specs=in_specs, out_specs=out_specs, check_vma=False)
```

```python
import jax
import jax.numpy as jnp
from jax import lax
from jax.experimental import pallas as pl
from jax.experimental.pallas import tpu as pltpu
from jax.sharding import PartitionSpec as P

HD = 64
STEP = 10
LANES = 128
LOG2E = 1.4426950408889634


eps_norm = 1e-05
mask_token = 103
temper = 2.0
beta_first = 0.9
beta_second = 0.999
adam_eps = 1e-08
rate_table = 0.5
rate_matrix = 0.1
rate_vector = 0.3
weight_decay = 0.01
clip_limit = 1.0
bf = jnp.bfloat16
f32 = jnp.float32
vmem_bytes = 56 * 1024 * 1024


def swap(x, bit):
    count = lax.axis_size("dp")
    return lax.ppermute(x, "dp", [(i, i ^ bit) for i in range(count)])


def rotate(x, by=1):
    count = lax.axis_size("mp")
    return lax.ppermute(x, "mp", [(i, (i + by) % count) for i in range(count)])


def chip_bits():
    count = lax.axis_size("dp")
    bits = []
    bit = 2
    while bit < count:
        bits.append(bit)
        bit *= 2
    return bits


def ordered(bit, mine, other, axis):
    low = (lax.axis_index("dp") & bit) == 0
    return jnp.where(
        low, jnp.concatenate([mine, other], axis), jnp.concatenate([other, mine], axis)
    )


def phase(*arrays):
    return lax.optimization_barrier(arrays)


def gather_start(x):
    half = x.shape[1] // 2
    bits = chip_bits()
    parts = []
    for part, order in ((x[:, :half], bits), (x[:, half:], bits[::-1])):
        pieces = {0: part}
        if order:
            pieces[order[0] // 2] = swap(part, order[0])
        parts.append(pieces)
    return parts


def gather_rest(parts):
    done = []
    bits = chip_bits()
    for pieces, order in zip(parts, (bits[1:], bits[::-1][1:])):
        pieces = dict(pieces)
        for bit in order:
            for chip in list(pieces):
                pieces[chip | (bit // 2)] = swap(pieces[chip], bit)
        done.append(pieces)
    return done


def gather_end(parts):
    placed, width = [], 0
    for pieces in parts:
        rows, columns = pieces[0].shape
        placed += [(piece, chip * rows, width) for chip, piece in pieces.items()]
        width += columns
    mine = assemble(placed, (len(parts[0]) * rows, width))
    return mine, swap(mine, 1)


def scatter_start(y):
    total_rows, columns = y.shape
    count = lax.axis_size("dp")
    half = columns // 2
    state = []
    for part in (y[:, :half], y[:, half:]):
        mine, other = part[: total_rows // 2], part[total_rows // 2 :]
        left = mine.astype(f32) + swap(other.astype(bf), 1).astype(f32)
        state.append(left.reshape(count // 2, total_rows // count, -1))
    return state


def scatter_step(state, step):
    bits = chip_bits()
    if step >= len(bits):
        return state
    after = []
    for which, left in enumerate(state):
        groups, rows, columns = left.shape
        if which == 0:
            bit = bits[::-1][step]
            keep, give = left[: groups // 2], left[groups // 2 :]
        else:
            bit = bits[step]
            split = left.reshape(groups // 2, 2, rows, columns)
            keep, give = split[:, 0], split[:, 1]
        after.append(keep + swap(give.astype(bf), bit).astype(f32))
    return after


def scatter_end(state):
    return jnp.concatenate([left[0] for left in state], 1)


def scatter_all(state):
    for step in range(1, len(chip_bits())):
        state = scatter_step(state, step)
    return state


def order_matrix(features, share):
    count = lax.axis_size("dp")
    at = jnp.arange(features)
    block, inside = at // share, at % share
    other_core, chip = block // (count // 2), block % (count // 2)
    source = (lax.axis_index("dp") ^ (chip * 2 + other_core)) * share + inside
    return (jnp.arange(features)[:, None] == source[None, :]).astype(bf)


def gather_mp(x):
    return [x] + [rotate(x, by) for by in range(1, lax.axis_size("mp"))]


def natural(entries):
    count = lax.axis_size("mp")
    index = lax.axis_index("mp")
    stacked = jnp.stack(entries)
    return jnp.stack(
        [
            lax.dynamic_index_in_dim(stacked, (index - i) % count, 0, keepdims=False)
            for i in range(count)
        ]
    )


def sum_mp(terms):
    total = terms[0].astype(f32)
    for k in range(1, len(terms)):
        total = total + rotate(terms[k].astype(bf), -k).astype(f32)
    return total


def sum_all(x):
    bit = 1
    while bit < lax.axis_size("dp"):
        x = x + swap(x, bit)
        bit *= 2
    count = lax.axis_size("mp")
    bit = 1
    while bit < count:
        x = x + lax.ppermute(x, "mp", [(i, i ^ bit) for i in range(count)])
        bit *= 2
    return x


def tile_of(total, cap):
    best = LANES
    for size in range(LANES, min(total, cap) + 1, LANES):
        if total % size == 0:
            best = size
    return best


def call(body, grid, in_specs, out_specs, out_shape, scratch, flops, moved):
    return pl.pallas_call(
        body,
        grid=grid,
        in_specs=in_specs,
        out_specs=out_specs,
        out_shape=out_shape,
        scratch_shapes=scratch,
        compiler_params=pltpu.CompilerParams(
            dimension_semantics=("arbitrary",) * len(grid), vmem_limit_bytes=vmem_bytes
        ),
        cost_estimate=pl.CostEstimate(flops=flops, bytes_accessed=moved, transcendentals=0),
    )


def assemble(placed, shape):
    kind = placed[0][0].dtype
    if any(at % LANES or x.shape[1] % LANES or x.shape[0] % 16 for x, _, at in placed):
        out = jnp.zeros(shape, kind)
        for x, row, at in placed:
            out = lax.dynamic_update_slice(out, x, (row, at))
        return out
    count = len(placed)

    def body(*refs):
        ins, out, sems = refs[:count], refs[count], refs[count + 1]
        copies = []
        for n, (x, row, at) in enumerate(placed):
            high, wide = x.shape
            copies.append(
                pltpu.make_async_copy(
                    ins[n], out.at[row : row + high, at : at + wide], sems.at[n]
                )
            )
        for copy in copies:
            copy.start()
        for copy in copies:
            copy.wait()

    moved = 2 * sum(x.size * x.dtype.itemsize for x, _, _ in placed)
    return pl.pallas_call(
        body,
        in_specs=[pl.BlockSpec(memory_space=pl.ANY)] * count,
        out_specs=pl.BlockSpec(memory_space=pltpu.VMEM),
        out_shape=jax.ShapeDtypeStruct(shape, kind),
        scratch_shapes=[pltpu.SemaphoreType.DMA((count,))],
        compiler_params=pltpu.CompilerParams(vmem_limit_bytes=vmem_bytes),
        cost_estimate=pl.CostEstimate(flops=0, bytes_accessed=moved, transcendentals=0),
    )(*[x for x, _, _ in placed])


def stacked(arrays):
    placed, row = [], 0
    for x in arrays:
        placed.append((x, row, 0))
        row += x.shape[0]
    return assemble(placed, (row, arrays[0].shape[1]))


def joined(project, output_t, expand, reduce_t):
    rows = expand.shape[0]
    parts = [project.shape[2]] * 3 + [x.shape[1] for x in (output_t, expand, reduce_t)]
    if any(part % LANES for part in parts):
        return jnp.concatenate(
            [x.astype(bf) for x in (*project, output_t, expand, reduce_t)], 1
        )

    def body(project_ref, output_ref, expand_ref, reduce_ref, out_ref):
        at = 0
        for value in (
            project_ref[0], project_ref[1], project_ref[2], output_ref[...], expand_ref[...],
            reduce_ref[...],
        ):
            out_ref[:, at : at + value.shape[1]] = value.astype(bf)
            at += value.shape[1]

    shape = (rows, sum(parts))
    return call(
        body,
        (1,),
        [whole(x.shape) for x in (project, output_t, expand, reduce_t)],
        whole(shape),
        jax.ShapeDtypeStruct(shape, bf),
        [],
        0,
        6 * shape[0] * shape[1],
    )(project, output_t, expand, reduce_t)


def by_kind(shares, cuts, models, tail):
    rows = shares[0].shape[0] // models
    placed, to = [], 0
    for model in range(models):
        at = 0
        for cut in cuts:
            for n in range(len(shares)):
                placed.append((n, model, at, cut, to))
                to += cut
            at += cut
    if any(cut % LANES for cut in cuts):
        return jnp.concatenate(
            [
                shares[n][model * rows : (model + 1) * rows, at : at + cut]
                for n, model, at, cut, _ in placed
            ]
            + [tail],
            1,
        )
    count = len(shares)

    def body(*refs):
        out_ref = refs[-1]
        for n, model, at, cut, into in placed:
            part = slice(model * rows, (model + 1) * rows)
            out_ref[:, into : into + cut] = refs[n][part, at : at + cut]
        out_ref[:, to:] = refs[count][...]

    shape = (rows, to + tail.shape[1])
    return call(
        body,
        (1,),
        [whole(x.shape) for x in (*shares, tail)],
        whole(shape),
        jax.ShapeDtypeStruct(shape, bf),
        [],
        0,
        4 * shape[0] * shape[1],
    )(*shares, tail)


def whole(shape):
    return pl.BlockSpec(shape, lambda *_: (0,) * len(shape))


def onto(x, tables):
    total, at = None, 0
    for table in tables:
        wide = table.shape[0]
        term = jnp.dot(x[:, at : at + wide], table, preferred_element_type=f32)
        total = term if total is None else total + term
        at += wide
    return total


def rows_times(x, flipped):
    return lax.dot_general(x, flipped, (((1,), (1,)), ((), ())), preferred_element_type=f32)


def pick_rows(ids, tables):
    half, vocab = tables[0].shape
    width = half * len(tables)
    tile = tile_of(vocab, 1536)
    rows = ids.shape[0]

    def body(ids_ref, *refs):
        table_refs, (out_ref, total) = refs[: len(tables)], refs[len(tables) :]
        j = pl.program_id(0)

        @pl.when(j == 0)
        def _():
            total[...] = jnp.zeros_like(total)

        lane = lax.broadcasted_iota(jnp.int32, (rows, tile), 1)
        hot = jnp.where(lane == ids_ref[...] - j * tile, 1.0, 0.0).astype(bf)
        for t, table_ref in enumerate(table_refs):
            total[:, t * half : (t + 1) * half] += rows_times(hot, table_ref[...])

        @pl.when(j == pl.num_programs(0) - 1)
        def _():
            out_ref[...] = total[...].astype(bf)

    return call(
        body,
        (vocab // tile,),
        [whole((rows, 1))] + [pl.BlockSpec((half, tile), lambda j: (0, j))] * len(tables),
        whole((rows, width)),
        jax.ShapeDtypeStruct((rows, width), bf),
        [pltpu.VMEM((rows, width), f32)],
        2 * rows * width * vocab,
        2 * width * vocab,
    )(ids, *tables)


def lane_value(values, j):
    lane = lax.broadcasted_iota(jnp.int32, values.shape, 1)
    return jnp.sum(jnp.where(lane == j, values, 0.0), 1, keepdims=True)


def head_tile(vocab):
    return tile_of(vocab, 1536)


def head_pass(x, table):
    vocab, width = table.shape
    rows = x.shape[0]
    tile = head_tile(vocab)
    step = min(rows, 256)
    fold = range(0, tile, LANES)

    def body(x_ref, table_ref, half_ref, peaks_ref, stats_ref):
        j = pl.program_id(0)

        @pl.when(j == 0)
        def _():
            lane = lax.broadcasted_iota(jnp.int32, stats_ref.shape, 1)
            stats_ref[...] = jnp.where(lane == 0, -1e30, 0.0)
            peaks_ref[...] = jnp.zeros_like(peaks_ref)

        for b in range(rows // step):
            part = pl.ds(b * step, step)
            z = rows_times(x_ref[part, :], table_ref[...])
            before = stats_ref[part, :]
            highest = z[:, :LANES]
            for at in fold[1:]:
                highest = jnp.maximum(highest, z[:, at : at + LANES])
            peak = jnp.maximum(before[:, 0:1], jnp.max(highest, 1, keepdims=True))
            shrink = jnp.exp((before[:, 0:1] - peak) * 0.5)
            lane = lax.broadcasted_iota(jnp.int32, (step, LANES), 1)
            half_sum, cross = jnp.zeros((step, LANES), f32), jnp.zeros((step, LANES), f32)
            for at in fold:
                piece = z[:, at : at + LANES]
                half = jnp.exp2((piece - peak) * (0.5 * LOG2E))
                half_ref[part, at : at + LANES] = half.astype(bf)
                half_sum += half
                cross += half * piece
            half_sum = before[:, 1:2] * shrink + jnp.sum(half_sum, 1, keepdims=True)
            cross = before[:, 3:4] * shrink + jnp.sum(cross, 1, keepdims=True)
            after = jnp.where(lane == 0, peak, before)
            after = jnp.where(lane == 1, half_sum, after)
            stats_ref[part, :] = jnp.where(lane == 3, cross, after)
            peaks_ref[part, :] = jnp.where(lane == j, peak, peaks_ref[part, :])

    lanes = whole((rows, LANES))
    stat = jax.ShapeDtypeStruct((rows, LANES), f32)
    return call(
        body,
        (vocab // tile,),
        [whole((rows, width)), pl.BlockSpec((tile, width), lambda j: (j, 0))],
        [pl.BlockSpec((rows, tile), lambda j: (0, j)), lanes, lanes],
        [jax.ShapeDtypeStruct((rows, vocab), bf), stat, stat],
        [],
        2 * rows * width * vocab,
        2 * width * vocab + 2 * rows * vocab,
    )(x, table)


def student_pass(x, tables, other, weight, targets):
    half_width, vocab = tables[0].shape
    rows, width = x.shape
    tile = head_tile(vocab)
    step = min(rows, 256)
    block_wide = 256 if tile % 256 == 0 else LANES
    count = len(tables)

    def body(x_ref, *refs):
        table_refs, refs = refs[:count], refs[count:]
        other_ref, weight_ref, target_ref, half_ref, peaks_ref, stats_ref = refs[:6]
        table, peak_ref, high_ref, *sums = refs[6:]
        new, total = sums[:4], sums[4:]
        j = pl.program_id(0)
        for t, table_ref in enumerate(table_refs):
            table[t * half_width : (t + 1) * half_width, :] = table_ref[...]

        def over_rows(work):
            @pl.loop(0, rows // step)
            def _(b):
                work(pl.ds(pl.multiple_of(b * step, step), step))

        @pl.when(j == 0)
        def _():
            peaks_ref[...] = jnp.zeros_like(peaks_ref)
            for ref in total:
                ref[...] = jnp.zeros_like(ref)

            def begin(part):
                z = jnp.dot(x_ref[part, :], table[:, :LANES], preferred_element_type=f32)
                top = jnp.broadcast_to(jnp.max(z, 1, keepdims=True), z.shape)
                peak_ref[part, :] = top
                high_ref[part, :] = top

            over_rows(begin)

        def digest(part):
            lane = lax.broadcasted_iota(jnp.int32, (step, LANES), 1)
            peak, high = peak_ref[part, :], high_ref[part, :]
            values = [jnp.zeros((step, LANES), f32) for _ in range(4)]
            target = jnp.broadcast_to(target_ref[part, :] - j * tile, (step, LANES)) - lane
            for first in range(0, tile, block_wide):
                z = jnp.dot(
                    x_ref[part, :],
                    table[:, first : first + block_wide],
                    preferred_element_type=f32,
                )
                for inner in range(0, block_wide, LANES):
                    at = first + inner
                    piece = z[:, inner : inner + LANES]
                    half = jnp.exp2((piece - peak) * (0.5 * LOG2E))
                    half_ref[part, at : at + LANES] = half.astype(bf)
                    high = jnp.maximum(high, piece)
                    values[0] += half
                    values[1] += half * half
                    values[2] += other_ref[part, at : at + LANES].astype(f32) * piece
                    values[3] += jnp.where(target == at, piece, 0.0)
            for ref, value in zip(new, values):
                ref[part, :] = value
            high_ref[part, :] = high

        over_rows(digest)

        def top_of(part):
            return jnp.broadcast_to(
                jnp.max(high_ref[part, :], 1, keepdims=True), (step, LANES)
            )

        @pl.when(jnp.max(high_ref[...] - peak_ref[...]) > 60.0)
        def _():
            def raise_peak(part):
                before, top = peak_ref[part, :], top_of(part)
                shrink = jnp.exp((before - top) * 0.5)
                total[0][part, :] *= shrink
                total[1][part, :] *= shrink * shrink
                peak_ref[part, :] = top

            over_rows(raise_peak)
            over_rows(digest)

        def settle(part):
            lane = lax.broadcasted_iota(jnp.int32, (step, LANES), 1)
            before, top = peak_ref[part, :], top_of(part)
            shrink = jnp.exp((before - top) * 0.5)
            weight_now = jnp.broadcast_to(lane_value(weight_ref[part, :], j), (step, LANES))
            total[0][part, :] = (total[0][part, :] + new[0][part, :]) * shrink
            total[1][part, :] = (total[1][part, :] + new[1][part, :]) * (shrink * shrink)
            total[2][part, :] += new[2][part, :] * weight_now
            total[3][part, :] += new[3][part, :]
            peaks_ref[part, :] = jnp.where(lane == j, before, peaks_ref[part, :])
            peak_ref[part, :] = top

            @pl.when(j == pl.num_programs(0) - 1)
            def _():
                out = jnp.where(lane == 0, top, 0.0)
                for n, ref in enumerate(total):
                    out = jnp.where(lane == n + 1, jnp.sum(ref[part, :], 1, keepdims=True), out)
                stats_ref[part, :] = out

        over_rows(settle)

    block = pl.BlockSpec((rows, tile), lambda j: (0, j))
    lanes = whole((rows, LANES))
    stat = jax.ShapeDtypeStruct((rows, LANES), f32)
    return call(
        body,
        (vocab // tile,),
        [whole((rows, width))]
        + [pl.BlockSpec((half_width, tile), lambda j: (0, j))] * count
        + [block, lanes, whole((rows, 1))],
        [block, lanes, lanes],
        [jax.ShapeDtypeStruct((rows, vocab), bf), stat, stat],
        [pltpu.VMEM((width, tile), bf)] + [pltpu.VMEM((rows, LANES), f32)] * 10,
        2 * rows * width * vocab,
        2 * width * vocab + 4 * rows * vocab,
    )(x, *tables, other, weight, targets)


def head_back(k, k_half, rows, s_half, t_half, s_scale, t_scale, f_scale, hit_scale, targets, tables):
    part_width, vocab = tables[0].shape
    width = part_width * len(tables)
    tile = head_tile(vocab)
    step = min(rows, 256)

    def body(s_ref, t_ref, a_ref, b_ref, c_ref, h_ref, target_ref, *refs):
        table_refs, (d_ref, out_ref, total) = refs[: len(tables)], refs[len(tables) :]
        j = pl.program_id(0)

        @pl.when(j == 0)
        def _():
            total[...] = jnp.zeros_like(total)

        for begin in range(0, rows, step):
            part = pl.ds(begin, step)
            a = jnp.broadcast_to(lane_value(a_ref[part, :], j), (step, LANES))
            b = jnp.broadcast_to(lane_value(b_ref[part, :], j), (step, LANES))
            c = jnp.broadcast_to(lane_value(c_ref[part, :], j), (step, LANES))
            h = jnp.broadcast_to(h_ref[part, :], (step, LANES))
            target = jnp.broadcast_to(target_ref[part, :] - j * tile, (step, LANES))
            lane = lax.broadcasted_iota(jnp.int32, (step, LANES), 1)
            for at in range(0, tile, LANES):
                half = s_ref[part, at : at + LANES].astype(f32)
                grad = half * (a + half * c) - t_ref[part, at : at + LANES].astype(f32) * b
                grad -= jnp.where(lane == target - at, h, 0.0)
                d_ref[part, at : at + LANES] = grad.astype(bf)
            for t, table_ref in enumerate(table_refs):
                total[part, t * part_width : (t + 1) * part_width] += rows_times(
                    d_ref[part, :], table_ref[...]
                )

        @pl.when(j == pl.num_programs(0) - 1)
        def _():
            out_ref[...] = total[...].astype(bf)

    block = pl.BlockSpec((rows, tile), lambda j: (k_half, j))
    lanes = pl.BlockSpec((rows, LANES), lambda j: (k, 0))
    column = pl.BlockSpec((rows, 1), lambda j: (k, 0))
    return call(
        body,
        (vocab // tile,),
        [block, block, lanes, lanes, lanes, column, column]
        + [pl.BlockSpec((part_width, tile), lambda j: (0, j))] * len(tables),
        [pl.BlockSpec((rows, tile), lambda j: (0, j)), whole((rows, width))],
        [jax.ShapeDtypeStruct((rows, vocab), bf), jax.ShapeDtypeStruct((rows, width), bf)],
        [pltpu.VMEM((rows, width), f32)],
        2 * rows * width * vocab,
        2 * width * vocab + 6 * rows * vocab,
    )(s_half, t_half, s_scale, t_scale, f_scale, hit_scale, targets, *tables)


def table_grad(x_flipped, d_logits):
    width = x_flipped.shape[0]
    rows, vocab = d_logits[0].shape
    tile = tile_of(vocab, 1536)
    count = len(d_logits)

    def body(x_ref, *refs):
        total = None
        for k, d_ref in enumerate(refs[:-1]):
            term = jnp.dot(
                x_ref[:, k * rows : (k + 1) * rows], d_ref[...], preferred_element_type=f32
            )
            total = term if total is None else total + term
        refs[-1][...] = total.astype(bf)

    return call(
        body,
        (vocab // tile,),
        [whole((width, rows * count))] + [pl.BlockSpec((rows, tile), lambda j: (0, j))] * count,
        pl.BlockSpec((width, tile), lambda j: (0, j)),
        jax.ShapeDtypeStruct((width, vocab), bf),
        [],
        2 * rows * count * width * vocab,
        2 * rows * count * vocab + 4 * width * vocab,
    )(x_flipped, *d_logits)


def add_rows(base, e_flipped, ids, half):
    width, vocab = base.shape
    rows = ids.shape[0]
    tile = tile_of(vocab, 768)
    step = tile_of(rows, 512)
    tiles = vocab // tile
    first, count = 0, tiles
    if half is not None:
        first, count = (0, tiles // 2) if half == 0 else (tiles // 2, tiles - tiles // 2)

    def body(base_ref, e_ref, ids_ref, out_ref):
        j = pl.program_id(0) + first
        lane = lax.broadcasted_iota(jnp.int32, (step, tile), 1)
        total = base_ref[...]
        for begin in range(0, rows, step):
            part = slice(begin, begin + step)
            hot = jnp.where(lane == ids_ref[part, :] - j * tile, 1.0, 0.0).astype(bf)
            total += jnp.dot(e_ref[:, part], hot, preferred_element_type=f32)
        out_ref[...] = total

    block = pl.BlockSpec((width, tile), lambda j: (0, j + first))
    return pl.pallas_call(
        body,
        grid=(count,),
        in_specs=[block, whole((width, rows)), whole((rows, 1))],
        out_specs=block,
        out_shape=jax.ShapeDtypeStruct((width, vocab), f32),
        input_output_aliases={0: 0},
        compiler_params=pltpu.CompilerParams(
            dimension_semantics=("arbitrary",), vmem_limit_bytes=vmem_bytes
        ),
        cost_estimate=pl.CostEstimate(
            flops=2 * rows * width * vocab, bytes_accessed=8 * width * vocab, transcendentals=0
        ),
    )(base, e_flipped, ids)


def heads_reordered(x):
    count = lax.axis_size("mp")
    return jnp.concatenate(list(natural(jnp.split(x, count, -1))), -1)


def gather_sequence(x, spans):
    parts = [x, swap(x, 1)]
    if spans > 1:
        count = lax.axis_size("mp")
        groups = [list(range(i, i + spans)) for i in range(0, count, spans)]
        both = heads_reordered(jnp.concatenate(parts, 1))
        both = lax.all_gather(both, "mp", axis=1, axis_index_groups=groups, tiled=True)
        parts = [heads_reordered(both)]
    return parts


def scatter_sequence(parts, spans):
    if spans > 1:
        count = lax.axis_size("mp")
        groups = [list(range(i, i + spans)) for i in range(0, count, spans)]
        x = lax.psum_scatter(
            heads_reordered(parts[0].astype(f32)),
            "mp",
            scatter_dimension=1,
            axis_index_groups=groups,
            tiled=True,
        )
        parts = jnp.split(heads_reordered(x), 2, 1)
    return parts[0].astype(f32) + swap(parts[1].astype(bf), 1).astype(f32)


def sequence_parts(core, spans):
    if spans == 1:
        return [core, 1 - core]
    return [chip * 2 + side for chip in range(spans) for side in (core, 1 - core)]


def norm_parts(x):
    centre = x - jnp.mean(x, -1, keepdims=True)
    spread = jnp.mean(centre * centre, -1, keepdims=True)
    scale = lax.rsqrt(spread + eps_norm)
    return centre * scale, scale


def norm_back(unit, scale, gain, grad):
    inner = grad * gain
    slope = inner - jnp.mean(inner, -1, keepdims=True)
    slope = (slope - unit * jnp.mean(inner * unit, -1, keepdims=True)) * scale
    return slope, jnp.sum(grad * unit, 0, keepdims=True), jnp.sum(grad, 0, keepdims=True)


def resident(shape):
    return pl.BlockSpec(shape, lambda *_: (0,) * len(shape), pipeline_mode=pl.Buffered(1))


def put_rows(ref, j, values):
    row = lax.broadcasted_iota(jnp.int32, ref.shape, 0)
    add = jnp.zeros(ref.shape, f32)
    for at, value in values.items():
        add = jnp.where(row == at, value, add)

    @pl.when(j == 0)
    def _():
        ref[...] = add

    @pl.when(j > 0)
    def _():
        ref[...] += add


def weight_blocks(classes, model, features, units, opening):
    columns = 4 * features + 2 * units
    wide = 3 * features if opening and columns % (3 * features) == 0 else columns
    return [
        pl.BlockSpec(
            (c.shape[0], wide),
            lambda *_: (0, model * columns // wide),
            pipeline_mode=pl.Buffered(1),
        )
        for c in classes
    ]


def columns_of(features, units):
    cuts, at = [], 0
    for wide in [features] * 4 + [units] * 2:
        cuts.append(slice(at, at + wide))
        at += wide
    return cuts


def side_by_side(x, classes, cut):
    return jnp.concatenate([rows_times(x, c[:, cut]) for c in classes], 1)


def through(x, classes, cut):
    high = classes[0].shape[0]
    total = None
    for t, c in enumerate(classes):
        term = jnp.dot(x[:, t * high : (t + 1) * high], c[:, cut], preferred_element_type=f32)
        total = term if total is None else total + term
    return total


def layer_open(embedded, vectors, classes, model, units):
    rows, features = embedded.shape
    cuts = columns_of(features, units)
    step = min(rows, 256)
    count = len(classes)

    def body(x_ref, vectors_ref, *refs):
        class_refs, (zero_ref, q_ref, kv_ref) = refs[:count], refs[count:]
        unit, _ = norm_parts(x_ref[...])
        zero = unit * vectors_ref[0:1, :] + vectors_ref[1:2, :]
        zero_ref[...] = zero
        low = zero.astype(bf)
        q_ref[...] = through(low, class_refs, cuts[0]).astype(bf)
        kv_ref[0] = through(low, class_refs, cuts[1]).astype(bf)
        kv_ref[1] = through(low, class_refs, cuts[2]).astype(bf)

    block = pl.BlockSpec((step, features), lambda j: (j, 0))
    return call(
        body,
        (rows // step,),
        [block, whole(vectors.shape)] + weight_blocks(classes, model, features, units, True),
        [block, block, pl.BlockSpec((2, step, features), lambda j: (0, j, 0))],
        [
            jax.ShapeDtypeStruct((rows, features), f32),
            jax.ShapeDtypeStruct((rows, features), bf),
            jax.ShapeDtypeStruct((2, rows, features), bf),
        ],
        [],
        6 * rows * features * features,
        6 * features * features + 16 * rows * features,
    )(embedded, vectors, *classes)


def head_lanes(shape, which):
    return (lax.broadcasted_iota(jnp.int32, shape, 1) // HD) == which


def layer_close(zero, query, parts, valid, vectors, classes, model, units):
    rows, features = zero.shape
    length = valid.shape[1]
    cells = len(parts)
    cuts = columns_of(features, units)
    step = min(rows, 256)
    count = len(classes)
    pair = LANES // HD

    def body(zero_ref, q_ref, valid_ref, vectors_ref, *refs):
        part_refs, class_refs, refs = refs[:cells], refs[cells : cells + count], refs[cells + count :]
        two_ref, attn_ref, log_ref, one_pre_ref, two_pre_ref = refs
        allowed = valid_ref[...] > 0.0
        log_lane = lax.broadcasted_iota(jnp.int32, (step, LANES), 1)
        logs = jnp.zeros((step, LANES), f32)
        pieces = []
        for block in range(features // LANES):
            lanes = slice(block * LANES, (block + 1) * LANES)
            keys = jnp.concatenate([ref[0, :, lanes] for ref in part_refs], 0)
            values = jnp.concatenate([ref[1, :, lanes] for ref in part_refs], 0)
            merged = jnp.zeros((step, LANES), f32)
            for which in range(pair):
                mine = head_lanes((step, LANES), which)
                q = jnp.where(mine, q_ref[:, lanes] * HD ** (-0.5), 0.0).astype(bf)
                score = jnp.where(allowed, rows_times(q, keys), -1e30)
                peak = jnp.max(score, 1, keepdims=True)
                expo = jnp.exp(score - peak)
                total = jnp.sum(expo, 1, keepdims=True)
                weight = (expo * (1.0 / total)).astype(bf)
                merged = jnp.where(
                    mine, jnp.dot(weight, values, preferred_element_type=f32), merged
                )
                logs = jnp.where(log_lane == block * pair + which, peak + jnp.log(total), logs)
            pieces.append(merged)
        log_ref[...] = logs
        attn = jnp.concatenate(pieces, 1).astype(bf)
        attn_ref[...] = attn
        one_pre = side_by_side(attn, class_refs, cuts[3]) + vectors_ref[2:3, :] + zero_ref[...]
        one_pre_ref[...] = one_pre
        one = norm_parts(one_pre)[0] * vectors_ref[3:4, :] + vectors_ref[4:5, :]
        hidden = through(one.astype(bf), class_refs, cuts[4])
        active = gelu(hidden).astype(bf)
        two_pre = side_by_side(active, class_refs, cuts[5]) + vectors_ref[5:6, :] + one
        two_pre_ref[...] = two_pre
        two_ref[...] = norm_parts(two_pre)[0] * vectors_ref[6:7, :] + vectors_ref[7:8, :]

    block = pl.BlockSpec((step, features), lambda j: (j, 0))
    wide = jax.ShapeDtypeStruct((rows, features), f32)
    columns = cuts[-1].stop
    return call(
        body,
        (rows // step,),
        [block, block, whole(valid.shape), whole(vectors.shape)]
        + [resident(x.shape) for x in parts]
        + weight_blocks(classes, model, features, units, False),
        [block, block, pl.BlockSpec((step, LANES), lambda j: (j, 0)), block, block],
        [
            wide,
            jax.ShapeDtypeStruct((rows, features), bf),
            jax.ShapeDtypeStruct((rows, LANES), f32),
            wide,
            wide,
        ],
        [],
        2 * rows * features * (2 * length + features + 2 * units),
        2 * features * columns + 20 * rows * features,
    )(zero, query, valid, vectors, *parts, *classes)


def gelu(x):
    return 0.5 * x * (1.0 + lax.erf(x * 0.7071067811865476))


def gelu_slope(x):
    return 0.5 * (1.0 + lax.erf(x * 0.7071067811865476)) + x * 0.3989422804014327 * jnp.exp(
        -0.5 * x * x
    )


def units_back(d_two, two_pre, one_pre, vectors, classes, model, units):
    rows, features = d_two.shape
    cuts = columns_of(features, units)
    step = min(rows, 256)
    count = len(classes)

    def body(d_ref, two_pre_ref, one_pre_ref, vectors_ref, *refs):
        class_refs, refs = refs[:count], refs[count:]
        reduce_ref, active_ref, low_ref, hidden_ref, branch_ref, pre_ref, attn_ref, sums_ref = refs
        unit, scale = norm_parts(two_pre_ref[...])
        d_two_pre, gain_two, shift_two = norm_back(unit, scale, vectors_ref[6:7, :], d_ref[...])
        low = d_two_pre.astype(bf)
        reduce_ref[...] = low
        d_active = through(low, class_refs, cuts[5])
        unit, scale = norm_parts(one_pre_ref[...])
        one_low = (unit * vectors_ref[3:4, :] + vectors_ref[4:5, :]).astype(bf)
        low_ref[...] = one_low
        hidden = through(one_low, class_refs, cuts[4])
        bell = 0.5 * (1.0 + lax.erf(hidden * 0.7071067811865476))
        active_ref[...] = (hidden * bell).astype(bf)
        slope = bell + hidden * 0.3989422804014327 * jnp.exp(-0.5 * hidden * hidden)
        d_hidden = (d_active * slope).astype(bf)
        hidden_ref[...] = d_hidden
        d_one = side_by_side(d_hidden, class_refs, cuts[4]) + d_two_pre
        d_one_pre, gain_one, shift_one = norm_back(unit, scale, vectors_ref[3:4, :], d_one)
        pre_ref[...] = d_one_pre
        d_branch = d_one_pre.astype(bf)
        branch_ref[...] = d_branch
        attn_ref[...] = through(d_branch, class_refs, cuts[3]).astype(bf)
        put_rows(
            sums_ref,
            pl.program_id(0),
            {
                2: jnp.sum(d_one_pre, 0, keepdims=True),
                3: gain_one,
                4: shift_one,
                5: jnp.sum(d_two_pre, 0, keepdims=True),
                6: gain_two,
                7: shift_two,
            },
        )

    block = pl.BlockSpec((step, features), lambda j: (j, 0))
    broad = pl.BlockSpec((step, units), lambda j: (j, 0))
    columns = cuts[-1].stop
    low = jax.ShapeDtypeStruct((rows, features), bf)
    full = jax.ShapeDtypeStruct((rows, features), f32)
    high = jax.ShapeDtypeStruct((rows, units), bf)
    return call(
        body,
        (rows // step,),
        [block, block, block, whole(vectors.shape)]
        + weight_blocks(classes, model, features, units, False),
        [block, broad, block, broad, block, block, block, whole((8, features))],
        [low, high, low, high, low, full, low, jax.ShapeDtypeStruct((8, features), f32)],
        [],
        2 * rows * features * (features + 3 * units),
        2 * features * columns + 20 * rows * features + 4 * rows * units,
    )(d_two, two_pre, one_pre, vectors, *classes)


def columns_times(left, right):
    return lax.dot_general(left, right, (((0,), (0,)), ((), ())), preferred_element_type=f32)


def attention_back(query, parts, d_attn, logs, valid):
    rows, features = query.shape
    length = valid.shape[1]
    cells = len(parts)
    pair = LANES // HD

    def body(q_ref, d_ref, log_ref, valid_ref, *refs):
        part_refs, dq_ref, d_refs = refs[:cells], refs[cells], refs[cells + 1 :]
        j = pl.program_id(0)
        d_parts = [[None, None] for _ in range(cells)]
        allowed = valid_ref[...] > 0.0
        keys = jnp.concatenate([ref[0] for ref in part_refs], 0)
        values = jnp.concatenate([ref[1] for ref in part_refs], 0)
        merged = jnp.zeros((rows, LANES), f32)
        for which in range(pair):
            mine = head_lanes((rows, LANES), which)
            q = jnp.where(mine, q_ref[...] * HD ** (-0.5), 0.0).astype(bf)
            d = jnp.where(mine, d_ref[...], 0.0).astype(bf)
            log_total = lane_value(log_ref[...], j * pair + which)
            score = jnp.where(allowed, rows_times(q, keys), -1e30)
            weight = jnp.exp(score - log_total)
            slope = rows_times(d, values)
            low = weight.astype(bf)
            inner = jnp.sum(weight * slope, 1, keepdims=True)
            d_score = (weight * (slope - inner)).astype(bf)
            merged = jnp.where(
                mine, jnp.dot(d_score, keys, preferred_element_type=f32), merged
            )
            at = 0
            for cell, ref in enumerate(part_refs):
                here = slice(at, at + ref.shape[1])
                at = here.stop
                for slot, (left, right) in enumerate(((d_score, q), (low, d))):
                    term = columns_times(left[:, here], right)
                    had = d_parts[cell][slot]
                    d_parts[cell][slot] = term if had is None else had + term
        dq_ref[...] = (merged * HD ** (-0.5)).astype(bf)
        for ref, pieces in zip(d_refs, d_parts):
            for slot, piece in enumerate(pieces):
                ref[slot] = piece.astype(ref.dtype)

    block = pl.BlockSpec((rows, LANES), lambda j: (0, j))
    tall = [pl.BlockSpec((2, x.shape[1], LANES), lambda j: (0, 0, j)) for x in parts]
    return call(
        body,
        (features // LANES,),
        [block, block, whole(logs.shape), whole(valid.shape)] + tall,
        [block] + tall,
        [jax.ShapeDtypeStruct((rows, features), bf)]
        + [jax.ShapeDtypeStruct(x.shape, f32 if n == 0 else bf) for n, x in enumerate(parts)],
        [],
        10 * rows * features * length,
        16 * length * features,
    )(query, d_attn, logs, valid, *parts)


def embed_back(d_parts, d_one_pre, embedded, vectors, classes, model, units):
    rows, features = d_one_pre.shape
    cuts = columns_of(features, units)
    step = min(rows, 256)
    count = len(classes)

    def body(q_ref, k_ref, v_ref, pre_ref, x_ref, vectors_ref, *refs):
        class_refs, (out_ref, sums_ref) = refs[:count], refs[count:]
        d_zero = pre_ref[...]
        for t, part in enumerate((q_ref, k_ref, v_ref)):
            d_zero += side_by_side(part[...], class_refs, cuts[t])
        unit, scale = norm_parts(x_ref[...])
        d_embed, gain, shift = norm_back(unit, scale, vectors_ref[0:1, :], d_zero)
        out_ref[...] = d_embed.astype(bf)
        put_rows(sums_ref, pl.program_id(0), {0: gain, 1: shift})

    block = pl.BlockSpec((step, features), lambda j: (j, 0))
    return call(
        body,
        (rows // step,),
        [block] * 5
        + [whole(vectors.shape)]
        + weight_blocks(classes, model, features, units, True),
        [block, whole((8, features))],
        [
            jax.ShapeDtypeStruct((rows, features), bf),
            jax.ShapeDtypeStruct((8, features), f32),
        ],
        [],
        6 * rows * features * features,
        6 * features * features + 16 * rows * features,
    )(*d_parts, d_one_pre, embedded, vectors, *classes)


def cosine_loss(x_student, x_teacher):
    s_len = jnp.sqrt(jnp.sum(x_student * x_student, -1))
    t_len = jnp.sqrt(jnp.sum(x_teacher * x_teacher, -1))
    return 1.0 - jnp.sum(x_student * x_teacher, -1) / (s_len * t_len)


def adam_update(master, first, square, grad, factor, rate, decay):
    clipped = grad * factor
    new_first = beta_first * first + (1.0 - beta_first) * clipped
    new_square = beta_second * square + (1.0 - beta_second) * clipped * clipped
    first_hat = new_first / (1.0 - beta_first**STEP)
    square_hat = new_square / (1.0 - beta_second**STEP)
    updated = master - rate * (first_hat / (jnp.sqrt(square_hat) + adam_eps) + decay * master)
    return [updated, new_first, new_square]


def body(
    token_ids,
    mlm_flags,
    pad_lengths,
    group_ids,
    group_weight,
    teacher_table,
    teacher_position,
    teacher_project,
    teacher_output,
    teacher_expand,
    teacher_reduce,
    teacher_vectors,
    student_table,
    student_position,
    student_project,
    student_output,
    student_expand,
    student_reduce,
    student_vectors,
    first_table,
    first_position,
    first_project,
    first_output,
    first_expand,
    first_reduce,
    first_vectors,
    square_table,
    square_position,
    square_project,
    square_output,
    square_expand,
    square_reduce,
    square_vectors,
):
    mp, dp = lax.axis_size("mp"), lax.axis_size("dp")
    place, index = lax.axis_index("mp"), lax.axis_index("dp")
    core = index & 1
    batch, length = token_ids.shape
    spans = mp // (2 * batch)
    rows = length // (2 * spans)
    vocab_rows = student_table.shape[0]
    share = student_table.shape[1]
    features = share * dp
    start = place * vocab_rows

    packed = jnp.concatenate(
        [
            token_ids * 2 + mlm_flags,
            jnp.pad((pad_lengths * 256 + group_ids)[None], ((0, 0), (0, length - batch))),
        ]
    )
    packed = ordered(1, packed[None], swap(packed, 1)[None], 0)
    column_ids = packed[:, :batch].reshape(2 * batch, spans, 2, rows)
    lengths = (packed[:, batch, :batch] // 256).reshape(-1)
    groups = (packed[:, batch, :batch] % 256).reshape(-1)
    chosen = groups[:, None] == jnp.arange(group_weight.shape[0])[None, :]
    seq_weight = jnp.sum(jnp.where(chosen, group_weight[None, :], 0.0), -1)
    line_place = (place - jnp.arange(mp)) % mp
    line = lax.dynamic_index_in_dim(column_ids, core, 2, keepdims=False).reshape(mp, rows)
    line = jnp.take(line, line_place, axis=0)
    line_targets, line_flags = line // 2, line % 2
    line_inputs = jnp.where(line_flags == 1, mask_token, line_targets)
    line_sequence = line_place // spans
    line_part = (line_place % spans) * 2 + core
    line_positions = line_part[:, None] * rows + jnp.arange(rows)[None, :]
    line_lengths = jnp.take(lengths, line_sequence)
    line_real = (line_positions < line_lengths[:, None]).astype(f32)
    line_masked = line_flags.astype(f32) * line_real
    line_weight = jnp.take(seq_weight, line_sequence)[:, None]
    tok_weight, mask_weight = line_weight * line_real, line_weight * line_masked
    own_part = line_part[0]
    held = jnp.concatenate(
        [part * rows + jnp.arange(rows) for part in sequence_parts(core, spans)]
    )
    valid = (held < line_lengths[0]).astype(f32)[None]

    slots = -(-(11 * rows // (10 * mp) + 16) // 32) * 32
    plain = (line_real > 0) & (line_inputs != mask_token)
    owner = line_inputs // vocab_rows
    wanted = plain & (owner == place)
    away = (owner[0] - place) % mp
    from_owner = plain[0] & (away[None, :] == jnp.arange(mp)[:, None])
    ordinal = jnp.arange(rows)
    earlier = (ordinal[:, None] <= ordinal[None, :]).astype(bf)
    ranks = jnp.dot(
        jnp.concatenate([wanted, from_owner], 0).astype(bf), earlier, preferred_element_type=f32
    )
    ranks = ranks.astype(jnp.int32) - 1
    wanted_rank = jnp.where(wanted, ranks[:mp], -1)
    own_rank = jnp.sum(jnp.where(from_owner, ranks[mp:], 0), 0)
    mask_owner = mask_token // vocab_rows
    pair_counts = jnp.sum(
        (plain[None] & (owner[None] == jnp.arange(mp)[:, None, None])).astype(f32), -1
    )

    def wanted_ids(turn):
        number = jnp.arange(slots - 1) + turn * (slots - 1)
        match = wanted_rank[:, None, :] == number[None, :, None]
        ids = jnp.sum(jnp.where(match, line_inputs[:, None, :] - start + 1, 0), -1) - 1
        shared_id = jnp.where((place == mask_owner) & (turn == 0), mask_token - start, -1)
        shared_id = jnp.broadcast_to(shared_id, (mp, 1))
        return jnp.concatenate([ids, shared_id], 1).reshape(-1, 1)

    def own_slots(turn):
        number = own_rank - turn * (slots - 1)
        at = jnp.where(plain[0] & (number >= 0) & (number < slots - 1), away * slots + number, -1)
        masked_at = ((mask_owner - place) % mp) * slots + slots - 1
        is_mask = (line_real[0] > 0) & (line_inputs[0] == mask_token) & (turn == 0)
        at = jnp.where(is_mask, masked_at, at)
        return (at[:, None] == jnp.arange(mp * slots)[None, :]).astype(bf)

    def sent(found):
        return found[:slots], [
            rotate(found[k * slots : (k + 1) * slots], -k) for k in range(1, mp)
        ]

    def placed_rows(got, turn):
        return jnp.dot(own_slots(turn), stacked([got[0], *got[1]]), preferred_element_type=f32)

    def every_owner(ids):
        bit = 1
        while bit < dp:
            ids = jnp.concatenate([ids, swap(ids, bit)], 0)
            bit *= 2
        return ids

    def at_owners(d_embed, turn):
        sums = columns_times(own_slots(turn), d_embed).astype(bf)
        return stacked(
            [sums[:slots]]
            + [rotate(sums[k * slots : (k + 1) * slots], k) for k in range(1, mp)]
        ).T

    def by_column(at_owner):
        placed, wide = [], mp * slots
        for other in range(dp):
            row = ((other & 1) * (dp // 2) + other // 2) * share
            part = at_owner[row : row + share]
            placed.append((swap(part, other) if other else part, 0, other * wide))
        return placed

    def returned(placed):
        return assemble(placed, (share, dp * mp * slots))

    local_targets = (line_targets - start).reshape(-1, 1)

    nonpad = (jnp.arange(length)[None, :] < pad_lengths[:, None]).astype(f32)
    masked = mlm_flags.astype(f32) * nonpad
    lane = jnp.arange(LANES)[None, :]
    counts = jnp.where(lane == 0, jnp.sum(nonpad), jnp.where(lane == 1, jnp.sum(masked), 0.0))
    counts = jnp.where(lane == 2, jnp.max(pair_counts), counts)
    counts = jnp.broadcast_to(counts, (8, LANES))
    bit = 1
    while bit < dp:
        got = swap(counts, bit)
        counts = jnp.where(lane == 2, jnp.maximum(counts, got), counts + got)
        bit *= 2
    count_tok, count_mask = counts[0, 0], jnp.maximum(counts[0, 1], 1.0)
    most = counts[0, 2].astype(jnp.int32)
    rounds = (most + slots - 2) // (slots - 1)

    head_cut = student_project.shape[2]
    unit_cut = student_expand.shape[1]
    cuts = [head_cut] * 4 + [unit_cut] * 2
    units = mp * unit_cut
    vector_rows = student_vectors.shape[0]

    table_parts = gather_start(student_table.T.astype(bf))

    def cut_rows(x, axis):
        return lax.dynamic_slice_in_dim(x, index * share, share, axis)

    s_share = joined(student_project, student_output.T, student_expand, student_reduce.T)
    t_share = joined(
        cut_rows(teacher_project, 1),
        cut_rows(teacher_output, 1).T,
        cut_rows(teacher_expand, 0),
        cut_rows(teacher_reduce, 1).T,
    )
    first_ids = wanted_ids(0)
    both_shares = stacked([t_share, s_share])

    def t_find(ids):
        return jnp.take(teacher_table, jnp.clip(ids[:, 0], 0, vocab_rows - 1), axis=0)

    table_parts, both_shares, first_ids = phase(table_parts, both_shares, first_ids)

    order = order_matrix(features, share)

    def reordered(x, back=False):
        return rows_times(x, order) if back else jnp.dot(x, order, preferred_element_type=f32)

    t_vectors = reordered(teacher_vectors)
    t_position = lax.dynamic_slice_in_dim(teacher_position, own_part * rows, rows, 0)
    t_position = reordered(t_position)
    vector_rows = student_vectors.shape[0]
    small_at = 2 * mp * sum(cuts)
    padded = -(small_at + length + vector_rows) % (2 * LANES)
    s_small = jnp.concatenate(
        [student_position.T, student_vectors.T, jnp.zeros((share, padded), f32)], 1
    ).astype(bf)

    table_parts = gather_rest(table_parts)
    both_shares = gather_mp(both_shares)
    table_parts, both_shares, s_small = phase(table_parts, both_shares, s_small)

    weight_parts = gather_start(by_kind(both_shares, cuts, 2, s_small))
    s_table = gather_end(table_parts)
    t_found = t_find(first_ids)
    s_table, weight_parts, t_found = phase(s_table, weight_parts, t_found)

    weight_parts = gather_rest(weight_parts)
    t_got = sent(t_found)
    s_found = pick_rows(first_ids, s_table)
    weight_parts, s_found, t_got = phase(weight_parts, s_found, t_got)

    classes = gather_end(weight_parts)
    s_got = sent(s_found)
    t_rows = lax.fori_loop(
        1,
        rounds,
        lambda turn, had: had + placed_rows(sent(t_find(wanted_ids(turn))), turn),
        placed_rows(t_got, 0),
    )
    t_embedded = reordered(t_rows.astype(bf)) + t_position
    classes, s_got, t_embedded = phase(classes, s_got, t_embedded)

    all_ids = every_owner(first_ids)

    s_rows = lax.fori_loop(
        1,
        rounds,
        lambda turn, had: had + placed_rows(sent(pick_rows(wanted_ids(turn), s_table)), turn),
        placed_rows(s_got, 0),
    )
    s_small = jnp.concatenate([c[:, small_at:] for c in classes], 0)
    s_vectors = s_small[:, length : length + vector_rows].T.astype(f32)
    s_position = lax.dynamic_slice_in_dim(s_small, own_part * rows, rows, 1).T
    s_embedded = s_rows + s_position.astype(f32)
    t_zero, t_query, t_own = layer_open(t_embedded, t_vectors, classes, 0, units)
    s_zero, s_query, s_own = layer_open(s_embedded, s_vectors, classes, 1, units)
    t_sequence, s_sequence = gather_sequence(t_own, spans), gather_sequence(s_own, spans)
    t_two = layer_close(t_zero, t_query, t_sequence, valid, t_vectors, classes, 0, units)[0]
    t_low = reordered(t_two.astype(bf), True).astype(bf)
    t_low, t_two, s_zero, s_query, s_sequence = phase(t_low, t_two, s_zero, s_query, s_sequence)

    t_parts = gather_mp(t_low)
    s_two, s_attn, s_logs, s_one_pre, s_two_pre = layer_close(
        s_zero, s_query, s_sequence, valid, s_vectors, classes, 1, units
    )
    cos_terms, cos_pull = jax.vjp(lambda x: cosine_loss(x, t_two), s_two)
    own_weight = tok_weight[0]
    (d_cos,) = cos_pull(own_weight / count_tok)
    own_cos = jnp.sum(own_weight * cos_terms)
    split = max(mp // 2, 1)
    t_near = t_parts[:split]
    t_near, s_two, d_cos = phase(t_near, s_two, d_cos)

    s_parts = gather_mp(s_two.astype(bf))
    chunk_groups = [slice(0, split), slice(split, mp)]
    t_first = head_pass(stacked(t_near), teacher_table)
    t_far, t_first = phase(t_parts[split:], t_first)
    t_second = head_pass(stacked(t_far), teacher_table)
    t_second, s_near = phase(t_second, s_parts[:split])
    t_outs, s_outs, s_all = [t_first, t_second], [], []
    for n, group in enumerate(chunk_groups):
        s_all.append(stacked(s_near if n == 0 else s_parts[group]))
        t_half, t_peaks, t_tail = t_outs[n]
        s_outs.append(
            student_pass(
                s_all[n],
                s_table,
                t_half,
                jnp.exp((t_peaks - t_tail[:, 0:1]) * 0.5),
                local_targets[group.start * rows : group.stop * rows],
            )
        )
    t_peaks, t_tail = [jnp.concatenate([x[n] for x in t_outs], 0) for n in (1, 2)]
    s_peaks, s_tail = [jnp.concatenate([x[n] for x in s_outs], 0) for n in (1, 2)]

    mine = jnp.concatenate([t_tail[:, :8], s_tail[:, :8]], 1).T.reshape(16, mp, rows)
    stats = jnp.stack([mine] + [jnp.roll(rotate(mine, by), by, 1) for by in range(1, mp)])
    t_stats, s_stats = stats[:, :8], stats[:, 8:]
    t_peak = jnp.max(t_stats[:, 0], 0)
    t_grow = jnp.exp((t_stats[:, 0] - t_peak) / temper)
    t_half_sum = jnp.sum(t_grow * t_stats[:, 1], 0)
    s_peak = jnp.max(s_stats[:, 0], 0)
    s_grow = jnp.exp((s_stats[:, 0] - s_peak) / temper)
    s_half_sum = jnp.sum(s_grow * s_stats[:, 1], 0)
    s_full_sum = jnp.sum(s_grow * s_grow * s_stats[:, 2], 0)

    apart = jnp.sum(t_grow[:, 0] * (t_stats[:, 3, 0] - s_stats[:, 3, 0]), 0) / temper
    log_half_s = s_peak[0] / temper + jnp.log(s_half_sum[0])
    log_half_t = t_peak[0] / temper + jnp.log(t_half_sum[0])
    log_full = s_peak[0] + jnp.log(s_full_sum[0])
    diverge = temper * temper * (apart / t_half_sum[0] - log_half_t + log_half_s)
    missed = log_full - jnp.sum(s_stats[:, 4, 0], 0)
    own_terms = jnp.stack(
        [
            jnp.sum(own_weight * diverge),
            jnp.sum(mask_weight[0] * missed),
            own_cos,
        ]
    )
    own_terms = jnp.pad(own_terms[None], ((0, 7), (0, LANES - 3)))
    own_terms = own_terms + swap(own_terms, 1)
    line_terms = natural([own_terms] + [rotate(own_terms, by) for by in range(1, mp)])
    seq_terms = jnp.sum(line_terms[:, 0, :3].reshape(2 * batch, spans, 3), 1)
    loss_terms = lax.dynamic_slice_in_dim(seq_terms, core * batch, batch, 0)

    coef_kl = 5.0 * temper * tok_weight / count_tok
    coef_mlm = 2.0 * mask_weight / count_mask

    def by_token(values):
        return values.reshape(-1, 1)

    s_tiles = jnp.exp((s_peaks - by_token(s_peak)) / temper)
    t_tiles = jnp.exp((t_peaks - by_token(t_peak)) / temper)
    back = (
        s_tiles * by_token(coef_kl / s_half_sum),
        t_tiles * by_token(coef_kl / t_half_sum),
        s_tiles * s_tiles * by_token(coef_mlm / s_full_sum),
        by_token(coef_mlm),
        local_targets,
        s_table,
    )
    d_logits, d_sent = [None] * mp, []
    for step in range(mp):
        k = (step + 1) % mp
        n = 0 if k < split else 1
        halves = s_outs[n][0], t_outs[n][0]
        if step >= 3:
            halves, d_sent[step - 3] = phase(halves, d_sent[step - 3])
        d_logits[k], d_row = head_back(k, k - chunk_groups[n].start, rows, *halves, *back)
        if k:
            d_sent.append(rotate(d_row, -k))
    if mp > 2:
        d_logits, d_sent[:-1] = phase(d_logits, d_sent[:-1])
    d_head = d_row.astype(f32)
    for got in d_sent:
        d_head = d_head + got.astype(f32)
    g_head = table_grad(jnp.concatenate([x.T for x in s_all], 1), d_logits)
    d_two = d_head + d_cos
    d_two, g_head = phase(d_two, g_head)

    table_sum = scatter_start(g_head)
    from_units = units_back(d_two, s_two_pre, s_one_pre, s_vectors, classes, 1, units)
    table_sum, from_units = phase(table_sum, from_units)
    d_reduce, active, one_low, d_hidden, d_branch, d_one_pre, d_attn, sums = from_units

    table_sum = scatter_step(table_sum, 0)
    from_attention = attention_back(s_query, s_sequence, d_attn, s_logs, valid)
    table_sum, from_attention, d_reduce, active, one_low, d_hidden = phase(
        table_sum, from_attention, d_reduce, active, one_low, d_hidden
    )

    table_sum = scatter_all(table_sum)
    d_both = scatter_sequence(from_attention[1:], spans).astype(bf)
    g_units = assemble(
        [
            (columns_times(one_low, d_hidden).astype(bf), 0, 0),
            (columns_times(d_reduce, active).astype(bf), 0, units),
        ],
        (features, 2 * units),
    )
    table_sum, d_both, g_units, s_zero = phase(table_sum, d_both, g_units, s_zero)

    units_sum = scatter_start(g_units)
    d_parts = (from_attention[0], d_both[0], d_both[1])
    d_embed, first_sums = embed_back(
        d_parts, d_one_pre, s_embedded, s_vectors, classes, 1, units
    )
    low = s_zero.astype(bf)
    g_heads = [columns_times(low, d).astype(bf) for d in d_parts]
    g_heads.append(columns_times(d_branch, s_attn).astype(bf))
    g_position = lax.dynamic_update_slice_in_dim(
        jnp.zeros((features, length), bf), d_embed.T, own_part * rows, 1
    )
    heads_at = mp * 4 * head_cut
    head_wide = mp * head_cut
    late_padded = -(heads_at + length + vector_rows) % (2 * LANES)
    g_vectors = jnp.pad((sums + first_sums).T.astype(bf), ((0, 0), (0, late_padded)))
    g_late = assemble(
        [(g, 0, t * head_wide) for t, g in enumerate(g_heads)]
        + [(g_position, 0, heads_at), (g_vectors, 0, heads_at + length)],
        (features, heads_at + length + vector_rows + late_padded),
    )
    units_sum, d_embed, g_late = phase(units_sum, d_embed, g_late)

    def by_place(summed, kinds, cut):
        return [
            jnp.concatenate(
                [summed[:, (t * mp + k) * cut : (t * mp + k + 1) * cut] for t in range(kinds)], 1
            )
            for k in range(mp)
        ]

    units_sum = scatter_step(units_sum, 0)
    late_sum = scatter_start(g_late)
    at_owner = at_owners(d_embed, 0)
    units_sum, late_sum, at_owner = phase(units_sum, late_sum, at_owner)

    units_sum = scatter_end(scatter_all(units_sum))
    late_sum = scatter_step(late_sum, 0)
    placed = by_column(at_owner)
    arrived, units_sum, late_sum = phase([x for x, _, _ in placed], units_sum, late_sum)

    late_sum = scatter_end(scatter_all(late_sum))
    own_units = sum_mp(by_place(units_sum, 2, unit_cut))
    e_rows = returned([(x, row, at) for x, (_, row, at) in zip(arrived, placed)])
    own_table = add_rows(scatter_end(table_sum), e_rows, all_ids, 0)
    own_table, own_units, late_sum = phase(own_table, own_units, late_sum)

    small = late_sum[:, heads_at:].astype(bf)
    heads = [x.astype(bf) for x in by_place(late_sum, 4, head_cut)]
    got = [jnp.concatenate([x, small], 1) for x in heads]
    got = got[:1] + [rotate(got[k], -k) for k in range(1, mp)]
    own_table = add_rows(own_table, e_rows, all_ids, 1)
    got, own_table = phase(got, own_table)
    own_heads = sum(x[:, : 4 * head_cut].astype(f32) for x in got)
    got = [got[-k % mp][:, 4 * head_cut :] for k in range(mp)]
    own_small = jnp.sum(natural(got).astype(f32), 0)
    own_table = lax.fori_loop(
        1,
        rounds,
        lambda turn, had: add_rows(
            had,
            returned(by_column(at_owners(d_embed, turn))),
            every_owner(wanted_ids(turn)),
            None,
        ),
        own_table,
    )

    shared_sq = jnp.sum(own_small * own_small) / mp
    squares = (
        jnp.sum(own_table * own_table)
        + jnp.sum(own_units * own_units)
        + jnp.sum(own_heads * own_heads)
        + shared_sq
    )
    squares = sum_all(jnp.broadcast_to(squares, (8, LANES)))[0, 0]
    norm = jnp.sqrt(squares)
    factor = clip_limit / jnp.maximum(norm, clip_limit)

    owned = (
        own_table.T,
        own_small[:, :length].T,
        jnp.stack([own_heads[:, t * head_cut : (t + 1) * head_cut] for t in range(3)]),
        own_heads[:, 3 * head_cut :].T,
        own_units[:, :unit_cut],
        own_units[:, unit_cut:].T,
        own_small[:, length : length + vector_rows].T,
    )
    masters = (
        student_table,
        student_position,
        student_project,
        student_output,
        student_expand,
        student_reduce,
        student_vectors,
    )
    firsts = (
        first_table,
        first_position,
        first_project,
        first_output,
        first_expand,
        first_reduce,
        first_vectors,
    )
    seconds = (
        square_table,
        square_position,
        square_project,
        square_output,
        square_expand,
        square_reduce,
        square_vectors,
    )
    results = []
    for index in range(7):
        rate = rate_vector if index == 6 else rate_table if index == 0 else rate_matrix
        decay = 0.0 if index == 6 else weight_decay
        results += adam_update(
            masters[index], firsts[index], seconds[index], owned[index], factor, rate, decay
        )
    loss_counts = jnp.stack([count_tok, count_mask])
    return (*results, norm, loss_terms, loss_counts)


def solution(mesh):
    in_specs = (
        P("dp", None),
        P("dp", None),
        P("dp"),
        P("dp"),
        P(),
        P("mp", None),
        P(),
        P(None, None, "mp"),
        P("mp", None),
        P(None, "mp"),
        P("mp", None),
        P(),
        P("mp", "dp"),
        P(None, "dp"),
        P(None, "dp", "mp"),
        P("mp", "dp"),
        P("dp", "mp"),
        P("mp", "dp"),
        P(None, "dp"),
        P("mp", "dp"),
        P(None, "dp"),
        P(None, "dp", "mp"),
        P("mp", "dp"),
        P("dp", "mp"),
        P("mp", "dp"),
        P(None, "dp"),
        P("mp", "dp"),
        P(None, "dp"),
        P(None, "dp", "mp"),
        P("mp", "dp"),
        P("dp", "mp"),
        P("mp", "dp"),
        P(None, "dp"),
    )
    out_specs = (
        P("mp", "dp"),
        P("mp", "dp"),
        P("mp", "dp"),
        P(None, "dp"),
        P(None, "dp"),
        P(None, "dp"),
        P(None, "dp", "mp"),
        P(None, "dp", "mp"),
        P(None, "dp", "mp"),
        P("mp", "dp"),
        P("mp", "dp"),
        P("mp", "dp"),
        P("dp", "mp"),
        P("dp", "mp"),
        P("dp", "mp"),
        P("mp", "dp"),
        P("mp", "dp"),
        P("mp", "dp"),
        P(None, "dp"),
        P(None, "dp"),
        P(None, "dp"),
        P(),
        P("dp", None),
        P(),
    )
    return jax.shard_map(body, mesh=mesh, in_specs=in_specs, out_specs=out_specs, check_vma=False)
```

```python
import jax
import jax.numpy as jnp
from jax import lax
from jax.experimental import pallas as pl
from jax.experimental.pallas import tpu as pltpu
from jax.sharding import PartitionSpec as P

HD = 64
STEP = 10
LANES = 128
LOG2E = 1.4426950408889634


eps_norm = 1e-05
mask_token = 103
temper = 2.0
beta_first = 0.9
beta_second = 0.999
adam_eps = 1e-08
rate_table = 0.5
rate_matrix = 0.1
rate_vector = 0.3
weight_decay = 0.01
clip_limit = 1.0
bf = jnp.bfloat16
f32 = jnp.float32
vmem_bytes = 56 * 1024 * 1024


def swap(x, bit):
    count = lax.axis_size("dp")
    return lax.ppermute(x, "dp", [(i, i ^ bit) for i in range(count)])


def rotate(x, by=1):
    count = lax.axis_size("mp")
    return lax.ppermute(x, "mp", [(i, (i + by) % count) for i in range(count)])


def chip_bits():
    count = lax.axis_size("dp")
    bits = []
    bit = 2
    while bit < count:
        bits.append(bit)
        bit *= 2
    return bits


def ordered(bit, mine, other, axis):
    low = (lax.axis_index("dp") & bit) == 0
    return jnp.where(
        low, jnp.concatenate([mine, other], axis), jnp.concatenate([other, mine], axis)
    )


def phase(*arrays):
    return lax.optimization_barrier(arrays)


def gather_start(x):
    half = x.shape[1] // 2
    bits = chip_bits()
    parts = []
    for part, order in ((x[:, :half], bits), (x[:, half:], bits[::-1])):
        pieces = {0: part}
        if order:
            pieces[order[0] // 2] = swap(part, order[0])
        parts.append(pieces)
    return parts


def gather_rest(parts):
    done = []
    bits = chip_bits()
    for pieces, order in zip(parts, (bits[1:], bits[::-1][1:])):
        pieces = dict(pieces)
        for bit in order:
            for chip in list(pieces):
                pieces[chip | (bit // 2)] = swap(pieces[chip], bit)
        done.append(pieces)
    return done


def gather_end(parts):
    placed, width = [], 0
    for pieces in parts:
        rows, columns = pieces[0].shape
        placed += [(piece, chip * rows, width) for chip, piece in pieces.items()]
        width += columns
    mine = assemble(placed, (len(parts[0]) * rows, width))
    return mine, swap(mine, 1)


def scatter_start(y):
    total_rows, columns = y.shape
    count = lax.axis_size("dp")
    half = columns // 2
    state = []
    for part in (y[:, :half], y[:, half:]):
        mine, other = part[: total_rows // 2], part[total_rows // 2 :]
        left = mine.astype(f32) + swap(other.astype(bf), 1).astype(f32)
        state.append(left.reshape(count // 2, total_rows // count, -1))
    return state


def scatter_step(state, step):
    bits = chip_bits()
    if step >= len(bits):
        return state
    after = []
    for which, left in enumerate(state):
        groups, rows, columns = left.shape
        if which == 0:
            bit = bits[::-1][step]
            keep, give = left[: groups // 2], left[groups // 2 :]
        else:
            bit = bits[step]
            split = left.reshape(groups // 2, 2, rows, columns)
            keep, give = split[:, 0], split[:, 1]
        after.append(keep + swap(give.astype(bf), bit).astype(f32))
    return after


def scatter_end(state):
    return jnp.concatenate([left[0] for left in state], 1)


def scatter_all(state):
    for step in range(1, len(chip_bits())):
        state = scatter_step(state, step)
    return state


def order_matrix(features, share):
    count = lax.axis_size("dp")
    at = jnp.arange(features)
    block, inside = at // share, at % share
    other_core, chip = block // (count // 2), block % (count // 2)
    source = (lax.axis_index("dp") ^ (chip * 2 + other_core)) * share + inside
    return (jnp.arange(features)[:, None] == source[None, :]).astype(bf)


def gather_mp(x):
    return [x] + [rotate(x, by) for by in range(1, lax.axis_size("mp"))]


def natural(entries):
    count = lax.axis_size("mp")
    index = lax.axis_index("mp")
    stacked = jnp.stack(entries)
    return jnp.stack(
        [
            lax.dynamic_index_in_dim(stacked, (index - i) % count, 0, keepdims=False)
            for i in range(count)
        ]
    )


def sum_mp(terms):
    total = terms[0].astype(f32)
    for k in range(1, len(terms)):
        total = total + rotate(terms[k].astype(bf), -k).astype(f32)
    return total


def sum_all(x):
    bit = 1
    while bit < lax.axis_size("dp"):
        x = x + swap(x, bit)
        bit *= 2
    count = lax.axis_size("mp")
    bit = 1
    while bit < count:
        x = x + lax.ppermute(x, "mp", [(i, i ^ bit) for i in range(count)])
        bit *= 2
    return x


def tile_of(total, cap):
    best = LANES
    for size in range(LANES, min(total, cap) + 1, LANES):
        if total % size == 0:
            best = size
    return best


def call(body, grid, in_specs, out_specs, out_shape, scratch, flops, moved):
    return pl.pallas_call(
        body,
        grid=grid,
        in_specs=in_specs,
        out_specs=out_specs,
        out_shape=out_shape,
        scratch_shapes=scratch,
        compiler_params=pltpu.CompilerParams(
            dimension_semantics=("arbitrary",) * len(grid), vmem_limit_bytes=vmem_bytes
        ),
        cost_estimate=pl.CostEstimate(flops=flops, bytes_accessed=moved, transcendentals=0),
    )


def assemble(placed, shape):
    kind = placed[0][0].dtype
    if any(at % LANES or x.shape[1] % LANES or x.shape[0] % 16 for x, _, at in placed):
        out = jnp.zeros(shape, kind)
        for x, row, at in placed:
            out = lax.dynamic_update_slice(out, x, (row, at))
        return out
    count = len(placed)

    def body(*refs):
        ins, out, sems = refs[:count], refs[count], refs[count + 1]
        copies = []
        for n, (x, row, at) in enumerate(placed):
            high, wide = x.shape
            copies.append(
                pltpu.make_async_copy(
                    ins[n], out.at[row : row + high, at : at + wide], sems.at[n]
                )
            )
        for copy in copies:
            copy.start()
        for copy in copies:
            copy.wait()

    moved = 2 * sum(x.size * x.dtype.itemsize for x, _, _ in placed)
    return pl.pallas_call(
        body,
        in_specs=[pl.BlockSpec(memory_space=pl.ANY)] * count,
        out_specs=pl.BlockSpec(memory_space=pltpu.VMEM),
        out_shape=jax.ShapeDtypeStruct(shape, kind),
        scratch_shapes=[pltpu.SemaphoreType.DMA((count,))],
        compiler_params=pltpu.CompilerParams(vmem_limit_bytes=vmem_bytes),
        cost_estimate=pl.CostEstimate(flops=0, bytes_accessed=moved, transcendentals=0),
    )(*[x for x, _, _ in placed])


def stacked(arrays):
    placed, row = [], 0
    for x in arrays:
        placed.append((x, row, 0))
        row += x.shape[0]
    return assemble(placed, (row, arrays[0].shape[1]))


def joined(project, output_t, expand, reduce_t):
    rows = expand.shape[0]
    parts = [project.shape[2]] * 3 + [x.shape[1] for x in (output_t, expand, reduce_t)]
    if any(part % LANES for part in parts):
        return jnp.concatenate(
            [x.astype(bf) for x in (*project, output_t, expand, reduce_t)], 1
        )

    def body(project_ref, output_ref, expand_ref, reduce_ref, out_ref):
        at = 0
        for value in (
            project_ref[0], project_ref[1], project_ref[2], output_ref[...], expand_ref[...],
            reduce_ref[...],
        ):
            out_ref[:, at : at + value.shape[1]] = value.astype(bf)
            at += value.shape[1]

    shape = (rows, sum(parts))
    return call(
        body,
        (1,),
        [whole(x.shape) for x in (project, output_t, expand, reduce_t)],
        whole(shape),
        jax.ShapeDtypeStruct(shape, bf),
        [],
        0,
        6 * shape[0] * shape[1],
    )(project, output_t, expand, reduce_t)


def by_kind(shares, cuts, models, tail):
    rows = shares[0].shape[0] // models
    placed, to = [], 0
    for model in range(models):
        at = 0
        for cut in cuts:
            for n in range(len(shares)):
                placed.append((n, model, at, cut, to))
                to += cut
            at += cut
    if any(cut % LANES for cut in cuts):
        return jnp.concatenate(
            [
                shares[n][model * rows : (model + 1) * rows, at : at + cut]
                for n, model, at, cut, _ in placed
            ]
            + [tail],
            1,
        )
    count = len(shares)

    def body(*refs):
        out_ref = refs[-1]
        for n, model, at, cut, into in placed:
            part = slice(model * rows, (model + 1) * rows)
            out_ref[:, into : into + cut] = refs[n][part, at : at + cut]
        out_ref[:, to:] = refs[count][...]

    shape = (rows, to + tail.shape[1])
    return call(
        body,
        (1,),
        [whole(x.shape) for x in (*shares, tail)],
        whole(shape),
        jax.ShapeDtypeStruct(shape, bf),
        [],
        0,
        4 * shape[0] * shape[1],
    )(*shares, tail)


def whole(shape):
    return pl.BlockSpec(shape, lambda *_: (0,) * len(shape))


def onto(x, tables):
    total, at = None, 0
    for table in tables:
        wide = table.shape[0]
        term = jnp.dot(x[:, at : at + wide], table, preferred_element_type=f32)
        total = term if total is None else total + term
        at += wide
    return total


def rows_times(x, flipped):
    return lax.dot_general(x, flipped, (((1,), (1,)), ((), ())), preferred_element_type=f32)


def pick_rows(ids, tables):
    half, vocab = tables[0].shape
    width = half * len(tables)
    tile = tile_of(vocab, 1536)
    rows = ids.shape[0]

    def body(ids_ref, *refs):
        table_refs, (out_ref, total) = refs[: len(tables)], refs[len(tables) :]
        j = pl.program_id(0)

        @pl.when(j == 0)
        def _():
            total[...] = jnp.zeros_like(total)

        lane = lax.broadcasted_iota(jnp.int32, (rows, tile), 1)
        hot = jnp.where(lane == ids_ref[...] - j * tile, 1.0, 0.0).astype(bf)
        for t, table_ref in enumerate(table_refs):
            total[:, t * half : (t + 1) * half] += rows_times(hot, table_ref[...])

        @pl.when(j == pl.num_programs(0) - 1)
        def _():
            out_ref[...] = total[...].astype(bf)

    return call(
        body,
        (vocab // tile,),
        [whole((rows, 1))] + [pl.BlockSpec((half, tile), lambda j: (0, j))] * len(tables),
        whole((rows, width)),
        jax.ShapeDtypeStruct((rows, width), bf),
        [pltpu.VMEM((rows, width), f32)],
        2 * rows * width * vocab,
        2 * width * vocab,
    )(ids, *tables)


def lane_value(values, j):
    lane = lax.broadcasted_iota(jnp.int32, values.shape, 1)
    return jnp.sum(jnp.where(lane == j, values, 0.0), 1, keepdims=True)


def head_tile(vocab):
    return tile_of(vocab, 1536)


def head_pass(x, table):
    vocab, width = table.shape
    rows = x.shape[0]
    tile = head_tile(vocab)
    step = min(rows, 256)
    fold = range(0, tile, LANES)

    def body(x_ref, table_ref, half_ref, peaks_ref, stats_ref):
        j = pl.program_id(0)

        @pl.when(j == 0)
        def _():
            lane = lax.broadcasted_iota(jnp.int32, stats_ref.shape, 1)
            stats_ref[...] = jnp.where(lane == 0, -1e30, 0.0)
            peaks_ref[...] = jnp.zeros_like(peaks_ref)

        for b in range(rows // step):
            part = pl.ds(b * step, step)
            z = rows_times(x_ref[part, :], table_ref[...])
            before = stats_ref[part, :]
            highest = z[:, :LANES]
            for at in fold[1:]:
                highest = jnp.maximum(highest, z[:, at : at + LANES])
            peak = jnp.maximum(before[:, 0:1], jnp.max(highest, 1, keepdims=True))
            shrink = jnp.exp((before[:, 0:1] - peak) * 0.5)
            lane = lax.broadcasted_iota(jnp.int32, (step, LANES), 1)
            half_sum, cross = jnp.zeros((step, LANES), f32), jnp.zeros((step, LANES), f32)
            for at in fold:
                piece = z[:, at : at + LANES]
                half = jnp.exp2((piece - peak) * (0.5 * LOG2E))
                half_ref[part, at : at + LANES] = half.astype(bf)
                half_sum += half
                cross += half * piece
            half_sum = before[:, 1:2] * shrink + jnp.sum(half_sum, 1, keepdims=True)
            cross = before[:, 3:4] * shrink + jnp.sum(cross, 1, keepdims=True)
            after = jnp.where(lane == 0, peak, before)
            after = jnp.where(lane == 1, half_sum, after)
            stats_ref[part, :] = jnp.where(lane == 3, cross, after)
            peaks_ref[part, :] = jnp.where(lane == j, peak, peaks_ref[part, :])

    lanes = whole((rows, LANES))
    stat = jax.ShapeDtypeStruct((rows, LANES), f32)
    return call(
        body,
        (vocab // tile,),
        [whole((rows, width)), pl.BlockSpec((tile, width), lambda j: (j, 0))],
        [pl.BlockSpec((rows, tile), lambda j: (0, j)), lanes, lanes],
        [jax.ShapeDtypeStruct((rows, vocab), bf), stat, stat],
        [],
        2 * rows * width * vocab,
        2 * width * vocab + 2 * rows * vocab,
    )(x, table)


def student_pass(x, tables, other, weight, targets):
    half_width, vocab = tables[0].shape
    rows, width = x.shape
    tile = head_tile(vocab)
    step = min(rows, 256)
    block_wide = 256 if tile % 256 == 0 else LANES
    count = len(tables)

    def body(x_ref, *refs):
        table_refs, refs = refs[:count], refs[count:]
        other_ref, weight_ref, target_ref, half_ref, peaks_ref, stats_ref = refs[:6]
        table, peak_ref, high_ref, *sums = refs[6:]
        new, total = sums[:4], sums[4:]
        j = pl.program_id(0)
        for t, table_ref in enumerate(table_refs):
            table[t * half_width : (t + 1) * half_width, :] = table_ref[...]

        def over_rows(work):
            @pl.loop(0, rows // step)
            def _(b):
                work(pl.ds(pl.multiple_of(b * step, step), step))

        @pl.when(j == 0)
        def _():
            peaks_ref[...] = jnp.zeros_like(peaks_ref)
            for ref in total:
                ref[...] = jnp.zeros_like(ref)

            def begin(part):
                z = jnp.dot(x_ref[part, :], table[:, :LANES], preferred_element_type=f32)
                top = jnp.broadcast_to(jnp.max(z, 1, keepdims=True), z.shape)
                peak_ref[part, :] = top
                high_ref[part, :] = top

            over_rows(begin)

        def digest(part):
            lane = lax.broadcasted_iota(jnp.int32, (step, LANES), 1)
            peak, high = peak_ref[part, :], high_ref[part, :]
            values = [jnp.zeros((step, LANES), f32) for _ in range(4)]
            target = jnp.broadcast_to(target_ref[part, :] - j * tile, (step, LANES)) - lane
            for first in range(0, tile, block_wide):
                z = jnp.dot(
                    x_ref[part, :],
                    table[:, first : first + block_wide],
                    preferred_element_type=f32,
                )
                for inner in range(0, block_wide, LANES):
                    at = first + inner
                    piece = z[:, inner : inner + LANES]
                    half = jnp.exp2((piece - peak) * (0.5 * LOG2E))
                    half_ref[part, at : at + LANES] = half.astype(bf)
                    high = jnp.maximum(high, piece)
                    values[0] += half
                    values[1] += half * half
                    values[2] += other_ref[part, at : at + LANES].astype(f32) * piece
                    values[3] += jnp.where(target == at, piece, 0.0)
            for ref, value in zip(new, values):
                ref[part, :] = value
            high_ref[part, :] = high

        pairs = 2 if rows // step % 2 == 0 else 1

        @pl.loop(0, rows // step // pairs)
        def _(b):
            for n in range(pairs):
                digest(pl.ds(pl.multiple_of((b * pairs + n) * step, step), step))

        def top_of(part):
            return jnp.broadcast_to(
                jnp.max(high_ref[part, :], 1, keepdims=True), (step, LANES)
            )

        @pl.when(jnp.max(high_ref[...] - peak_ref[...]) > 60.0)
        def _():
            def raise_peak(part):
                before, top = peak_ref[part, :], top_of(part)
                shrink = jnp.exp((before - top) * 0.5)
                total[0][part, :] *= shrink
                total[1][part, :] *= shrink * shrink
                peak_ref[part, :] = top

            over_rows(raise_peak)
            over_rows(digest)

        def settle(part):
            lane = lax.broadcasted_iota(jnp.int32, (step, LANES), 1)
            before, top = peak_ref[part, :], top_of(part)
            shrink = jnp.exp((before - top) * 0.5)
            weight_now = jnp.broadcast_to(lane_value(weight_ref[part, :], j), (step, LANES))
            total[0][part, :] = (total[0][part, :] + new[0][part, :]) * shrink
            total[1][part, :] = (total[1][part, :] + new[1][part, :]) * (shrink * shrink)
            total[2][part, :] += new[2][part, :] * weight_now
            total[3][part, :] += new[3][part, :]
            peaks_ref[part, :] = jnp.where(lane == j, before, peaks_ref[part, :])
            peak_ref[part, :] = top

            @pl.when(j == pl.num_programs(0) - 1)
            def _():
                out = jnp.where(lane == 0, top, 0.0)
                for n, ref in enumerate(total):
                    out = jnp.where(lane == n + 1, jnp.sum(ref[part, :], 1, keepdims=True), out)
                stats_ref[part, :] = out

        over_rows(settle)

    block = pl.BlockSpec((rows, tile), lambda j: (0, j))
    lanes = whole((rows, LANES))
    stat = jax.ShapeDtypeStruct((rows, LANES), f32)
    return call(
        body,
        (vocab // tile,),
        [whole((rows, width))]
        + [pl.BlockSpec((half_width, tile), lambda j: (0, j))] * count
        + [block, lanes, whole((rows, 1))],
        [block, lanes, lanes],
        [jax.ShapeDtypeStruct((rows, vocab), bf), stat, stat],
        [pltpu.VMEM((width, tile), bf)] + [pltpu.VMEM((rows, LANES), f32)] * 10,
        2 * rows * width * vocab,
        2 * width * vocab + 4 * rows * vocab,
    )(x, *tables, other, weight, targets)


def head_back(k, k_half, rows, s_half, t_half, s_scale, t_scale, f_scale, hit_scale, targets, tables):
    part_width, vocab = tables[0].shape
    width = part_width * len(tables)
    tile = head_tile(vocab)
    step = min(rows, 256)

    def body(s_ref, t_ref, a_ref, b_ref, c_ref, h_ref, target_ref, *refs):
        table_refs, (d_ref, out_ref, total) = refs[: len(tables)], refs[len(tables) :]
        j = pl.program_id(0)

        @pl.when(j == 0)
        def _():
            total[...] = jnp.zeros_like(total)

        for begin in range(0, rows, step):
            part = pl.ds(begin, step)
            a = jnp.broadcast_to(lane_value(a_ref[part, :], j), (step, LANES))
            b = jnp.broadcast_to(lane_value(b_ref[part, :], j), (step, LANES))
            c = jnp.broadcast_to(lane_value(c_ref[part, :], j), (step, LANES))
            h = jnp.broadcast_to(h_ref[part, :], (step, LANES))
            target = jnp.broadcast_to(target_ref[part, :] - j * tile, (step, LANES))
            lane = lax.broadcasted_iota(jnp.int32, (step, LANES), 1)
            for at in range(0, tile, LANES):
                half = s_ref[part, at : at + LANES].astype(f32)
                grad = half * (a + half * c) - t_ref[part, at : at + LANES].astype(f32) * b
                grad -= jnp.where(lane == target - at, h, 0.0)
                d_ref[part, at : at + LANES] = grad.astype(bf)
            for t, table_ref in enumerate(table_refs):
                total[part, t * part_width : (t + 1) * part_width] += rows_times(
                    d_ref[part, :], table_ref[...]
                )

        @pl.when(j == pl.num_programs(0) - 1)
        def _():
            out_ref[...] = total[...].astype(bf)

    block = pl.BlockSpec((rows, tile), lambda j: (k_half, j))
    lanes = pl.BlockSpec((rows, LANES), lambda j: (k, 0))
    column = pl.BlockSpec((rows, 1), lambda j: (k, 0))
    return call(
        body,
        (vocab // tile,),
        [block, block, lanes, lanes, lanes, column, column]
        + [pl.BlockSpec((part_width, tile), lambda j: (0, j))] * len(tables),
        [pl.BlockSpec((rows, tile), lambda j: (0, j)), whole((rows, width))],
        [jax.ShapeDtypeStruct((rows, vocab), bf), jax.ShapeDtypeStruct((rows, width), bf)],
        [pltpu.VMEM((rows, width), f32)],
        2 * rows * width * vocab,
        2 * width * vocab + 6 * rows * vocab,
    )(s_half, t_half, s_scale, t_scale, f_scale, hit_scale, targets, *tables)


def table_grad(x_flipped, d_logits):
    width = x_flipped.shape[0]
    rows, vocab = d_logits[0].shape
    tile = tile_of(vocab, 1536)
    count = len(d_logits)

    def body(x_ref, *refs):
        total = None
        for k, d_ref in enumerate(refs[:-1]):
            term = jnp.dot(
                x_ref[:, k * rows : (k + 1) * rows], d_ref[...], preferred_element_type=f32
            )
            total = term if total is None else total + term
        refs[-1][...] = total.astype(bf)

    return call(
        body,
        (vocab // tile,),
        [whole((width, rows * count))] + [pl.BlockSpec((rows, tile), lambda j: (0, j))] * count,
        pl.BlockSpec((width, tile), lambda j: (0, j)),
        jax.ShapeDtypeStruct((width, vocab), bf),
        [],
        2 * rows * count * width * vocab,
        2 * rows * count * vocab + 4 * width * vocab,
    )(x_flipped, *d_logits)


def add_rows(base, e_flipped, ids, half):
    width, vocab = base.shape
    rows = ids.shape[0]
    tile = tile_of(vocab, 768)
    step = tile_of(rows, 512)
    tiles = vocab // tile
    first, count = 0, tiles
    if half is not None:
        first, count = (0, tiles // 2) if half == 0 else (tiles // 2, tiles - tiles // 2)

    def body(base_ref, e_ref, ids_ref, out_ref):
        j = pl.program_id(0) + first
        lane = lax.broadcasted_iota(jnp.int32, (step, tile), 1)
        total = base_ref[...]
        for begin in range(0, rows, step):
            part = slice(begin, begin + step)
            hot = jnp.where(lane == ids_ref[part, :] - j * tile, 1.0, 0.0).astype(bf)
            total += jnp.dot(e_ref[:, part], hot, preferred_element_type=f32)
        out_ref[...] = total

    block = pl.BlockSpec((width, tile), lambda j: (0, j + first))
    return pl.pallas_call(
        body,
        grid=(count,),
        in_specs=[block, whole((width, rows)), whole((rows, 1))],
        out_specs=block,
        out_shape=jax.ShapeDtypeStruct((width, vocab), f32),
        input_output_aliases={0: 0},
        compiler_params=pltpu.CompilerParams(
            dimension_semantics=("arbitrary",), vmem_limit_bytes=vmem_bytes
        ),
        cost_estimate=pl.CostEstimate(
            flops=2 * rows * width * vocab, bytes_accessed=8 * width * vocab, transcendentals=0
        ),
    )(base, e_flipped, ids)


def heads_reordered(x):
    count = lax.axis_size("mp")
    return jnp.concatenate(list(natural(jnp.split(x, count, -1))), -1)


def gather_sequence(x, spans):
    parts = [x, swap(x, 1)]
    if spans > 1:
        count = lax.axis_size("mp")
        groups = [list(range(i, i + spans)) for i in range(0, count, spans)]
        both = heads_reordered(jnp.concatenate(parts, 1))
        both = lax.all_gather(both, "mp", axis=1, axis_index_groups=groups, tiled=True)
        parts = [heads_reordered(both)]
    return parts


def scatter_sequence(parts, spans):
    if spans > 1:
        count = lax.axis_size("mp")
        groups = [list(range(i, i + spans)) for i in range(0, count, spans)]
        x = lax.psum_scatter(
            heads_reordered(parts[0].astype(f32)),
            "mp",
            scatter_dimension=1,
            axis_index_groups=groups,
            tiled=True,
        )
        parts = jnp.split(heads_reordered(x), 2, 1)
    return parts[0].astype(f32) + swap(parts[1].astype(bf), 1).astype(f32)


def sequence_parts(core, spans):
    if spans == 1:
        return [core, 1 - core]
    return [chip * 2 + side for chip in range(spans) for side in (core, 1 - core)]


def norm_parts(x):
    centre = x - jnp.mean(x, -1, keepdims=True)
    spread = jnp.mean(centre * centre, -1, keepdims=True)
    scale = lax.rsqrt(spread + eps_norm)
    return centre * scale, scale


def norm_back(unit, scale, gain, grad):
    inner = grad * gain
    slope = inner - jnp.mean(inner, -1, keepdims=True)
    slope = (slope - unit * jnp.mean(inner * unit, -1, keepdims=True)) * scale
    return slope, jnp.sum(grad * unit, 0, keepdims=True), jnp.sum(grad, 0, keepdims=True)


def resident(shape):
    return pl.BlockSpec(shape, lambda *_: (0,) * len(shape), pipeline_mode=pl.Buffered(1))


def put_rows(ref, j, values):
    row = lax.broadcasted_iota(jnp.int32, ref.shape, 0)
    add = jnp.zeros(ref.shape, f32)
    for at, value in values.items():
        add = jnp.where(row == at, value, add)

    @pl.when(j == 0)
    def _():
        ref[...] = add

    @pl.when(j > 0)
    def _():
        ref[...] += add


def weight_blocks(classes, model, features, units, opening):
    columns = 4 * features + 2 * units
    wide = 3 * features if opening and columns % (3 * features) == 0 else columns
    return [
        pl.BlockSpec(
            (c.shape[0], wide),
            lambda *_: (0, model * columns // wide),
            pipeline_mode=pl.Buffered(1),
        )
        for c in classes
    ]


def columns_of(features, units):
    cuts, at = [], 0
    for wide in [features] * 4 + [units] * 2:
        cuts.append(slice(at, at + wide))
        at += wide
    return cuts


def side_by_side(x, classes, cut):
    return jnp.concatenate([rows_times(x, c[:, cut]) for c in classes], 1)


def through(x, classes, cut):
    high = classes[0].shape[0]
    total = None
    for t, c in enumerate(classes):
        term = jnp.dot(x[:, t * high : (t + 1) * high], c[:, cut], preferred_element_type=f32)
        total = term if total is None else total + term
    return total


def layer_open(embedded, vectors, classes, model, units):
    rows, features = embedded.shape
    cuts = columns_of(features, units)
    step = min(rows, 256)
    count = len(classes)

    def body(x_ref, vectors_ref, *refs):
        class_refs, (zero_ref, q_ref, kv_ref) = refs[:count], refs[count:]
        unit, _ = norm_parts(x_ref[...])
        zero = unit * vectors_ref[0:1, :] + vectors_ref[1:2, :]
        zero_ref[...] = zero
        low = zero.astype(bf)
        q_ref[...] = through(low, class_refs, cuts[0]).astype(bf)
        kv_ref[0] = through(low, class_refs, cuts[1]).astype(bf)
        kv_ref[1] = through(low, class_refs, cuts[2]).astype(bf)

    block = pl.BlockSpec((step, features), lambda j: (j, 0))
    return call(
        body,
        (rows // step,),
        [block, whole(vectors.shape)] + weight_blocks(classes, model, features, units, True),
        [block, block, pl.BlockSpec((2, step, features), lambda j: (0, j, 0))],
        [
            jax.ShapeDtypeStruct((rows, features), f32),
            jax.ShapeDtypeStruct((rows, features), bf),
            jax.ShapeDtypeStruct((2, rows, features), bf),
        ],
        [],
        6 * rows * features * features,
        6 * features * features + 16 * rows * features,
    )(embedded, vectors, *classes)


def head_lanes(shape, which):
    return (lax.broadcasted_iota(jnp.int32, shape, 1) // HD) == which


def layer_close(zero, query, parts, valid, vectors, classes, model, units):
    rows, features = zero.shape
    length = valid.shape[1]
    cells = len(parts)
    cuts = columns_of(features, units)
    step = min(rows, 256)
    count = len(classes)
    pair = LANES // HD

    def body(zero_ref, q_ref, valid_ref, vectors_ref, *refs):
        part_refs, class_refs, refs = refs[:cells], refs[cells : cells + count], refs[cells + count :]
        two_ref, attn_ref, log_ref, one_pre_ref, two_pre_ref = refs
        allowed = valid_ref[...] > 0.0
        log_lane = lax.broadcasted_iota(jnp.int32, (step, LANES), 1)
        logs = jnp.zeros((step, LANES), f32)
        pieces = []
        for block in range(features // LANES):
            lanes = slice(block * LANES, (block + 1) * LANES)
            keys = jnp.concatenate([ref[0, :, lanes] for ref in part_refs], 0)
            values = jnp.concatenate([ref[1, :, lanes] for ref in part_refs], 0)
            merged = jnp.zeros((step, LANES), f32)
            for which in range(pair):
                mine = head_lanes((step, LANES), which)
                q = jnp.where(mine, q_ref[:, lanes] * HD ** (-0.5), 0.0).astype(bf)
                score = jnp.where(allowed, rows_times(q, keys), -1e30)
                peak = jnp.max(score, 1, keepdims=True)
                expo = jnp.exp(score - peak)
                total = jnp.sum(expo, 1, keepdims=True)
                weight = (expo * (1.0 / total)).astype(bf)
                merged = jnp.where(
                    mine, jnp.dot(weight, values, preferred_element_type=f32), merged
                )
                logs = jnp.where(log_lane == block * pair + which, peak + jnp.log(total), logs)
            pieces.append(merged)
        log_ref[...] = logs
        attn = jnp.concatenate(pieces, 1).astype(bf)
        attn_ref[...] = attn
        one_pre = side_by_side(attn, class_refs, cuts[3]) + vectors_ref[2:3, :] + zero_ref[...]
        one_pre_ref[...] = one_pre
        one = norm_parts(one_pre)[0] * vectors_ref[3:4, :] + vectors_ref[4:5, :]
        hidden = through(one.astype(bf), class_refs, cuts[4])
        active = gelu(hidden).astype(bf)
        two_pre = side_by_side(active, class_refs, cuts[5]) + vectors_ref[5:6, :] + one
        two_pre_ref[...] = two_pre
        two_ref[...] = norm_parts(two_pre)[0] * vectors_ref[6:7, :] + vectors_ref[7:8, :]

    block = pl.BlockSpec((step, features), lambda j: (j, 0))
    wide = jax.ShapeDtypeStruct((rows, features), f32)
    columns = cuts[-1].stop
    return call(
        body,
        (rows // step,),
        [block, block, whole(valid.shape), whole(vectors.shape)]
        + [resident(x.shape) for x in parts]
        + weight_blocks(classes, model, features, units, False),
        [block, block, pl.BlockSpec((step, LANES), lambda j: (j, 0)), block, block],
        [
            wide,
            jax.ShapeDtypeStruct((rows, features), bf),
            jax.ShapeDtypeStruct((rows, LANES), f32),
            wide,
            wide,
        ],
        [],
        2 * rows * features * (2 * length + features + 2 * units),
        2 * features * columns + 20 * rows * features,
    )(zero, query, valid, vectors, *parts, *classes)


def gelu(x):
    return 0.5 * x * (1.0 + lax.erf(x * 0.7071067811865476))


def gelu_slope(x):
    return 0.5 * (1.0 + lax.erf(x * 0.7071067811865476)) + x * 0.3989422804014327 * jnp.exp(
        -0.5 * x * x
    )


def units_back(d_two, two_pre, one_pre, vectors, classes, model, units):
    rows, features = d_two.shape
    cuts = columns_of(features, units)
    step = min(rows, 256)
    count = len(classes)

    def body(d_ref, two_pre_ref, one_pre_ref, vectors_ref, *refs):
        class_refs, refs = refs[:count], refs[count:]
        reduce_ref, active_ref, low_ref, hidden_ref, branch_ref, pre_ref, attn_ref, sums_ref = refs
        unit, scale = norm_parts(two_pre_ref[...])
        d_two_pre, gain_two, shift_two = norm_back(unit, scale, vectors_ref[6:7, :], d_ref[...])
        low = d_two_pre.astype(bf)
        reduce_ref[...] = low
        d_active = through(low, class_refs, cuts[5])
        unit, scale = norm_parts(one_pre_ref[...])
        one_low = (unit * vectors_ref[3:4, :] + vectors_ref[4:5, :]).astype(bf)
        low_ref[...] = one_low
        hidden = through(one_low, class_refs, cuts[4])
        bell = 0.5 * (1.0 + lax.erf(hidden * 0.7071067811865476))
        active_ref[...] = (hidden * bell).astype(bf)
        slope = bell + hidden * 0.3989422804014327 * jnp.exp(-0.5 * hidden * hidden)
        d_hidden = (d_active * slope).astype(bf)
        hidden_ref[...] = d_hidden
        d_one = side_by_side(d_hidden, class_refs, cuts[4]) + d_two_pre
        d_one_pre, gain_one, shift_one = norm_back(unit, scale, vectors_ref[3:4, :], d_one)
        pre_ref[...] = d_one_pre
        d_branch = d_one_pre.astype(bf)
        branch_ref[...] = d_branch
        attn_ref[...] = through(d_branch, class_refs, cuts[3]).astype(bf)
        put_rows(
            sums_ref,
            pl.program_id(0),
            {
                2: jnp.sum(d_one_pre, 0, keepdims=True),
                3: gain_one,
                4: shift_one,
                5: jnp.sum(d_two_pre, 0, keepdims=True),
                6: gain_two,
                7: shift_two,
            },
        )

    block = pl.BlockSpec((step, features), lambda j: (j, 0))
    broad = pl.BlockSpec((step, units), lambda j: (j, 0))
    columns = cuts[-1].stop
    low = jax.ShapeDtypeStruct((rows, features), bf)
    full = jax.ShapeDtypeStruct((rows, features), f32)
    high = jax.ShapeDtypeStruct((rows, units), bf)
    return call(
        body,
        (rows // step,),
        [block, block, block, whole(vectors.shape)]
        + weight_blocks(classes, model, features, units, False),
        [block, broad, block, broad, block, block, block, whole((8, features))],
        [low, high, low, high, low, full, low, jax.ShapeDtypeStruct((8, features), f32)],
        [],
        2 * rows * features * (features + 3 * units),
        2 * features * columns + 20 * rows * features + 4 * rows * units,
    )(d_two, two_pre, one_pre, vectors, *classes)


def columns_times(left, right):
    return lax.dot_general(left, right, (((0,), (0,)), ((), ())), preferred_element_type=f32)


def attention_back(query, parts, d_attn, logs, valid):
    rows, features = query.shape
    length = valid.shape[1]
    cells = len(parts)
    pair = LANES // HD

    def body(q_ref, d_ref, log_ref, valid_ref, *refs):
        part_refs, dq_ref, d_refs = refs[:cells], refs[cells], refs[cells + 1 :]
        j = pl.program_id(0)
        d_parts = [[None, None] for _ in range(cells)]
        allowed = valid_ref[...] > 0.0
        keys = jnp.concatenate([ref[0] for ref in part_refs], 0)
        values = jnp.concatenate([ref[1] for ref in part_refs], 0)
        merged = jnp.zeros((rows, LANES), f32)
        for which in range(pair):
            mine = head_lanes((rows, LANES), which)
            q = jnp.where(mine, q_ref[...] * HD ** (-0.5), 0.0).astype(bf)
            d = jnp.where(mine, d_ref[...], 0.0).astype(bf)
            log_total = lane_value(log_ref[...], j * pair + which)
            score = jnp.where(allowed, rows_times(q, keys), -1e30)
            weight = jnp.exp(score - log_total)
            slope = rows_times(d, values)
            low = weight.astype(bf)
            inner = jnp.sum(weight * slope, 1, keepdims=True)
            d_score = (weight * (slope - inner)).astype(bf)
            merged = jnp.where(
                mine, jnp.dot(d_score, keys, preferred_element_type=f32), merged
            )
            at = 0
            for cell, ref in enumerate(part_refs):
                here = slice(at, at + ref.shape[1])
                at = here.stop
                for slot, (left, right) in enumerate(((d_score, q), (low, d))):
                    term = columns_times(left[:, here], right)
                    had = d_parts[cell][slot]
                    d_parts[cell][slot] = term if had is None else had + term
        dq_ref[...] = (merged * HD ** (-0.5)).astype(bf)
        for ref, pieces in zip(d_refs, d_parts):
            for slot, piece in enumerate(pieces):
                ref[slot] = piece.astype(ref.dtype)

    block = pl.BlockSpec((rows, LANES), lambda j: (0, j))
    tall = [pl.BlockSpec((2, x.shape[1], LANES), lambda j: (0, 0, j)) for x in parts]
    return call(
        body,
        (features // LANES,),
        [block, block, whole(logs.shape), whole(valid.shape)] + tall,
        [block] + tall,
        [jax.ShapeDtypeStruct((rows, features), bf)]
        + [jax.ShapeDtypeStruct(x.shape, f32 if n == 0 else bf) for n, x in enumerate(parts)],
        [],
        10 * rows * features * length,
        16 * length * features,
    )(query, d_attn, logs, valid, *parts)


def embed_back(d_parts, d_one_pre, embedded, vectors, classes, model, units):
    rows, features = d_one_pre.shape
    cuts = columns_of(features, units)
    step = min(rows, 256)
    count = len(classes)

    def body(q_ref, k_ref, v_ref, pre_ref, x_ref, vectors_ref, *refs):
        class_refs, (out_ref, sums_ref) = refs[:count], refs[count:]
        d_zero = pre_ref[...]
        for t, part in enumerate((q_ref, k_ref, v_ref)):
            d_zero += side_by_side(part[...], class_refs, cuts[t])
        unit, scale = norm_parts(x_ref[...])
        d_embed, gain, shift = norm_back(unit, scale, vectors_ref[0:1, :], d_zero)
        out_ref[...] = d_embed.astype(bf)
        put_rows(sums_ref, pl.program_id(0), {0: gain, 1: shift})

    block = pl.BlockSpec((step, features), lambda j: (j, 0))
    return call(
        body,
        (rows // step,),
        [block] * 5
        + [whole(vectors.shape)]
        + weight_blocks(classes, model, features, units, True),
        [block, whole((8, features))],
        [
            jax.ShapeDtypeStruct((rows, features), bf),
            jax.ShapeDtypeStruct((8, features), f32),
        ],
        [],
        6 * rows * features * features,
        6 * features * features + 16 * rows * features,
    )(*d_parts, d_one_pre, embedded, vectors, *classes)


def cosine_loss(x_student, x_teacher):
    s_len = jnp.sqrt(jnp.sum(x_student * x_student, -1))
    t_len = jnp.sqrt(jnp.sum(x_teacher * x_teacher, -1))
    return 1.0 - jnp.sum(x_student * x_teacher, -1) / (s_len * t_len)


def adam_update(master, first, square, grad, factor, rate, decay):
    clipped = grad * factor
    new_first = beta_first * first + (1.0 - beta_first) * clipped
    new_square = beta_second * square + (1.0 - beta_second) * clipped * clipped
    first_hat = new_first / (1.0 - beta_first**STEP)
    square_hat = new_square / (1.0 - beta_second**STEP)
    updated = master - rate * (first_hat / (jnp.sqrt(square_hat) + adam_eps) + decay * master)
    return [updated, new_first, new_square]


def body(
    token_ids,
    mlm_flags,
    pad_lengths,
    group_ids,
    group_weight,
    teacher_table,
    teacher_position,
    teacher_project,
    teacher_output,
    teacher_expand,
    teacher_reduce,
    teacher_vectors,
    student_table,
    student_position,
    student_project,
    student_output,
    student_expand,
    student_reduce,
    student_vectors,
    first_table,
    first_position,
    first_project,
    first_output,
    first_expand,
    first_reduce,
    first_vectors,
    square_table,
    square_position,
    square_project,
    square_output,
    square_expand,
    square_reduce,
    square_vectors,
):
    mp, dp = lax.axis_size("mp"), lax.axis_size("dp")
    place, index = lax.axis_index("mp"), lax.axis_index("dp")
    core = index & 1
    batch, length = token_ids.shape
    spans = mp // (2 * batch)
    rows = length // (2 * spans)
    vocab_rows = student_table.shape[0]
    share = student_table.shape[1]
    features = share * dp
    start = place * vocab_rows

    packed = jnp.concatenate(
        [
            token_ids * 2 + mlm_flags,
            jnp.pad((pad_lengths * 256 + group_ids)[None], ((0, 0), (0, length - batch))),
        ]
    )
    packed = ordered(1, packed[None], swap(packed, 1)[None], 0)
    column_ids = packed[:, :batch].reshape(2 * batch, spans, 2, rows)
    lengths = (packed[:, batch, :batch] // 256).reshape(-1)
    groups = (packed[:, batch, :batch] % 256).reshape(-1)
    chosen = groups[:, None] == jnp.arange(group_weight.shape[0])[None, :]
    seq_weight = jnp.sum(jnp.where(chosen, group_weight[None, :], 0.0), -1)
    line_place = (place - jnp.arange(mp)) % mp
    line = lax.dynamic_index_in_dim(column_ids, core, 2, keepdims=False).reshape(mp, rows)
    line = jnp.take(line, line_place, axis=0)
    line_targets, line_flags = line // 2, line % 2
    line_inputs = jnp.where(line_flags == 1, mask_token, line_targets)
    line_sequence = line_place // spans
    line_part = (line_place % spans) * 2 + core
    line_positions = line_part[:, None] * rows + jnp.arange(rows)[None, :]
    line_lengths = jnp.take(lengths, line_sequence)
    line_real = (line_positions < line_lengths[:, None]).astype(f32)
    line_masked = line_flags.astype(f32) * line_real
    line_weight = jnp.take(seq_weight, line_sequence)[:, None]
    tok_weight, mask_weight = line_weight * line_real, line_weight * line_masked
    own_part = line_part[0]
    held = jnp.concatenate(
        [part * rows + jnp.arange(rows) for part in sequence_parts(core, spans)]
    )
    valid = (held < line_lengths[0]).astype(f32)[None]

    slots = -(-(11 * rows // (10 * mp) + 16) // 32) * 32
    plain = (line_real > 0) & (line_inputs != mask_token)
    owner = line_inputs // vocab_rows
    wanted = plain & (owner == place)
    away = (owner[0] - place) % mp
    from_owner = plain[0] & (away[None, :] == jnp.arange(mp)[:, None])
    ordinal = jnp.arange(rows)
    earlier = (ordinal[:, None] <= ordinal[None, :]).astype(bf)
    ranks = jnp.dot(
        jnp.concatenate([wanted, from_owner], 0).astype(bf), earlier, preferred_element_type=f32
    )
    ranks = ranks.astype(jnp.int32) - 1
    wanted_rank = jnp.where(wanted, ranks[:mp], -1)
    own_rank = jnp.sum(jnp.where(from_owner, ranks[mp:], 0), 0)
    mask_owner = mask_token // vocab_rows
    pair_counts = jnp.sum(
        (plain[None] & (owner[None] == jnp.arange(mp)[:, None, None])).astype(f32), -1
    )

    def wanted_ids(turn):
        number = jnp.arange(slots - 1) + turn * (slots - 1)
        match = wanted_rank[:, None, :] == number[None, :, None]
        ids = jnp.sum(jnp.where(match, line_inputs[:, None, :] - start + 1, 0), -1) - 1
        shared_id = jnp.where((place == mask_owner) & (turn == 0), mask_token - start, -1)
        shared_id = jnp.broadcast_to(shared_id, (mp, 1))
        return jnp.concatenate([ids, shared_id], 1).reshape(-1, 1)

    def own_slots(turn):
        number = own_rank - turn * (slots - 1)
        at = jnp.where(plain[0] & (number >= 0) & (number < slots - 1), away * slots + number, -1)
        masked_at = ((mask_owner - place) % mp) * slots + slots - 1
        is_mask = (line_real[0] > 0) & (line_inputs[0] == mask_token) & (turn == 0)
        at = jnp.where(is_mask, masked_at, at)
        return (at[:, None] == jnp.arange(mp * slots)[None, :]).astype(bf)

    def sent(found):
        return found[:slots], [
            rotate(found[k * slots : (k + 1) * slots], -k) for k in range(1, mp)
        ]

    def placed_rows(got, turn):
        return jnp.dot(own_slots(turn), stacked([got[0], *got[1]]), preferred_element_type=f32)

    def every_owner(ids):
        bit = 1
        while bit < dp:
            ids = jnp.concatenate([ids, swap(ids, bit)], 0)
            bit *= 2
        return ids

    def at_owners(d_embed, turn):
        sums = columns_times(own_slots(turn), d_embed).astype(bf)
        return stacked(
            [sums[:slots]]
            + [rotate(sums[k * slots : (k + 1) * slots], k) for k in range(1, mp)]
        ).T

    def by_column(at_owner):
        placed, wide = [], mp * slots
        for other in range(dp):
            row = ((other & 1) * (dp // 2) + other // 2) * share
            part = at_owner[row : row + share]
            placed.append((swap(part, other) if other else part, 0, other * wide))
        return placed

    def returned(placed):
        return assemble(placed, (share, dp * mp * slots))

    local_targets = (line_targets - start).reshape(-1, 1)

    nonpad = (jnp.arange(length)[None, :] < pad_lengths[:, None]).astype(f32)
    masked = mlm_flags.astype(f32) * nonpad
    lane = jnp.arange(LANES)[None, :]
    counts = jnp.where(lane == 0, jnp.sum(nonpad), jnp.where(lane == 1, jnp.sum(masked), 0.0))
    counts = jnp.where(lane == 2, jnp.max(pair_counts), counts)
    counts = jnp.broadcast_to(counts, (8, LANES))
    bit = 1
    while bit < dp:
        got = swap(counts, bit)
        counts = jnp.where(lane == 2, jnp.maximum(counts, got), counts + got)
        bit *= 2
    count_tok, count_mask = counts[0, 0], jnp.maximum(counts[0, 1], 1.0)
    most = counts[0, 2].astype(jnp.int32)
    rounds = (most + slots - 2) // (slots - 1)

    head_cut = student_project.shape[2]
    unit_cut = student_expand.shape[1]
    cuts = [head_cut] * 4 + [unit_cut] * 2
    units = mp * unit_cut
    vector_rows = student_vectors.shape[0]

    table_parts = gather_start(student_table.T.astype(bf))

    def cut_rows(x, axis):
        return lax.dynamic_slice_in_dim(x, index * share, share, axis)

    s_share = joined(student_project, student_output.T, student_expand, student_reduce.T)
    t_share = joined(
        cut_rows(teacher_project, 1),
        cut_rows(teacher_output, 1).T,
        cut_rows(teacher_expand, 0),
        cut_rows(teacher_reduce, 1).T,
    )
    first_ids = wanted_ids(0)
    both_shares = stacked([t_share, s_share])

    def t_find(ids):
        return jnp.take(teacher_table, jnp.clip(ids[:, 0], 0, vocab_rows - 1), axis=0)

    table_parts, both_shares, first_ids = phase(table_parts, both_shares, first_ids)

    order = order_matrix(features, share)

    def reordered(x, back=False):
        return rows_times(x, order) if back else jnp.dot(x, order, preferred_element_type=f32)

    t_vectors = reordered(teacher_vectors)
    t_position = lax.dynamic_slice_in_dim(teacher_position, own_part * rows, rows, 0)
    t_position = reordered(t_position)
    vector_rows = student_vectors.shape[0]
    small_at = 2 * mp * sum(cuts)
    padded = -(small_at + length + vector_rows) % (2 * LANES)
    s_small = jnp.concatenate(
        [student_position.T, student_vectors.T, jnp.zeros((share, padded), f32)], 1
    ).astype(bf)

    table_parts = gather_rest(table_parts)
    both_shares = gather_mp(both_shares)
    table_parts, both_shares, s_small = phase(table_parts, both_shares, s_small)

    weight_parts = gather_start(by_kind(both_shares, cuts, 2, s_small))
    s_table = gather_end(table_parts)
    t_found = t_find(first_ids)
    s_table, weight_parts, t_found = phase(s_table, weight_parts, t_found)

    weight_parts = gather_rest(weight_parts)
    t_got = sent(t_found)
    s_found = pick_rows(first_ids, s_table)
    weight_parts, s_found, t_got = phase(weight_parts, s_found, t_got)

    classes = gather_end(weight_parts)
    s_got = sent(s_found)
    t_rows = lax.fori_loop(
        1,
        rounds,
        lambda turn, had: had + placed_rows(sent(t_find(wanted_ids(turn))), turn),
        placed_rows(t_got, 0),
    )
    t_embedded = reordered(t_rows.astype(bf)) + t_position
    classes, s_got, t_embedded = phase(classes, s_got, t_embedded)

    all_ids = every_owner(first_ids)

    s_rows = lax.fori_loop(
        1,
        rounds,
        lambda turn, had: had + placed_rows(sent(pick_rows(wanted_ids(turn), s_table)), turn),
        placed_rows(s_got, 0),
    )
    s_small = jnp.concatenate([c[:, small_at:] for c in classes], 0)
    s_vectors = s_small[:, length : length + vector_rows].T.astype(f32)
    s_position = lax.dynamic_slice_in_dim(s_small, own_part * rows, rows, 1).T
    s_embedded = s_rows + s_position.astype(f32)
    t_zero, t_query, t_own = layer_open(t_embedded, t_vectors, classes, 0, units)
    s_zero, s_query, s_own = layer_open(s_embedded, s_vectors, classes, 1, units)
    t_sequence, s_sequence = gather_sequence(t_own, spans), gather_sequence(s_own, spans)
    t_two = layer_close(t_zero, t_query, t_sequence, valid, t_vectors, classes, 0, units)[0]
    t_low = reordered(t_two.astype(bf), True).astype(bf)
    t_low, t_two, s_zero, s_query, s_sequence = phase(t_low, t_two, s_zero, s_query, s_sequence)

    def further(ring, steps):
        ring = list(ring)
        for _ in range(steps):
            ring.append(rotate(ring[-1]))
        return ring

    split = max(mp // 2, 1)
    far = mp - split
    t_ring = further([t_low], split - 1)
    s_two, s_attn, s_logs, s_one_pre, s_two_pre = layer_close(
        s_zero, s_query, s_sequence, valid, s_vectors, classes, 1, units
    )
    cos_terms, cos_pull = jax.vjp(lambda x: cosine_loss(x, t_two), s_two)
    own_weight = tok_weight[0]
    (d_cos,) = cos_pull(own_weight / count_tok)
    own_cos = jnp.sum(own_weight * cos_terms)
    t_ring, s_two, d_cos = phase(t_ring, s_two, d_cos)

    chunk_groups = [slice(0, split), slice(split, mp)]
    s_all = []

    def student(ring, n, t_out):
        group = chunk_groups[n]
        s_all.append(stacked(ring[group]))
        t_half, t_peaks, t_tail = t_out
        return student_pass(
            s_all[n],
            s_table,
            t_half,
            jnp.exp((t_peaks - t_tail[:, 0:1]) * 0.5),
            local_targets[group.start * rows : group.stop * rows],
        )

    t_first = head_pass(stacked(t_ring), teacher_table)
    t_ring = further(t_ring, far - far // 2)
    s_ring = further([s_two.astype(bf)], split - 1)
    t_ring, s_ring, t_first = phase(t_ring, s_ring, t_first)

    s_first = student(s_ring, 0, t_first)
    t_ring = further(t_ring, far // 2)
    s_ring = further(s_ring, far - far // 2)
    t_ring, s_ring, s_first = phase(t_ring, s_ring, s_first)

    t_second = head_pass(stacked(t_ring[split:]), teacher_table)
    s_ring = further(s_ring, far // 2)
    s_ring, t_second = phase(s_ring, t_second)

    s_second = student(s_ring, 1, t_second)
    t_outs, s_outs = [t_first, t_second], [s_first, s_second]
    t_peaks, t_tail = [jnp.concatenate([x[n] for x in t_outs], 0) for n in (1, 2)]
    s_peaks, s_tail = [jnp.concatenate([x[n] for x in s_outs], 0) for n in (1, 2)]

    mine = jnp.concatenate([t_tail[:, :8], s_tail[:, :8]], 1).T.reshape(16, mp, rows)
    stats = jnp.stack([mine] + [jnp.roll(rotate(mine, by), by, 1) for by in range(1, mp)])
    t_stats, s_stats = stats[:, :8], stats[:, 8:]
    t_peak = jnp.max(t_stats[:, 0], 0)
    t_grow = jnp.exp((t_stats[:, 0] - t_peak) / temper)
    t_half_sum = jnp.sum(t_grow * t_stats[:, 1], 0)
    s_peak = jnp.max(s_stats[:, 0], 0)
    s_grow = jnp.exp((s_stats[:, 0] - s_peak) / temper)
    s_half_sum = jnp.sum(s_grow * s_stats[:, 1], 0)
    s_full_sum = jnp.sum(s_grow * s_grow * s_stats[:, 2], 0)

    apart = jnp.sum(t_grow[:, 0] * (t_stats[:, 3, 0] - s_stats[:, 3, 0]), 0) / temper
    log_half_s = s_peak[0] / temper + jnp.log(s_half_sum[0])
    log_half_t = t_peak[0] / temper + jnp.log(t_half_sum[0])
    log_full = s_peak[0] + jnp.log(s_full_sum[0])
    diverge = temper * temper * (apart / t_half_sum[0] - log_half_t + log_half_s)
    missed = log_full - jnp.sum(s_stats[:, 4, 0], 0)
    own_terms = jnp.stack(
        [
            jnp.sum(own_weight * diverge),
            jnp.sum(mask_weight[0] * missed),
            own_cos,
        ]
    )
    own_terms = jnp.pad(own_terms[None], ((0, 7), (0, LANES - 3)))
    own_terms = own_terms + swap(own_terms, 1)
    line_terms = natural([own_terms] + [rotate(own_terms, by) for by in range(1, mp)])
    seq_terms = jnp.sum(line_terms[:, 0, :3].reshape(2 * batch, spans, 3), 1)
    loss_terms = lax.dynamic_slice_in_dim(seq_terms, core * batch, batch, 0)

    coef_kl = 5.0 * temper * tok_weight / count_tok
    coef_mlm = 2.0 * mask_weight / count_mask

    def by_token(values):
        return values.reshape(-1, 1)

    s_tiles = jnp.exp((s_peaks - by_token(s_peak)) / temper)
    t_tiles = jnp.exp((t_peaks - by_token(t_peak)) / temper)
    back = (
        s_tiles * by_token(coef_kl / s_half_sum),
        t_tiles * by_token(coef_kl / t_half_sum),
        s_tiles * s_tiles * by_token(coef_mlm / s_full_sum),
        by_token(coef_mlm),
        local_targets,
        s_table,
    )
    d_logits, d_sent = [None] * mp, []
    for step in range(mp):
        k = (step + 1) % mp
        n = 0 if k < split else 1
        halves = s_outs[n][0], t_outs[n][0]
        if step >= 3:
            halves, d_sent[step - 3] = phase(halves, d_sent[step - 3])
        d_logits[k], d_row = head_back(k, k - chunk_groups[n].start, rows, *halves, *back)
        if k:
            d_sent.append(rotate(d_row, -k))
    if mp > 2:
        d_logits, d_sent[:-1] = phase(d_logits, d_sent[:-1])
    d_head = d_row.astype(f32)
    for got in d_sent:
        d_head = d_head + got.astype(f32)
    g_head = table_grad(jnp.concatenate([x.T for x in s_all], 1), d_logits)
    d_two = d_head + d_cos
    d_two, g_head = phase(d_two, g_head)

    table_sum = scatter_start(g_head)
    from_units = units_back(d_two, s_two_pre, s_one_pre, s_vectors, classes, 1, units)
    table_sum, from_units = phase(table_sum, from_units)
    d_reduce, active, one_low, d_hidden, d_branch, d_one_pre, d_attn, sums = from_units

    table_sum = scatter_step(table_sum, 0)
    from_attention = attention_back(s_query, s_sequence, d_attn, s_logs, valid)
    table_sum, from_attention, d_reduce, active, one_low, d_hidden = phase(
        table_sum, from_attention, d_reduce, active, one_low, d_hidden
    )

    table_sum = scatter_all(table_sum)
    d_both = scatter_sequence(from_attention[1:], spans).astype(bf)
    g_units = assemble(
        [
            (columns_times(one_low, d_hidden).astype(bf), 0, 0),
            (columns_times(d_reduce, active).astype(bf), 0, units),
        ],
        (features, 2 * units),
    )
    table_sum, d_both, g_units, s_zero = phase(table_sum, d_both, g_units, s_zero)

    units_sum = scatter_start(g_units)
    d_parts = (from_attention[0], d_both[0], d_both[1])
    d_embed, first_sums = embed_back(
        d_parts, d_one_pre, s_embedded, s_vectors, classes, 1, units
    )
    low = s_zero.astype(bf)
    g_heads = [columns_times(low, d).astype(bf) for d in d_parts]
    g_heads.append(columns_times(d_branch, s_attn).astype(bf))
    g_position = lax.dynamic_update_slice_in_dim(
        jnp.zeros((features, length), bf), d_embed.T, own_part * rows, 1
    )
    heads_at = mp * 4 * head_cut
    head_wide = mp * head_cut
    late_padded = -(heads_at + length + vector_rows) % (2 * LANES)
    g_vectors = jnp.pad((sums + first_sums).T.astype(bf), ((0, 0), (0, late_padded)))
    g_late = assemble(
        [(g, 0, t * head_wide) for t, g in enumerate(g_heads)]
        + [(g_position, 0, heads_at), (g_vectors, 0, heads_at + length)],
        (features, heads_at + length + vector_rows + late_padded),
    )
    units_sum, d_embed, g_late = phase(units_sum, d_embed, g_late)

    def by_place(summed, kinds, cut):
        return [
            jnp.concatenate(
                [summed[:, (t * mp + k) * cut : (t * mp + k + 1) * cut] for t in range(kinds)], 1
            )
            for k in range(mp)
        ]

    units_sum = scatter_step(units_sum, 0)
    late_sum = scatter_start(g_late)
    at_owner = at_owners(d_embed, 0)
    units_sum, late_sum, at_owner = phase(units_sum, late_sum, at_owner)

    units_sum = scatter_end(scatter_all(units_sum))
    late_sum = scatter_step(late_sum, 0)
    placed = by_column(at_owner)
    arrived, units_sum, late_sum = phase([x for x, _, _ in placed], units_sum, late_sum)

    late_sum = scatter_end(scatter_all(late_sum))
    own_units = sum_mp(by_place(units_sum, 2, unit_cut))
    e_rows = returned([(x, row, at) for x, (_, row, at) in zip(arrived, placed)])
    own_table = add_rows(scatter_end(table_sum), e_rows, all_ids, 0)
    own_table, own_units, late_sum = phase(own_table, own_units, late_sum)

    small = late_sum[:, heads_at:].astype(bf)
    heads = [x.astype(bf) for x in by_place(late_sum, 4, head_cut)]
    got = [jnp.concatenate([x, small], 1) for x in heads]
    got = got[:1] + [rotate(got[k], -k) for k in range(1, mp)]
    own_table = add_rows(own_table, e_rows, all_ids, 1)
    got, own_table = phase(got, own_table)
    own_heads = sum(x[:, : 4 * head_cut].astype(f32) for x in got)
    got = [got[-k % mp][:, 4 * head_cut :] for k in range(mp)]
    own_small = jnp.sum(natural(got).astype(f32), 0)
    own_table = lax.fori_loop(
        1,
        rounds,
        lambda turn, had: add_rows(
            had,
            returned(by_column(at_owners(d_embed, turn))),
            every_owner(wanted_ids(turn)),
            None,
        ),
        own_table,
    )

    shared_sq = jnp.sum(own_small * own_small) / mp
    squares = (
        jnp.sum(own_table * own_table)
        + jnp.sum(own_units * own_units)
        + jnp.sum(own_heads * own_heads)
        + shared_sq
    )
    squares = sum_all(jnp.broadcast_to(squares, (8, LANES)))[0, 0]
    norm = jnp.sqrt(squares)
    factor = clip_limit / jnp.maximum(norm, clip_limit)

    owned = (
        own_table.T,
        own_small[:, :length].T,
        jnp.stack([own_heads[:, t * head_cut : (t + 1) * head_cut] for t in range(3)]),
        own_heads[:, 3 * head_cut :].T,
        own_units[:, :unit_cut],
        own_units[:, unit_cut:].T,
        own_small[:, length : length + vector_rows].T,
    )
    masters = (
        student_table,
        student_position,
        student_project,
        student_output,
        student_expand,
        student_reduce,
        student_vectors,
    )
    firsts = (
        first_table,
        first_position,
        first_project,
        first_output,
        first_expand,
        first_reduce,
        first_vectors,
    )
    seconds = (
        square_table,
        square_position,
        square_project,
        square_output,
        square_expand,
        square_reduce,
        square_vectors,
    )
    results = []
    for index in range(7):
        rate = rate_vector if index == 6 else rate_table if index == 0 else rate_matrix
        decay = 0.0 if index == 6 else weight_decay
        results += adam_update(
            masters[index], firsts[index], seconds[index], owned[index], factor, rate, decay
        )
    loss_counts = jnp.stack([count_tok, count_mask])
    return (*results, norm, loss_terms, loss_counts)


def solution(mesh):
    in_specs = (
        P("dp", None),
        P("dp", None),
        P("dp"),
        P("dp"),
        P(),
        P("mp", None),
        P(),
        P(None, None, "mp"),
        P("mp", None),
        P(None, "mp"),
        P("mp", None),
        P(),
        P("mp", "dp"),
        P(None, "dp"),
        P(None, "dp", "mp"),
        P("mp", "dp"),
        P("dp", "mp"),
        P("mp", "dp"),
        P(None, "dp"),
        P("mp", "dp"),
        P(None, "dp"),
        P(None, "dp", "mp"),
        P("mp", "dp"),
        P("dp", "mp"),
        P("mp", "dp"),
        P(None, "dp"),
        P("mp", "dp"),
        P(None, "dp"),
        P(None, "dp", "mp"),
        P("mp", "dp"),
        P("dp", "mp"),
        P("mp", "dp"),
        P(None, "dp"),
    )
    out_specs = (
        P("mp", "dp"),
        P("mp", "dp"),
        P("mp", "dp"),
        P(None, "dp"),
        P(None, "dp"),
        P(None, "dp"),
        P(None, "dp", "mp"),
        P(None, "dp", "mp"),
        P(None, "dp", "mp"),
        P("mp", "dp"),
        P("mp", "dp"),
        P("mp", "dp"),
        P("dp", "mp"),
        P("dp", "mp"),
        P("dp", "mp"),
        P("mp", "dp"),
        P("mp", "dp"),
        P("mp", "dp"),
        P(None, "dp"),
        P(None, "dp"),
        P(None, "dp"),
        P(),
        P("dp", None),
        P(),
    )
    return jax.shard_map(body, mesh=mesh, in_specs=in_specs, out_specs=out_specs, check_vma=False)
```

```python
import jax
import jax.numpy as jnp
from jax import lax
from jax.experimental import pallas as pl
from jax.experimental.pallas import tpu as pltpu
from jax.sharding import PartitionSpec as P

HD = 64
STEP = 10
LANES = 128
LOG2E = 1.4426950408889634


eps_norm = 1e-05
mask_token = 103
temper = 2.0
beta_first = 0.9
beta_second = 0.999
adam_eps = 1e-08
rate_table = 0.5
rate_matrix = 0.1
rate_vector = 0.3
weight_decay = 0.01
clip_limit = 1.0
bf = jnp.bfloat16
f32 = jnp.float32
vmem_bytes = 56 * 1024 * 1024


def swap(x, bit):
    count = lax.axis_size("dp")
    return lax.ppermute(x, "dp", [(i, i ^ bit) for i in range(count)])


def rotate(x, by=1):
    count = lax.axis_size("mp")
    return lax.ppermute(x, "mp", [(i, (i + by) % count) for i in range(count)])


def chip_bits():
    count = lax.axis_size("dp")
    bits = []
    bit = 2
    while bit < count:
        bits.append(bit)
        bit *= 2
    return bits


def ordered(bit, mine, other, axis):
    low = (lax.axis_index("dp") & bit) == 0
    return jnp.where(
        low, jnp.concatenate([mine, other], axis), jnp.concatenate([other, mine], axis)
    )


def phase(*arrays):
    return lax.optimization_barrier(arrays)


def gather_start(x):
    half = x.shape[1] // 2
    bits = chip_bits()
    parts = []
    for part, order in ((x[:, :half], bits), (x[:, half:], bits[::-1])):
        pieces = {0: part}
        if order:
            pieces[order[0] // 2] = swap(part, order[0])
        parts.append(pieces)
    return parts


def gather_rest(parts):
    done = []
    bits = chip_bits()
    for pieces, order in zip(parts, (bits[1:], bits[::-1][1:])):
        pieces = dict(pieces)
        for bit in order:
            for chip in list(pieces):
                pieces[chip | (bit // 2)] = swap(pieces[chip], bit)
        done.append(pieces)
    return done


def gather_end(parts):
    placed, width = [], 0
    for pieces in parts:
        rows, columns = pieces[0].shape
        placed += [(piece, chip * rows, width) for chip, piece in pieces.items()]
        width += columns
    mine = assemble(placed, (len(parts[0]) * rows, width))
    return mine, swap(mine, 1)


def scatter_start(y):
    total_rows, columns = y.shape
    count = lax.axis_size("dp")
    half = columns // 2
    state = []
    for part in (y[:, :half], y[:, half:]):
        mine, other = part[: total_rows // 2], part[total_rows // 2 :]
        left = mine.astype(f32) + swap(other.astype(bf), 1).astype(f32)
        state.append(left.reshape(count // 2, total_rows // count, -1))
    return state


def scatter_step(state, step):
    bits = chip_bits()
    if step >= len(bits):
        return state
    after = []
    for which, left in enumerate(state):
        groups, rows, columns = left.shape
        if which == 0:
            bit = bits[::-1][step]
            keep, give = left[: groups // 2], left[groups // 2 :]
        else:
            bit = bits[step]
            split = left.reshape(groups // 2, 2, rows, columns)
            keep, give = split[:, 0], split[:, 1]
        after.append(keep + swap(give.astype(bf), bit).astype(f32))
    return after


def scatter_end(state):
    return jnp.concatenate([left[0] for left in state], 1)


def scatter_all(state):
    for step in range(1, len(chip_bits())):
        state = scatter_step(state, step)
    return state


def order_matrix(features, share):
    count = lax.axis_size("dp")
    at = jnp.arange(features)
    block, inside = at // share, at % share
    other_core, chip = block // (count // 2), block % (count // 2)
    source = (lax.axis_index("dp") ^ (chip * 2 + other_core)) * share + inside
    return (jnp.arange(features)[:, None] == source[None, :]).astype(bf)


def gather_mp(x):
    return [x] + [rotate(x, by) for by in range(1, lax.axis_size("mp"))]


def natural(entries):
    count = lax.axis_size("mp")
    index = lax.axis_index("mp")
    stacked = jnp.stack(entries)
    return jnp.stack(
        [
            lax.dynamic_index_in_dim(stacked, (index - i) % count, 0, keepdims=False)
            for i in range(count)
        ]
    )


def sum_mp(terms):
    total = terms[0].astype(f32)
    for k in range(1, len(terms)):
        total = total + rotate(terms[k].astype(bf), -k).astype(f32)
    return total


def sum_all(x):
    bit = 1
    while bit < lax.axis_size("dp"):
        x = x + swap(x, bit)
        bit *= 2
    count = lax.axis_size("mp")
    bit = 1
    while bit < count:
        x = x + lax.ppermute(x, "mp", [(i, i ^ bit) for i in range(count)])
        bit *= 2
    return x


def tile_of(total, cap):
    best = LANES
    for size in range(LANES, min(total, cap) + 1, LANES):
        if total % size == 0:
            best = size
    return best


def call(body, grid, in_specs, out_specs, out_shape, scratch, flops, moved):
    return pl.pallas_call(
        body,
        grid=grid,
        in_specs=in_specs,
        out_specs=out_specs,
        out_shape=out_shape,
        scratch_shapes=scratch,
        compiler_params=pltpu.CompilerParams(
            dimension_semantics=("arbitrary",) * len(grid), vmem_limit_bytes=vmem_bytes
        ),
        cost_estimate=pl.CostEstimate(flops=flops, bytes_accessed=moved, transcendentals=0),
    )


def assemble(placed, shape):
    kind = placed[0][0].dtype
    if any(at % LANES or x.shape[1] % LANES or x.shape[0] % 16 for x, _, at in placed):
        out = jnp.zeros(shape, kind)
        for x, row, at in placed:
            out = lax.dynamic_update_slice(out, x, (row, at))
        return out
    count = len(placed)

    def body(*refs):
        ins, out, sems = refs[:count], refs[count], refs[count + 1]
        copies = []
        for n, (x, row, at) in enumerate(placed):
            high, wide = x.shape
            copies.append(
                pltpu.make_async_copy(
                    ins[n], out.at[row : row + high, at : at + wide], sems.at[n]
                )
            )
        for copy in copies:
            copy.start()
        for copy in copies:
            copy.wait()

    moved = 2 * sum(x.size * x.dtype.itemsize for x, _, _ in placed)
    return pl.pallas_call(
        body,
        in_specs=[pl.BlockSpec(memory_space=pl.ANY)] * count,
        out_specs=pl.BlockSpec(memory_space=pltpu.VMEM),
        out_shape=jax.ShapeDtypeStruct(shape, kind),
        scratch_shapes=[pltpu.SemaphoreType.DMA((count,))],
        compiler_params=pltpu.CompilerParams(vmem_limit_bytes=vmem_bytes),
        cost_estimate=pl.CostEstimate(flops=0, bytes_accessed=moved, transcendentals=0),
    )(*[x for x, _, _ in placed])


def stacked(arrays):
    placed, row = [], 0
    for x in arrays:
        placed.append((x, row, 0))
        row += x.shape[0]
    return assemble(placed, (row, arrays[0].shape[1]))


def joined(project, output_t, expand, reduce_t):
    rows = expand.shape[0]
    parts = [project.shape[2]] * 3 + [x.shape[1] for x in (output_t, expand, reduce_t)]
    if any(part % LANES for part in parts):
        return jnp.concatenate(
            [x.astype(bf) for x in (*project, output_t, expand, reduce_t)], 1
        )

    def body(project_ref, output_ref, expand_ref, reduce_ref, out_ref):
        at = 0
        for value in (
            project_ref[0], project_ref[1], project_ref[2], output_ref[...], expand_ref[...],
            reduce_ref[...],
        ):
            out_ref[:, at : at + value.shape[1]] = value.astype(bf)
            at += value.shape[1]

    shape = (rows, sum(parts))
    return call(
        body,
        (1,),
        [whole(x.shape) for x in (project, output_t, expand, reduce_t)],
        whole(shape),
        jax.ShapeDtypeStruct(shape, bf),
        [],
        0,
        6 * shape[0] * shape[1],
    )(project, output_t, expand, reduce_t)


def by_kind(shares, cuts, models, tail):
    rows = shares[0].shape[0] // models
    placed, to = [], 0
    for model in range(models):
        at = 0
        for cut in cuts:
            for n in range(len(shares)):
                placed.append((n, model, at, cut, to))
                to += cut
            at += cut
    if any(cut % LANES for cut in cuts):
        return jnp.concatenate(
            [
                shares[n][model * rows : (model + 1) * rows, at : at + cut]
                for n, model, at, cut, _ in placed
            ]
            + [tail],
            1,
        )
    count = len(shares)

    def body(*refs):
        out_ref = refs[-1]
        for n, model, at, cut, into in placed:
            part = slice(model * rows, (model + 1) * rows)
            out_ref[:, into : into + cut] = refs[n][part, at : at + cut]
        out_ref[:, to:] = refs[count][...]

    shape = (rows, to + tail.shape[1])
    return call(
        body,
        (1,),
        [whole(x.shape) for x in (*shares, tail)],
        whole(shape),
        jax.ShapeDtypeStruct(shape, bf),
        [],
        0,
        4 * shape[0] * shape[1],
    )(*shares, tail)


def whole(shape):
    return pl.BlockSpec(shape, lambda *_: (0,) * len(shape))


def onto(x, tables):
    total, at = None, 0
    for table in tables:
        wide = table.shape[0]
        term = jnp.dot(x[:, at : at + wide], table, preferred_element_type=f32)
        total = term if total is None else total + term
        at += wide
    return total


def rows_times(x, flipped):
    return lax.dot_general(x, flipped, (((1,), (1,)), ((), ())), preferred_element_type=f32)


def pick_rows(ids, tables):
    half, vocab = tables[0].shape
    width = half * len(tables)
    tile = tile_of(vocab, 1536)
    rows = ids.shape[0]

    def body(ids_ref, *refs):
        table_refs, (out_ref, total) = refs[: len(tables)], refs[len(tables) :]
        j = pl.program_id(0)

        @pl.when(j == 0)
        def _():
            total[...] = jnp.zeros_like(total)

        lane = lax.broadcasted_iota(jnp.int32, (rows, tile), 1)
        hot = jnp.where(lane == ids_ref[...] - j * tile, 1.0, 0.0).astype(bf)
        for t, table_ref in enumerate(table_refs):
            total[:, t * half : (t + 1) * half] += rows_times(hot, table_ref[...])

        @pl.when(j == pl.num_programs(0) - 1)
        def _():
            out_ref[...] = total[...].astype(bf)

    return call(
        body,
        (vocab // tile,),
        [whole((rows, 1))] + [pl.BlockSpec((half, tile), lambda j: (0, j))] * len(tables),
        whole((rows, width)),
        jax.ShapeDtypeStruct((rows, width), bf),
        [pltpu.VMEM((rows, width), f32)],
        2 * rows * width * vocab,
        2 * width * vocab,
    )(ids, *tables)


def lane_value(values, j):
    lane = lax.broadcasted_iota(jnp.int32, values.shape, 1)
    return jnp.sum(jnp.where(lane == j, values, 0.0), 1, keepdims=True)


def head_tile(vocab):
    return tile_of(vocab, 1536)


def head_pass(t_x, s_x, t_table, s_tables, targets):
    vocab, width = t_table.shape
    half_width = s_tables[0].shape[0]
    rows = t_x.shape[0]
    tile = head_tile(vocab)
    step = min(rows, 256)
    block_wide = 256 if tile % 256 == 0 else LANES
    count = len(s_tables)

    def body(t_ref, s_ref, t_table_ref, *refs):
        table_refs, refs = refs[:count], refs[count:]
        target_ref, t_half_ref, s_half_ref, t_peaks_ref, s_peaks_ref, stats_ref = refs[:6]
        table, t_peak, s_peak, t_high, s_high, *sums = refs[6:]
        new, total = sums[:5], sums[5:]
        j = pl.program_id(0)
        for t, table_ref in enumerate(table_refs):
            table[t * half_width : (t + 1) * half_width, :] = table_ref[...]

        def over_rows(work):
            for b in range(rows // step):
                work(pl.ds(b * step, step))

        def top_of(ref, part):
            return jnp.broadcast_to(jnp.max(ref[part, :], 1, keepdims=True), (step, LANES))

        @pl.when(j == 0)
        def _():
            for ref in (t_peaks_ref, s_peaks_ref, *total):
                ref[...] = jnp.zeros_like(ref)

            def begin(part):
                t_high[part, :] = rows_times(t_ref[part, :], t_table_ref[:LANES, :])
                s_high[part, :] = jnp.dot(
                    s_ref[part, :], table[:, :LANES], preferred_element_type=f32
                )
                t_peak[part, :] = top_of(t_high, part)
                s_peak[part, :] = top_of(s_high, part)

            over_rows(begin)

        def digest(part):
            lane = lax.broadcasted_iota(jnp.int32, (step, LANES), 1)
            t_ref_peak, s_ref_peak = t_peak[part, :], s_peak[part, :]
            t_top, s_top = t_high[part, :], s_high[part, :]
            values = [jnp.zeros((step, LANES), f32) for _ in new]
            target = jnp.broadcast_to(target_ref[part, :] - j * tile, (step, LANES)) - lane
            for first in range(0, tile, block_wide):
                here = slice(first, first + block_wide)
                t_z = rows_times(t_ref[part, :], t_table_ref[here, :])
                s_z = jnp.dot(s_ref[part, :], table[:, here], preferred_element_type=f32)
                for inner in range(0, block_wide, LANES):
                    at = first + inner
                    t_piece = t_z[:, inner : inner + LANES]
                    s_piece = s_z[:, inner : inner + LANES]
                    t_half = jnp.exp2((t_piece - t_ref_peak) * (0.5 * LOG2E))
                    s_half = jnp.exp2((s_piece - s_ref_peak) * (0.5 * LOG2E))
                    t_half_ref[part, at : at + LANES] = t_half.astype(bf)
                    s_half_ref[part, at : at + LANES] = s_half.astype(bf)
                    t_top = jnp.maximum(t_top, t_piece)
                    s_top = jnp.maximum(s_top, s_piece)
                    values[0] += t_half
                    values[1] += s_half
                    values[2] += s_half * s_half
                    values[3] += t_half * (t_piece - s_piece)
                    values[4] += jnp.where(target == at, s_piece, 0.0)
            for ref, value in zip(new, values):
                ref[part, :] = value
            t_high[part, :] = t_top
            s_high[part, :] = s_top

        over_rows(digest)
        above = jnp.maximum(t_high[...] - t_peak[...], s_high[...] - s_peak[...])

        @pl.when(jnp.max(above) > 60.0)
        def _():
            @pl.loop(0, rows // step)
            def _(b):
                part = pl.ds(pl.multiple_of(b * step, step), step)
                t_top, s_top = top_of(t_high, part), top_of(s_high, part)
                t_shrink = jnp.exp((t_peak[part, :] - t_top) * 0.5)
                s_shrink = jnp.exp((s_peak[part, :] - s_top) * 0.5)
                for ref, shrink in zip(
                    total, (t_shrink, s_shrink, s_shrink * s_shrink, t_shrink)
                ):
                    ref[part, :] *= shrink
                t_peak[part, :] = t_top
                s_peak[part, :] = s_top
                digest(part)

        def settle(part):
            lane = lax.broadcasted_iota(jnp.int32, (step, LANES), 1)
            t_before, s_before = t_peak[part, :], s_peak[part, :]
            t_top, s_top = top_of(t_high, part), top_of(s_high, part)
            t_shrink = jnp.exp((t_before - t_top) * 0.5)
            s_shrink = jnp.exp((s_before - s_top) * 0.5)
            shrinks = (t_shrink, s_shrink, s_shrink * s_shrink, t_shrink)
            for ref, add, shrink in zip(total, new, shrinks):
                ref[part, :] = (ref[part, :] + add[part, :]) * shrink
            total[4][part, :] += new[4][part, :]
            t_peaks_ref[part, :] = jnp.where(lane == j, t_before, t_peaks_ref[part, :])
            s_peaks_ref[part, :] = jnp.where(lane == j, s_before, s_peaks_ref[part, :])
            t_peak[part, :] = t_top
            s_peak[part, :] = s_top

        over_rows(settle)

        @pl.when(j == pl.num_programs(0) - 1)
        def _():
            lane = lax.broadcasted_iota(jnp.int32, (rows, LANES), 1)
            t_sum, s_sum, full, cross, target = [
                jnp.sum(ref[...], 1, keepdims=True) for ref in total
            ]
            out = jnp.where(lane == 0, t_peak[...], jnp.where(lane == 2, s_peak[...], 0.0))
            for slot, value in ((1, t_sum), (3, s_sum), (4, full), (5, cross), (6, target)):
                out = jnp.where(lane == slot, value, out)
            stats_ref[...] = out

    block = pl.BlockSpec((rows, tile), lambda j: (0, j))
    lanes = whole((rows, LANES))
    stat = jax.ShapeDtypeStruct((rows, LANES), f32)
    half = jax.ShapeDtypeStruct((rows, vocab), bf)
    return call(
        body,
        (vocab // tile,),
        [whole((rows, width))] * 2
        + [pl.BlockSpec((tile, width), lambda j: (j, 0))]
        + [pl.BlockSpec((half_width, tile), lambda j: (0, j))] * count
        + [whole((rows, 1))],
        [block, block, lanes, lanes, lanes],
        [half, half, stat, stat, stat],
        [pltpu.VMEM((width, tile), bf)] + [pltpu.VMEM((rows, LANES), f32)] * 14,
        4 * rows * width * vocab,
        4 * width * vocab + 4 * rows * vocab,
    )(t_x, s_x, t_table, *s_tables, targets)


def head_back(k, k_half, rows, s_half, t_half, s_scale, t_scale, f_scale, hit_scale, targets, tables):
    part_width, vocab = tables[0].shape
    width = part_width * len(tables)
    tile = head_tile(vocab)
    step = min(rows, 256)

    def body(s_ref, t_ref, a_ref, b_ref, c_ref, h_ref, target_ref, *refs):
        table_refs, (d_ref, out_ref, total) = refs[: len(tables)], refs[len(tables) :]
        j = pl.program_id(0)

        @pl.when(j == 0)
        def _():
            total[...] = jnp.zeros_like(total)

        for begin in range(0, rows, step):
            part = pl.ds(begin, step)
            a = jnp.broadcast_to(lane_value(a_ref[part, :], j), (step, LANES))
            b = jnp.broadcast_to(lane_value(b_ref[part, :], j), (step, LANES))
            c = jnp.broadcast_to(lane_value(c_ref[part, :], j), (step, LANES))
            h = jnp.broadcast_to(h_ref[part, :], (step, LANES))
            target = jnp.broadcast_to(target_ref[part, :] - j * tile, (step, LANES))
            lane = lax.broadcasted_iota(jnp.int32, (step, LANES), 1)
            for at in range(0, tile, LANES):
                half = s_ref[part, at : at + LANES].astype(f32)
                grad = half * (a + half * c) - t_ref[part, at : at + LANES].astype(f32) * b
                grad -= jnp.where(lane == target - at, h, 0.0)
                d_ref[part, at : at + LANES] = grad.astype(bf)
            for t, table_ref in enumerate(table_refs):
                total[part, t * part_width : (t + 1) * part_width] += rows_times(
                    d_ref[part, :], table_ref[...]
                )

        @pl.when(j == pl.num_programs(0) - 1)
        def _():
            out_ref[...] = total[...].astype(bf)

    block = pl.BlockSpec((rows, tile), lambda j: (k_half, j))
    lanes = pl.BlockSpec((rows, LANES), lambda j: (k, 0))
    column = pl.BlockSpec((rows, 1), lambda j: (k, 0))
    return call(
        body,
        (vocab // tile,),
        [block, block, lanes, lanes, lanes, column, column]
        + [pl.BlockSpec((part_width, tile), lambda j: (0, j))] * len(tables),
        [pl.BlockSpec((rows, tile), lambda j: (0, j)), whole((rows, width))],
        [jax.ShapeDtypeStruct((rows, vocab), bf), jax.ShapeDtypeStruct((rows, width), bf)],
        [pltpu.VMEM((rows, width), f32)],
        2 * rows * width * vocab,
        2 * width * vocab + 6 * rows * vocab,
    )(s_half, t_half, s_scale, t_scale, f_scale, hit_scale, targets, *tables)


def table_grad(x_flipped, d_logits):
    width = x_flipped.shape[0]
    rows, vocab = d_logits[0].shape
    tile = tile_of(vocab, 1536)
    count = len(d_logits)

    def body(x_ref, *refs):
        total = None
        for k, d_ref in enumerate(refs[:-1]):
            term = jnp.dot(
                x_ref[:, k * rows : (k + 1) * rows], d_ref[...], preferred_element_type=f32
            )
            total = term if total is None else total + term
        refs[-1][...] = total.astype(bf)

    return call(
        body,
        (vocab // tile,),
        [whole((width, rows * count))] + [pl.BlockSpec((rows, tile), lambda j: (0, j))] * count,
        pl.BlockSpec((width, tile), lambda j: (0, j)),
        jax.ShapeDtypeStruct((width, vocab), bf),
        [],
        2 * rows * count * width * vocab,
        2 * rows * count * vocab + 4 * width * vocab,
    )(x_flipped, *d_logits)


def add_rows(base, e_flipped, ids, half):
    width, vocab = base.shape
    rows = ids.shape[0]
    tile = tile_of(vocab, 768)
    step = tile_of(rows, 512)
    tiles = vocab // tile
    first, count = 0, tiles
    if half is not None:
        first, count = (0, tiles // 2) if half == 0 else (tiles // 2, tiles - tiles // 2)

    def body(base_ref, e_ref, ids_ref, out_ref):
        j = pl.program_id(0) + first
        lane = lax.broadcasted_iota(jnp.int32, (step, tile), 1)
        total = base_ref[...]
        for begin in range(0, rows, step):
            part = slice(begin, begin + step)
            hot = jnp.where(lane == ids_ref[part, :] - j * tile, 1.0, 0.0).astype(bf)
            total += jnp.dot(e_ref[:, part], hot, preferred_element_type=f32)
        out_ref[...] = total

    block = pl.BlockSpec((width, tile), lambda j: (0, j + first))
    return pl.pallas_call(
        body,
        grid=(count,),
        in_specs=[block, whole((width, rows)), whole((rows, 1))],
        out_specs=block,
        out_shape=jax.ShapeDtypeStruct((width, vocab), f32),
        input_output_aliases={0: 0},
        compiler_params=pltpu.CompilerParams(
            dimension_semantics=("arbitrary",), vmem_limit_bytes=vmem_bytes
        ),
        cost_estimate=pl.CostEstimate(
            flops=2 * rows * width * vocab, bytes_accessed=8 * width * vocab, transcendentals=0
        ),
    )(base, e_flipped, ids)


def heads_reordered(x):
    count = lax.axis_size("mp")
    return jnp.concatenate(list(natural(jnp.split(x, count, -1))), -1)


def gather_sequence(x, spans):
    parts = [x, swap(x, 1)]
    if spans > 1:
        count = lax.axis_size("mp")
        groups = [list(range(i, i + spans)) for i in range(0, count, spans)]
        both = heads_reordered(jnp.concatenate(parts, 1))
        both = lax.all_gather(both, "mp", axis=1, axis_index_groups=groups, tiled=True)
        parts = [heads_reordered(both)]
    return parts


def scatter_sequence(parts, spans):
    if spans > 1:
        count = lax.axis_size("mp")
        groups = [list(range(i, i + spans)) for i in range(0, count, spans)]
        x = lax.psum_scatter(
            heads_reordered(parts[0].astype(f32)),
            "mp",
            scatter_dimension=1,
            axis_index_groups=groups,
            tiled=True,
        )
        parts = jnp.split(heads_reordered(x), 2, 1)
    return parts[0].astype(f32) + swap(parts[1].astype(bf), 1).astype(f32)


def sequence_parts(core, spans):
    if spans == 1:
        return [core, 1 - core]
    return [chip * 2 + side for chip in range(spans) for side in (core, 1 - core)]


def norm_parts(x):
    centre = x - jnp.mean(x, -1, keepdims=True)
    spread = jnp.mean(centre * centre, -1, keepdims=True)
    scale = lax.rsqrt(spread + eps_norm)
    return centre * scale, scale


def norm_back(unit, scale, gain, grad):
    inner = grad * gain
    slope = inner - jnp.mean(inner, -1, keepdims=True)
    slope = (slope - unit * jnp.mean(inner * unit, -1, keepdims=True)) * scale
    return slope, jnp.sum(grad * unit, 0, keepdims=True), jnp.sum(grad, 0, keepdims=True)


def resident(shape):
    return pl.BlockSpec(shape, lambda *_: (0,) * len(shape), pipeline_mode=pl.Buffered(1))


def put_rows(ref, j, values):
    row = lax.broadcasted_iota(jnp.int32, ref.shape, 0)
    add = jnp.zeros(ref.shape, f32)
    for at, value in values.items():
        add = jnp.where(row == at, value, add)

    @pl.when(j == 0)
    def _():
        ref[...] = add

    @pl.when(j > 0)
    def _():
        ref[...] += add


def weight_blocks(classes, model, features, units, opening):
    columns = 4 * features + 2 * units
    wide = 3 * features if opening and columns % (3 * features) == 0 else columns
    return [
        pl.BlockSpec(
            (c.shape[0], wide),
            lambda *_: (0, model * columns // wide),
            pipeline_mode=pl.Buffered(1),
        )
        for c in classes
    ]


def columns_of(features, units):
    cuts, at = [], 0
    for wide in [features] * 4 + [units] * 2:
        cuts.append(slice(at, at + wide))
        at += wide
    return cuts


def side_by_side(x, classes, cut):
    return jnp.concatenate([rows_times(x, c[:, cut]) for c in classes], 1)


def through(x, classes, cut):
    high = classes[0].shape[0]
    total = None
    for t, c in enumerate(classes):
        term = jnp.dot(x[:, t * high : (t + 1) * high], c[:, cut], preferred_element_type=f32)
        total = term if total is None else total + term
    return total


def layer_open(embedded, vectors, classes, model, units):
    rows, features = embedded.shape
    cuts = columns_of(features, units)
    step = min(rows, 256)
    count = len(classes)

    def body(x_ref, vectors_ref, *refs):
        class_refs, (zero_ref, q_ref, kv_ref) = refs[:count], refs[count:]
        unit, _ = norm_parts(x_ref[...])
        zero = unit * vectors_ref[0:1, :] + vectors_ref[1:2, :]
        zero_ref[...] = zero
        low = zero.astype(bf)
        q_ref[...] = through(low, class_refs, cuts[0]).astype(bf)
        kv_ref[0] = through(low, class_refs, cuts[1]).astype(bf)
        kv_ref[1] = through(low, class_refs, cuts[2]).astype(bf)

    block = pl.BlockSpec((step, features), lambda j: (j, 0))
    return call(
        body,
        (rows // step,),
        [block, whole(vectors.shape)] + weight_blocks(classes, model, features, units, True),
        [block, block, pl.BlockSpec((2, step, features), lambda j: (0, j, 0))],
        [
            jax.ShapeDtypeStruct((rows, features), f32),
            jax.ShapeDtypeStruct((rows, features), bf),
            jax.ShapeDtypeStruct((2, rows, features), bf),
        ],
        [],
        6 * rows * features * features,
        6 * features * features + 16 * rows * features,
    )(embedded, vectors, *classes)


def head_lanes(shape, which):
    return (lax.broadcasted_iota(jnp.int32, shape, 1) // HD) == which


def layer_close(zero, query, parts, valid, vectors, classes, model, units):
    rows, features = zero.shape
    length = valid.shape[1]
    cells = len(parts)
    cuts = columns_of(features, units)
    step = min(rows, 256)
    count = len(classes)
    pair = LANES // HD

    def body(zero_ref, q_ref, valid_ref, vectors_ref, *refs):
        part_refs, class_refs, refs = refs[:cells], refs[cells : cells + count], refs[cells + count :]
        two_ref, attn_ref, log_ref, one_pre_ref, two_pre_ref = refs
        allowed = valid_ref[...] > 0.0
        log_lane = lax.broadcasted_iota(jnp.int32, (step, LANES), 1)
        logs = jnp.zeros((step, LANES), f32)
        pieces = []
        for block in range(features // LANES):
            lanes = slice(block * LANES, (block + 1) * LANES)
            keys = jnp.concatenate([ref[0, :, lanes] for ref in part_refs], 0)
            values = jnp.concatenate([ref[1, :, lanes] for ref in part_refs], 0)
            merged = jnp.zeros((step, LANES), f32)
            for which in range(pair):
                mine = head_lanes((step, LANES), which)
                q = jnp.where(mine, q_ref[:, lanes] * HD ** (-0.5), 0.0).astype(bf)
                score = jnp.where(allowed, rows_times(q, keys), -1e30)
                peak = jnp.max(score, 1, keepdims=True)
                expo = jnp.exp(score - peak)
                total = jnp.sum(expo, 1, keepdims=True)
                weight = (expo * (1.0 / total)).astype(bf)
                merged = jnp.where(
                    mine, jnp.dot(weight, values, preferred_element_type=f32), merged
                )
                logs = jnp.where(log_lane == block * pair + which, peak + jnp.log(total), logs)
            pieces.append(merged)
        log_ref[...] = logs
        attn = jnp.concatenate(pieces, 1).astype(bf)
        attn_ref[...] = attn
        one_pre = side_by_side(attn, class_refs, cuts[3]) + vectors_ref[2:3, :] + zero_ref[...]
        one_pre_ref[...] = one_pre
        one = norm_parts(one_pre)[0] * vectors_ref[3:4, :] + vectors_ref[4:5, :]
        hidden = through(one.astype(bf), class_refs, cuts[4])
        active = gelu(hidden).astype(bf)
        two_pre = side_by_side(active, class_refs, cuts[5]) + vectors_ref[5:6, :] + one
        two_pre_ref[...] = two_pre
        two_ref[...] = norm_parts(two_pre)[0] * vectors_ref[6:7, :] + vectors_ref[7:8, :]

    block = pl.BlockSpec((step, features), lambda j: (j, 0))
    wide = jax.ShapeDtypeStruct((rows, features), f32)
    columns = cuts[-1].stop
    return call(
        body,
        (rows // step,),
        [block, block, whole(valid.shape), whole(vectors.shape)]
        + [resident(x.shape) for x in parts]
        + weight_blocks(classes, model, features, units, False),
        [block, block, pl.BlockSpec((step, LANES), lambda j: (j, 0)), block, block],
        [
            wide,
            jax.ShapeDtypeStruct((rows, features), bf),
            jax.ShapeDtypeStruct((rows, LANES), f32),
            wide,
            wide,
        ],
        [],
        2 * rows * features * (2 * length + features + 2 * units),
        2 * features * columns + 20 * rows * features,
    )(zero, query, valid, vectors, *parts, *classes)


def gelu(x):
    return 0.5 * x * (1.0 + lax.erf(x * 0.7071067811865476))


def gelu_slope(x):
    return 0.5 * (1.0 + lax.erf(x * 0.7071067811865476)) + x * 0.3989422804014327 * jnp.exp(
        -0.5 * x * x
    )


def units_back(d_two, two_pre, one_pre, vectors, classes, model, units):
    rows, features = d_two.shape
    cuts = columns_of(features, units)
    step = min(rows, 256)
    count = len(classes)

    def body(d_ref, two_pre_ref, one_pre_ref, vectors_ref, *refs):
        class_refs, refs = refs[:count], refs[count:]
        reduce_ref, active_ref, low_ref, hidden_ref, branch_ref, pre_ref, attn_ref, sums_ref = refs
        unit, scale = norm_parts(two_pre_ref[...])
        d_two_pre, gain_two, shift_two = norm_back(unit, scale, vectors_ref[6:7, :], d_ref[...])
        low = d_two_pre.astype(bf)
        reduce_ref[...] = low
        d_active = through(low, class_refs, cuts[5])
        unit, scale = norm_parts(one_pre_ref[...])
        one_low = (unit * vectors_ref[3:4, :] + vectors_ref[4:5, :]).astype(bf)
        low_ref[...] = one_low
        hidden = through(one_low, class_refs, cuts[4])
        bell = 0.5 * (1.0 + lax.erf(hidden * 0.7071067811865476))
        active_ref[...] = (hidden * bell).astype(bf)
        slope = bell + hidden * 0.3989422804014327 * jnp.exp(-0.5 * hidden * hidden)
        d_hidden = (d_active * slope).astype(bf)
        hidden_ref[...] = d_hidden
        d_one = side_by_side(d_hidden, class_refs, cuts[4]) + d_two_pre
        d_one_pre, gain_one, shift_one = norm_back(unit, scale, vectors_ref[3:4, :], d_one)
        pre_ref[...] = d_one_pre
        d_branch = d_one_pre.astype(bf)
        branch_ref[...] = d_branch
        attn_ref[...] = through(d_branch, class_refs, cuts[3]).astype(bf)
        put_rows(
            sums_ref,
            pl.program_id(0),
            {
                2: jnp.sum(d_one_pre, 0, keepdims=True),
                3: gain_one,
                4: shift_one,
                5: jnp.sum(d_two_pre, 0, keepdims=True),
                6: gain_two,
                7: shift_two,
            },
        )

    block = pl.BlockSpec((step, features), lambda j: (j, 0))
    broad = pl.BlockSpec((step, units), lambda j: (j, 0))
    columns = cuts[-1].stop
    low = jax.ShapeDtypeStruct((rows, features), bf)
    full = jax.ShapeDtypeStruct((rows, features), f32)
    high = jax.ShapeDtypeStruct((rows, units), bf)
    return call(
        body,
        (rows // step,),
        [block, block, block, whole(vectors.shape)]
        + weight_blocks(classes, model, features, units, False),
        [block, broad, block, broad, block, block, block, whole((8, features))],
        [low, high, low, high, low, full, low, jax.ShapeDtypeStruct((8, features), f32)],
        [],
        2 * rows * features * (features + 3 * units),
        2 * features * columns + 20 * rows * features + 4 * rows * units,
    )(d_two, two_pre, one_pre, vectors, *classes)


def columns_times(left, right):
    return lax.dot_general(left, right, (((0,), (0,)), ((), ())), preferred_element_type=f32)


def attention_back(query, parts, d_attn, logs, valid):
    rows, features = query.shape
    length = valid.shape[1]
    cells = len(parts)
    pair = LANES // HD

    def body(q_ref, d_ref, log_ref, valid_ref, *refs):
        part_refs, dq_ref, d_refs = refs[:cells], refs[cells], refs[cells + 1 :]
        j = pl.program_id(0)
        d_parts = [[None, None] for _ in range(cells)]
        allowed = valid_ref[...] > 0.0
        keys = jnp.concatenate([ref[0] for ref in part_refs], 0)
        values = jnp.concatenate([ref[1] for ref in part_refs], 0)
        merged = jnp.zeros((rows, LANES), f32)
        for which in range(pair):
            mine = head_lanes((rows, LANES), which)
            q = jnp.where(mine, q_ref[...] * HD ** (-0.5), 0.0).astype(bf)
            d = jnp.where(mine, d_ref[...], 0.0).astype(bf)
            log_total = lane_value(log_ref[...], j * pair + which)
            score = jnp.where(allowed, rows_times(q, keys), -1e30)
            weight = jnp.exp(score - log_total)
            slope = rows_times(d, values)
            low = weight.astype(bf)
            inner = jnp.sum(weight * slope, 1, keepdims=True)
            d_score = (weight * (slope - inner)).astype(bf)
            merged = jnp.where(
                mine, jnp.dot(d_score, keys, preferred_element_type=f32), merged
            )
            at = 0
            for cell, ref in enumerate(part_refs):
                here = slice(at, at + ref.shape[1])
                at = here.stop
                for slot, (left, right) in enumerate(((d_score, q), (low, d))):
                    term = columns_times(left[:, here], right)
                    had = d_parts[cell][slot]
                    d_parts[cell][slot] = term if had is None else had + term
        dq_ref[...] = (merged * HD ** (-0.5)).astype(bf)
        for ref, pieces in zip(d_refs, d_parts):
            for slot, piece in enumerate(pieces):
                ref[slot] = piece.astype(ref.dtype)

    block = pl.BlockSpec((rows, LANES), lambda j: (0, j))
    tall = [pl.BlockSpec((2, x.shape[1], LANES), lambda j: (0, 0, j)) for x in parts]
    return call(
        body,
        (features // LANES,),
        [block, block, whole(logs.shape), whole(valid.shape)] + tall,
        [block] + tall,
        [jax.ShapeDtypeStruct((rows, features), bf)]
        + [jax.ShapeDtypeStruct(x.shape, f32 if n == 0 else bf) for n, x in enumerate(parts)],
        [],
        10 * rows * features * length,
        16 * length * features,
    )(query, d_attn, logs, valid, *parts)


def embed_back(d_parts, d_one_pre, embedded, vectors, classes, model, units):
    rows, features = d_one_pre.shape
    cuts = columns_of(features, units)
    step = min(rows, 256)
    count = len(classes)

    def body(q_ref, k_ref, v_ref, pre_ref, x_ref, vectors_ref, *refs):
        class_refs, (out_ref, sums_ref) = refs[:count], refs[count:]
        d_zero = pre_ref[...]
        for t, part in enumerate((q_ref, k_ref, v_ref)):
            d_zero += side_by_side(part[...], class_refs, cuts[t])
        unit, scale = norm_parts(x_ref[...])
        d_embed, gain, shift = norm_back(unit, scale, vectors_ref[0:1, :], d_zero)
        out_ref[...] = d_embed.astype(bf)
        put_rows(sums_ref, pl.program_id(0), {0: gain, 1: shift})

    block = pl.BlockSpec((step, features), lambda j: (j, 0))
    return call(
        body,
        (rows // step,),
        [block] * 5
        + [whole(vectors.shape)]
        + weight_blocks(classes, model, features, units, True),
        [block, whole((8, features))],
        [
            jax.ShapeDtypeStruct((rows, features), bf),
            jax.ShapeDtypeStruct((8, features), f32),
        ],
        [],
        6 * rows * features * features,
        6 * features * features + 16 * rows * features,
    )(*d_parts, d_one_pre, embedded, vectors, *classes)


def cosine_loss(x_student, x_teacher):
    s_len = jnp.sqrt(jnp.sum(x_student * x_student, -1))
    t_len = jnp.sqrt(jnp.sum(x_teacher * x_teacher, -1))
    return 1.0 - jnp.sum(x_student * x_teacher, -1) / (s_len * t_len)


def adam_update(master, first, square, grad, factor, rate, decay):
    clipped = grad * factor
    new_first = beta_first * first + (1.0 - beta_first) * clipped
    new_square = beta_second * square + (1.0 - beta_second) * clipped * clipped
    first_hat = new_first / (1.0 - beta_first**STEP)
    square_hat = new_square / (1.0 - beta_second**STEP)
    updated = master - rate * (first_hat / (jnp.sqrt(square_hat) + adam_eps) + decay * master)
    return [updated, new_first, new_square]


def body(
    token_ids,
    mlm_flags,
    pad_lengths,
    group_ids,
    group_weight,
    teacher_table,
    teacher_position,
    teacher_project,
    teacher_output,
    teacher_expand,
    teacher_reduce,
    teacher_vectors,
    student_table,
    student_position,
    student_project,
    student_output,
    student_expand,
    student_reduce,
    student_vectors,
    first_table,
    first_position,
    first_project,
    first_output,
    first_expand,
    first_reduce,
    first_vectors,
    square_table,
    square_position,
    square_project,
    square_output,
    square_expand,
    square_reduce,
    square_vectors,
):
    mp, dp = lax.axis_size("mp"), lax.axis_size("dp")
    place, index = lax.axis_index("mp"), lax.axis_index("dp")
    core = index & 1
    batch, length = token_ids.shape
    spans = mp // (2 * batch)
    rows = length // (2 * spans)
    vocab_rows = student_table.shape[0]
    share = student_table.shape[1]
    features = share * dp
    start = place * vocab_rows

    packed = jnp.concatenate(
        [
            token_ids * 2 + mlm_flags,
            jnp.pad((pad_lengths * 256 + group_ids)[None], ((0, 0), (0, length - batch))),
        ]
    )
    packed = ordered(1, packed[None], swap(packed, 1)[None], 0)
    column_ids = packed[:, :batch].reshape(2 * batch, spans, 2, rows)
    lengths = (packed[:, batch, :batch] // 256).reshape(-1)
    groups = (packed[:, batch, :batch] % 256).reshape(-1)
    chosen = groups[:, None] == jnp.arange(group_weight.shape[0])[None, :]
    seq_weight = jnp.sum(jnp.where(chosen, group_weight[None, :], 0.0), -1)
    line_place = (place - jnp.arange(mp)) % mp
    line = lax.dynamic_index_in_dim(column_ids, core, 2, keepdims=False).reshape(mp, rows)
    line = jnp.take(line, line_place, axis=0)
    line_targets, line_flags = line // 2, line % 2
    line_inputs = jnp.where(line_flags == 1, mask_token, line_targets)
    line_sequence = line_place // spans
    line_part = (line_place % spans) * 2 + core
    line_positions = line_part[:, None] * rows + jnp.arange(rows)[None, :]
    line_lengths = jnp.take(lengths, line_sequence)
    line_real = (line_positions < line_lengths[:, None]).astype(f32)
    line_masked = line_flags.astype(f32) * line_real
    line_weight = jnp.take(seq_weight, line_sequence)[:, None]
    tok_weight, mask_weight = line_weight * line_real, line_weight * line_masked
    own_part = line_part[0]
    held = jnp.concatenate(
        [part * rows + jnp.arange(rows) for part in sequence_parts(core, spans)]
    )
    valid = (held < line_lengths[0]).astype(f32)[None]

    slots = -(-(11 * rows // (10 * mp) + 16) // 32) * 32
    plain = (line_real > 0) & (line_inputs != mask_token)
    owner = line_inputs // vocab_rows
    wanted = plain & (owner == place)
    away = (owner[0] - place) % mp
    from_owner = plain[0] & (away[None, :] == jnp.arange(mp)[:, None])
    ordinal = jnp.arange(rows)
    earlier = (ordinal[:, None] <= ordinal[None, :]).astype(bf)
    ranks = jnp.dot(
        jnp.concatenate([wanted, from_owner], 0).astype(bf), earlier, preferred_element_type=f32
    )
    ranks = ranks.astype(jnp.int32) - 1
    wanted_rank = jnp.where(wanted, ranks[:mp], -1)
    own_rank = jnp.sum(jnp.where(from_owner, ranks[mp:], 0), 0)
    mask_owner = mask_token // vocab_rows
    pair_counts = jnp.sum(
        (plain[None] & (owner[None] == jnp.arange(mp)[:, None, None])).astype(f32), -1
    )

    def wanted_ids(turn):
        number = jnp.arange(slots - 1) + turn * (slots - 1)
        match = wanted_rank[:, None, :] == number[None, :, None]
        ids = jnp.sum(jnp.where(match, line_inputs[:, None, :] - start + 1, 0), -1) - 1
        shared_id = jnp.where((place == mask_owner) & (turn == 0), mask_token - start, -1)
        shared_id = jnp.broadcast_to(shared_id, (mp, 1))
        return jnp.concatenate([ids, shared_id], 1).reshape(-1, 1)

    def own_slots(turn):
        number = own_rank - turn * (slots - 1)
        at = jnp.where(plain[0] & (number >= 0) & (number < slots - 1), away * slots + number, -1)
        masked_at = ((mask_owner - place) % mp) * slots + slots - 1
        is_mask = (line_real[0] > 0) & (line_inputs[0] == mask_token) & (turn == 0)
        at = jnp.where(is_mask, masked_at, at)
        return (at[:, None] == jnp.arange(mp * slots)[None, :]).astype(bf)

    def sent(found):
        return found[:slots], [
            rotate(found[k * slots : (k + 1) * slots], -k) for k in range(1, mp)
        ]

    def placed_rows(got, turn):
        return jnp.dot(own_slots(turn), stacked([got[0], *got[1]]), preferred_element_type=f32)

    def every_owner(ids):
        bit = 1
        while bit < dp:
            ids = jnp.concatenate([ids, swap(ids, bit)], 0)
            bit *= 2
        return ids

    def at_owners(d_embed, turn):
        sums = columns_times(own_slots(turn), d_embed).astype(bf)
        return stacked(
            [sums[:slots]]
            + [rotate(sums[k * slots : (k + 1) * slots], k) for k in range(1, mp)]
        ).T

    def by_column(at_owner):
        placed, wide = [], mp * slots
        for other in range(dp):
            row = ((other & 1) * (dp // 2) + other // 2) * share
            part = at_owner[row : row + share]
            placed.append((swap(part, other) if other else part, 0, other * wide))
        return placed

    def returned(placed):
        return assemble(placed, (share, dp * mp * slots))

    local_targets = (line_targets - start).reshape(-1, 1)

    nonpad = (jnp.arange(length)[None, :] < pad_lengths[:, None]).astype(f32)
    masked = mlm_flags.astype(f32) * nonpad
    lane = jnp.arange(LANES)[None, :]
    counts = jnp.where(lane == 0, jnp.sum(nonpad), jnp.where(lane == 1, jnp.sum(masked), 0.0))
    counts = jnp.where(lane == 2, jnp.max(pair_counts), counts)
    counts = jnp.broadcast_to(counts, (8, LANES))
    bit = 1
    while bit < dp:
        got = swap(counts, bit)
        counts = jnp.where(lane == 2, jnp.maximum(counts, got), counts + got)
        bit *= 2
    count_tok, count_mask = counts[0, 0], jnp.maximum(counts[0, 1], 1.0)
    most = counts[0, 2].astype(jnp.int32)
    rounds = (most + slots - 2) // (slots - 1)

    head_cut = student_project.shape[2]
    unit_cut = student_expand.shape[1]
    cuts = [head_cut] * 4 + [unit_cut] * 2
    units = mp * unit_cut
    vector_rows = student_vectors.shape[0]

    table_parts = gather_start(student_table.T.astype(bf))

    def cut_rows(x, axis):
        return lax.dynamic_slice_in_dim(x, index * share, share, axis)

    s_share = joined(student_project, student_output.T, student_expand, student_reduce.T)
    t_share = joined(
        cut_rows(teacher_project, 1),
        cut_rows(teacher_output, 1).T,
        cut_rows(teacher_expand, 0),
        cut_rows(teacher_reduce, 1).T,
    )
    first_ids = wanted_ids(0)
    both_shares = stacked([t_share, s_share])

    def t_find(ids):
        return jnp.take(teacher_table, jnp.clip(ids[:, 0], 0, vocab_rows - 1), axis=0)

    table_parts, both_shares, first_ids = phase(table_parts, both_shares, first_ids)

    order = order_matrix(features, share)

    def reordered(x, back=False):
        return rows_times(x, order) if back else jnp.dot(x, order, preferred_element_type=f32)

    t_vectors = reordered(teacher_vectors)
    t_position = lax.dynamic_slice_in_dim(teacher_position, own_part * rows, rows, 0)
    t_position = reordered(t_position)
    vector_rows = student_vectors.shape[0]
    small_at = 2 * mp * sum(cuts)
    padded = -(small_at + length + vector_rows) % (2 * LANES)
    s_small = jnp.concatenate(
        [student_position.T, student_vectors.T, jnp.zeros((share, padded), f32)], 1
    ).astype(bf)

    table_parts = gather_rest(table_parts)
    both_shares = gather_mp(both_shares)
    table_parts, both_shares, s_small = phase(table_parts, both_shares, s_small)

    weight_parts = gather_start(by_kind(both_shares, cuts, 2, s_small))
    s_table = gather_end(table_parts)
    t_found = t_find(first_ids)
    s_table, weight_parts, t_found = phase(s_table, weight_parts, t_found)

    weight_parts = gather_rest(weight_parts)
    t_got = sent(t_found)
    s_found = pick_rows(first_ids, s_table)
    weight_parts, s_found, t_got = phase(weight_parts, s_found, t_got)

    classes = gather_end(weight_parts)
    s_got = sent(s_found)
    t_rows = lax.fori_loop(
        1,
        rounds,
        lambda turn, had: had + placed_rows(sent(t_find(wanted_ids(turn))), turn),
        placed_rows(t_got, 0),
    )
    t_embedded = reordered(t_rows.astype(bf)) + t_position
    classes, s_got, t_embedded = phase(classes, s_got, t_embedded)

    all_ids = every_owner(first_ids)

    s_rows = lax.fori_loop(
        1,
        rounds,
        lambda turn, had: had + placed_rows(sent(pick_rows(wanted_ids(turn), s_table)), turn),
        placed_rows(s_got, 0),
    )
    s_small = jnp.concatenate([c[:, small_at:] for c in classes], 0)
    s_vectors = s_small[:, length : length + vector_rows].T.astype(f32)
    s_position = lax.dynamic_slice_in_dim(s_small, own_part * rows, rows, 1).T
    s_embedded = s_rows + s_position.astype(f32)
    t_zero, t_query, t_own = layer_open(t_embedded, t_vectors, classes, 0, units)
    s_zero, s_query, s_own = layer_open(s_embedded, s_vectors, classes, 1, units)
    t_sequence, s_sequence = gather_sequence(t_own, spans), gather_sequence(s_own, spans)
    t_two = layer_close(t_zero, t_query, t_sequence, valid, t_vectors, classes, 0, units)[0]
    t_low = reordered(t_two.astype(bf), True).astype(bf)
    t_low, t_two, s_zero, s_query, s_sequence = phase(t_low, t_two, s_zero, s_query, s_sequence)

    def further(ring, steps):
        ring = list(ring)
        for _ in range(steps):
            ring.append(rotate(ring[-1]))
        return ring

    t_ring = further([t_low], 1 if mp > 1 else 0)
    s_two, s_attn, s_logs, s_one_pre, s_two_pre = layer_close(
        s_zero, s_query, s_sequence, valid, s_vectors, classes, 1, units
    )
    cos_terms, cos_pull = jax.vjp(lambda x: cosine_loss(x, t_two), s_two)
    own_weight = tok_weight[0]
    (d_cos,) = cos_pull(own_weight / count_tok)
    own_cos = jnp.sum(own_weight * cos_terms)
    t_ring, s_two, d_cos = phase(t_ring, s_two, d_cos)

    s_ring, outs = [s_two.astype(bf)], []
    for k in range(mp):
        chunk_targets = local_targets[k * rows : (k + 1) * rows]
        out = head_pass(t_ring[k], s_ring[k], teacher_table, s_table, chunk_targets)
        t_ring = further(t_ring, 1 if len(t_ring) < mp else 0)
        s_ring = further(s_ring, 1 if len(s_ring) < mp else 0)
        t_ring, s_ring, out = phase(t_ring, s_ring, out)
        outs.append(out)
    t_peaks, s_peaks, tail = [jnp.concatenate([x[n] for x in outs], 0) for n in (2, 3, 4)]

    mine = tail[:, :8].T.reshape(8, mp, rows)
    stats = jnp.stack([mine] + [jnp.roll(rotate(mine, by), by, 1) for by in range(1, mp)])
    t_peak = jnp.max(stats[:, 0], 0)
    t_grow = jnp.exp((stats[:, 0] - t_peak) / temper)
    t_half_sum = jnp.sum(t_grow * stats[:, 1], 0)
    s_peak = jnp.max(stats[:, 2], 0)
    s_grow = jnp.exp((stats[:, 2] - s_peak) / temper)
    s_half_sum = jnp.sum(s_grow * stats[:, 3], 0)
    s_full_sum = jnp.sum(s_grow * s_grow * stats[:, 4], 0)

    apart = jnp.sum(t_grow[:, 0] * stats[:, 5, 0], 0) / temper
    log_half_s = s_peak[0] / temper + jnp.log(s_half_sum[0])
    log_half_t = t_peak[0] / temper + jnp.log(t_half_sum[0])
    log_full = s_peak[0] + jnp.log(s_full_sum[0])
    diverge = temper * temper * (apart / t_half_sum[0] - log_half_t + log_half_s)
    missed = log_full - jnp.sum(stats[:, 6, 0], 0)
    own_terms = jnp.stack(
        [
            jnp.sum(own_weight * diverge),
            jnp.sum(mask_weight[0] * missed),
            own_cos,
        ]
    )
    own_terms = jnp.pad(own_terms[None], ((0, 7), (0, LANES - 3)))
    own_terms = own_terms + swap(own_terms, 1)
    line_terms = natural([own_terms] + [rotate(own_terms, by) for by in range(1, mp)])
    seq_terms = jnp.sum(line_terms[:, 0, :3].reshape(2 * batch, spans, 3), 1)
    loss_terms = lax.dynamic_slice_in_dim(seq_terms, core * batch, batch, 0)

    coef_kl = 5.0 * temper * tok_weight / count_tok
    coef_mlm = 2.0 * mask_weight / count_mask

    def by_token(values):
        return values.reshape(-1, 1)

    s_tiles = jnp.exp((s_peaks - by_token(s_peak)) / temper)
    t_tiles = jnp.exp((t_peaks - by_token(t_peak)) / temper)
    back = (
        s_tiles * by_token(coef_kl / s_half_sum),
        t_tiles * by_token(coef_kl / t_half_sum),
        s_tiles * s_tiles * by_token(coef_mlm / s_full_sum),
        by_token(coef_mlm),
        local_targets,
        s_table,
    )
    d_logits, d_sent = [None] * mp, []
    for step in range(mp):
        k = (step + 1) % mp
        halves = outs[k][1], outs[k][0]
        if step >= 3:
            halves, d_sent[step - 3] = phase(halves, d_sent[step - 3])
        d_logits[k], d_row = head_back(k, 0, rows, *halves, *back)
        if k:
            d_sent.append(rotate(d_row, -k))
    if mp > 2:
        d_logits, d_sent[:-1] = phase(d_logits, d_sent[:-1])
    d_head = d_row.astype(f32)
    for got in d_sent:
        d_head = d_head + got.astype(f32)
    g_head = table_grad(jnp.concatenate([x.T for x in s_ring], 1), d_logits)
    d_two = d_head + d_cos
    d_two, g_head = phase(d_two, g_head)

    table_sum = scatter_start(g_head)
    from_units = units_back(d_two, s_two_pre, s_one_pre, s_vectors, classes, 1, units)
    table_sum, from_units = phase(table_sum, from_units)
    d_reduce, active, one_low, d_hidden, d_branch, d_one_pre, d_attn, sums = from_units

    table_sum = scatter_step(table_sum, 0)
    from_attention = attention_back(s_query, s_sequence, d_attn, s_logs, valid)
    table_sum, from_attention, d_reduce, active, one_low, d_hidden = phase(
        table_sum, from_attention, d_reduce, active, one_low, d_hidden
    )

    table_sum = scatter_all(table_sum)
    d_both = scatter_sequence(from_attention[1:], spans).astype(bf)
    g_units = assemble(
        [
            (columns_times(one_low, d_hidden).astype(bf), 0, 0),
            (columns_times(d_reduce, active).astype(bf), 0, units),
        ],
        (features, 2 * units),
    )
    table_sum, d_both, g_units, s_zero = phase(table_sum, d_both, g_units, s_zero)

    units_sum = scatter_start(g_units)
    d_parts = (from_attention[0], d_both[0], d_both[1])
    d_embed, first_sums = embed_back(
        d_parts, d_one_pre, s_embedded, s_vectors, classes, 1, units
    )
    low = s_zero.astype(bf)
    g_heads = [columns_times(low, d).astype(bf) for d in d_parts]
    g_heads.append(columns_times(d_branch, s_attn).astype(bf))
    g_position = lax.dynamic_update_slice_in_dim(
        jnp.zeros((features, length), bf), d_embed.T, own_part * rows, 1
    )
    heads_at = mp * 4 * head_cut
    head_wide = mp * head_cut
    late_padded = -(heads_at + length + vector_rows) % (2 * LANES)
    g_vectors = jnp.pad((sums + first_sums).T.astype(bf), ((0, 0), (0, late_padded)))
    g_late = assemble(
        [(g, 0, t * head_wide) for t, g in enumerate(g_heads)]
        + [(g_position, 0, heads_at), (g_vectors, 0, heads_at + length)],
        (features, heads_at + length + vector_rows + late_padded),
    )
    units_sum, d_embed, g_late = phase(units_sum, d_embed, g_late)

    def by_place(summed, kinds, cut):
        return [
            jnp.concatenate(
                [summed[:, (t * mp + k) * cut : (t * mp + k + 1) * cut] for t in range(kinds)], 1
            )
            for k in range(mp)
        ]

    units_sum = scatter_step(units_sum, 0)
    late_sum = scatter_start(g_late)
    at_owner = at_owners(d_embed, 0)
    units_sum, late_sum, at_owner = phase(units_sum, late_sum, at_owner)

    units_sum = scatter_end(scatter_all(units_sum))
    late_sum = scatter_step(late_sum, 0)
    placed = by_column(at_owner)
    arrived, units_sum, late_sum = phase([x for x, _, _ in placed], units_sum, late_sum)

    late_sum = scatter_end(scatter_all(late_sum))
    own_units = sum_mp(by_place(units_sum, 2, unit_cut))
    e_rows = returned([(x, row, at) for x, (_, row, at) in zip(arrived, placed)])
    own_table = add_rows(scatter_end(table_sum), e_rows, all_ids, 0)
    own_table, own_units, late_sum = phase(own_table, own_units, late_sum)

    small = late_sum[:, heads_at:].astype(bf)
    heads = [x.astype(bf) for x in by_place(late_sum, 4, head_cut)]
    got = [jnp.concatenate([x, small], 1) for x in heads]
    got = got[:1] + [rotate(got[k], -k) for k in range(1, mp)]
    own_table = add_rows(own_table, e_rows, all_ids, 1)
    got, own_table = phase(got, own_table)
    own_heads = sum(x[:, : 4 * head_cut].astype(f32) for x in got)
    got = [got[-k % mp][:, 4 * head_cut :] for k in range(mp)]
    own_small = jnp.sum(natural(got).astype(f32), 0)
    own_table = lax.fori_loop(
        1,
        rounds,
        lambda turn, had: add_rows(
            had,
            returned(by_column(at_owners(d_embed, turn))),
            every_owner(wanted_ids(turn)),
            None,
        ),
        own_table,
    )

    shared_sq = jnp.sum(own_small * own_small) / mp
    squares = (
        jnp.sum(own_table * own_table)
        + jnp.sum(own_units * own_units)
        + jnp.sum(own_heads * own_heads)
        + shared_sq
    )
    squares = sum_all(jnp.broadcast_to(squares, (8, LANES)))[0, 0]
    norm = jnp.sqrt(squares)
    factor = clip_limit / jnp.maximum(norm, clip_limit)

    owned = (
        own_table.T,
        own_small[:, :length].T,
        jnp.stack([own_heads[:, t * head_cut : (t + 1) * head_cut] for t in range(3)]),
        own_heads[:, 3 * head_cut :].T,
        own_units[:, :unit_cut],
        own_units[:, unit_cut:].T,
        own_small[:, length : length + vector_rows].T,
    )
    masters = (
        student_table,
        student_position,
        student_project,
        student_output,
        student_expand,
        student_reduce,
        student_vectors,
    )
    firsts = (
        first_table,
        first_position,
        first_project,
        first_output,
        first_expand,
        first_reduce,
        first_vectors,
    )
    seconds = (
        square_table,
        square_position,
        square_project,
        square_output,
        square_expand,
        square_reduce,
        square_vectors,
    )
    results = []
    for index in range(7):
        rate = rate_vector if index == 6 else rate_table if index == 0 else rate_matrix
        decay = 0.0 if index == 6 else weight_decay
        results += adam_update(
            masters[index], firsts[index], seconds[index], owned[index], factor, rate, decay
        )
    loss_counts = jnp.stack([count_tok, count_mask])
    return (*results, norm, loss_terms, loss_counts)


def solution(mesh):
    in_specs = (
        P("dp", None),
        P("dp", None),
        P("dp"),
        P("dp"),
        P(),
        P("mp", None),
        P(),
        P(None, None, "mp"),
        P("mp", None),
        P(None, "mp"),
        P("mp", None),
        P(),
        P("mp", "dp"),
        P(None, "dp"),
        P(None, "dp", "mp"),
        P("mp", "dp"),
        P("dp", "mp"),
        P("mp", "dp"),
        P(None, "dp"),
        P("mp", "dp"),
        P(None, "dp"),
        P(None, "dp", "mp"),
        P("mp", "dp"),
        P("dp", "mp"),
        P("mp", "dp"),
        P(None, "dp"),
        P("mp", "dp"),
        P(None, "dp"),
        P(None, "dp", "mp"),
        P("mp", "dp"),
        P("dp", "mp"),
        P("mp", "dp"),
        P(None, "dp"),
    )
    out_specs = (
        P("mp", "dp"),
        P("mp", "dp"),
        P("mp", "dp"),
        P(None, "dp"),
        P(None, "dp"),
        P(None, "dp"),
        P(None, "dp", "mp"),
        P(None, "dp", "mp"),
        P(None, "dp", "mp"),
        P("mp", "dp"),
        P("mp", "dp"),
        P("mp", "dp"),
        P("dp", "mp"),
        P("dp", "mp"),
        P("dp", "mp"),
        P("mp", "dp"),
        P("mp", "dp"),
        P("mp", "dp"),
        P(None, "dp"),
        P(None, "dp"),
        P(None, "dp"),
        P(),
        P("dp", None),
        P(),
    )
    return jax.shard_map(body, mesh=mesh, in_specs=in_specs, out_specs=out_specs, check_vma=False)
```
